32 devices in a mesh: batch: 4 (over z), ty: 2 (over y), tx: 4 (over x, core).
Axes of the slice: x: 2, y: 2, z: 4, core: 2. Of those that a mesh axis runs over, the one named last changes fastest.
Arguments:
- tokens: bfloat16 [96, 16, 16, 768], P('batch', 'ty', 'tx'), may hold values from -6 to 6
- skip_tokens: bfloat16 [96, 16, 16, 768], P('batch', 'ty', 'tx'), may hold values from -6 to 6
- extra_tokens: bfloat16 [96, 2, 768], P('batch'), may hold values from -6 to 6
- extra_skip: bfloat16 [96, 2, 768], P('batch'), may hold values from -6 to 6
- timesteps: int32 [96], P('batch'), may hold values from 0 to 999, as said below
- target: float32 [96, 32, 32, 4], P('batch', 'ty', 'tx'), may hold values from -6 to 6
- w_skip: bfloat16 [1536, 768], replicated, may hold values from -0.15625 to 0.15625
- b_skip: bfloat16 [768], replicated, may hold values from -3 to 3
- norm1_gain: bfloat16 [768], replicated, may hold values from 0.5 to 1.5
- norm1_shift: bfloat16 [768], replicated, may hold values from -2 to 2
- w_qkv: bfloat16 [768, 2304], replicated, may hold values from -0.3125 to 0.3125
- w_out: bfloat16 [768, 768], replicated, may hold values from -0.875 to 0.875
- b_out: bfloat16 [768], replicated, may hold values from -3 to 3
- norm2_gain: bfloat16 [768], replicated, may hold values from 0.5 to 1.5
- norm2_shift: bfloat16 [768], replicated, may hold values from -2 to 2
- w_up: bfloat16 [768, 3072], replicated, may hold values from -0.21875 to 0.21875
- b_up: bfloat16 [3072], replicated, may hold values from -3 to 3
- w_down: bfloat16 [3072, 768], replicated, may hold values from -0.109375 to 0.109375
- b_down: bfloat16 [768], replicated, may hold values from -3 to 3
- final_gain: bfloat16 [768], replicated, may hold values from 0.5 to 1.5
- final_shift: bfloat16 [768], replicated, may hold values from -2 to 2
- w_head: bfloat16 [768, 16], replicated, may hold values from -0.21875 to 0.21875
- b_head: bfloat16 [16], replicated, may hold values from -3 to 3
- w_conv: bfloat16 [3, 3, 4, 4], replicated, may hold values from -1 to 1
- b_conv: bfloat16 [4], replicated, may hold values from -3 to 3
Outputs:
- latent_out: bfloat16 [96, 32, 32, 4], P('batch', 'ty', 'tx')
- grad_tokens: bfloat16 [96, 16, 16, 768], P('batch', 'ty', 'tx')
- grad_skip_tokens: bfloat16 [96, 16, 16, 768], P('batch', 'ty', 'tx')
- grad_extra_tokens: bfloat16 [96, 2, 768], P('batch')
- grad_extra_skip: bfloat16 [96, 2, 768], P('batch')
- grad_w_skip: float32 [1536, 768], P(('batch', 'ty', 'tx'))
- grad_b_skip: float32 [768], P(('batch', 'ty', 'tx'))
- grad_norm1_gain: float32 [768], P(('batch', 'ty', 'tx'))
- grad_norm1_shift: float32 [768], P(('batch', 'ty', 'tx'))
- grad_w_qkv: float32 [768, 2304], P(('batch', 'ty', 'tx'))
- grad_w_out: float32 [768, 768], P(('batch', 'ty', 'tx'))
- grad_b_out: float32 [768], P(('batch', 'ty', 'tx'))
- grad_norm2_gain: float32 [768], P(('batch', 'ty', 'tx'))
- grad_norm2_shift: float32 [768], P(('batch', 'ty', 'tx'))
- grad_w_up: float32 [768, 3072], P(('batch', 'ty', 'tx'))
- grad_b_up: float32 [3072], P(('batch', 'ty', 'tx'))
- grad_w_down: float32 [3072, 768], P(('batch', 'ty', 'tx'))
- grad_b_down: float32 [768], P(('batch', 'ty', 'tx'))
- grad_final_gain: float32 [768], P(('batch', 'ty', 'tx'))
- grad_final_shift: float32 [768], P(('batch', 'ty', 'tx'))
- grad_w_head: float32 [768, 16], P(('batch', 'ty', 'tx'))
- grad_b_head: float32 [16], replicated
- grad_w_conv: float32 [3, 3, 4, 4], replicated
- grad_b_conv: float32 [4], replicated
The draws below stay inside these ranges and needn't reach their ends.
Inputs may be any that keep to these rules, and one draw needn't show every extreme that they name: `timesteps`: diffusion steps lean toward high noise.
All inputs are finite; a program needn't handle non-finite values.
Results may differ from the reference program's by a relative error of at most 0.014.
Values may be sent and summed in bfloat16 or wider, within the bound.
No kernel may reach another device: no remote copies, remote signals or barrier semaphores. Data moves between devices by JAX's collectives and lax.ppermute only.
A program may use at most 192 MiB of HBM per device.

```python
from functools import partial
import jax
import jax.numpy as jnp
from jax import lax

D = 768
HEADS = 12
FF = 3072
PATCH = 2
CHANNELS = 4
GRID = 16
EXTRA = 2
ITEMS = 96
N_BATCH = 4


def draw_timesteps(key, part):
    key = jax.random.fold_in(key, 11)
    first, second = jax.random.split(key)
    left = jax.random.randint(first, (ITEMS,), 0, 1000)
    right = jax.random.randint(second, (ITEMS,), 0, 1000)
    return (999 - left * right // 1000).astype(jnp.int32)


def block_levels(own_key, shape, cuts, low, top_value):
    def one(position, blocks):
        steps = jax.random.uniform(jax.random.fold_in(jax.random.fold_in(own_key, 6), position), (blocks,), jnp.float32, low / len(cuts), top_value / len(cuts))
        return jnp.repeat(jnp.exp(steps), shape[position] // blocks).reshape((-1,) + (1,) * (len(shape) - position - 1))

    level = one(*cuts[0])
    for cut in cuts[1:]:
        level = level * one(*cut)
    return level


def scatter_about(key, extent, scale, most, pieces=(), held_as=jnp.bfloat16):
    drawn = scale * jax.random.normal(key, extent, jnp.float32)
    if pieces:
        drawn = drawn * block_levels(key, extent, pieces, -0.22, 0.18)
    return jnp.clip(drawn, -most, most).astype(held_as)


def setup_inputs(seed: int = 0) -> dict:
    splits = jax.random.split(jax.random.key(seed), 26)
    return {
        "tokens": scatter_about(splits[0], (ITEMS, GRID, GRID, D), 1.0, 6.0, ((0, 4), (1, 2), (2, 4))),
        "skip_tokens": scatter_about(splits[1], (ITEMS, GRID, GRID, D), 1.0, 6.0, ((0, 4), (1, 2), (2, 4))),
        "extra_tokens": scatter_about(splits[2], (ITEMS, EXTRA, D), 1.0, 6.0, ((0, 4),)),
        "extra_skip": scatter_about(splits[3], (ITEMS, EXTRA, D), 1.0, 6.0, ((0, 4),)),
        "timesteps": draw_timesteps(jax.random.fold_in(splits[25], 71), 0),
        "target": scatter_about(splits[5], (ITEMS, GRID * PATCH, GRID * PATCH, CHANNELS), 1.0, 6.0, ((0, 4), (1, 2), (2, 4)), jnp.float32),
        "w_skip": scatter_about(splits[6], (2 * D, D), (2 * D) ** -0.5, 0.15625),
        "b_skip": scatter_about(splits[7], (D,), 0.5, 3.0),
        "norm1_gain": jnp.clip(1.0 + 0.1 * jax.random.normal(splits[8], (D,), jnp.float32), 0.5, 1.5).astype(jnp.bfloat16),
        "norm1_shift": scatter_about(splits[9], (D,), 0.3, 2.0),
        "w_qkv": scatter_about(splits[10], (D, 3 * D), (D // 2) ** -0.5, 0.3125),
        "w_out": scatter_about(splits[11], (D, D), (D // 16) ** -0.5, 0.875),
        "b_out": scatter_about(splits[12], (D,), 0.5, 3.0),
        "norm2_gain": jnp.clip(1.0 + 0.1 * jax.random.normal(splits[13], (D,), jnp.float32), 0.5, 1.5).astype(jnp.bfloat16),
        "norm2_shift": scatter_about(splits[14], (D,), 0.3, 2.0),
        "w_up": scatter_about(splits[15], (D, FF), D ** -0.5, 0.21875),
        "b_up": scatter_about(splits[16], (FF,), 0.5, 3.0),
        "w_down": scatter_about(splits[17], (FF, D), FF ** -0.5, 0.109375),
        "b_down": scatter_about(splits[18], (D,), 0.5, 3.0),
        "final_gain": jnp.clip(1.0 + 0.1 * jax.random.normal(splits[19], (D,), jnp.float32), 0.5, 1.5).astype(jnp.bfloat16),
        "final_shift": scatter_about(splits[20], (D,), 0.3, 2.0),
        "w_head": scatter_about(splits[21], (D, PATCH * PATCH * CHANNELS), D ** -0.5, 0.21875),
        "b_head": scatter_about(splits[22], (PATCH * PATCH * CHANNELS,), 0.5, 3.0),
        "w_conv": scatter_about(splits[23], (3, 3, CHANNELS, CHANNELS), (9 * CHANNELS) ** -0.5, 1.0),
        "b_conv": scatter_about(splits[24], (CHANNELS,), 0.5, 3.0),
    }


@jax.custom_vjp
def low(v):
    return lax.optimization_barrier(v.astype(jnp.bfloat16)).astype(jnp.float32)

@jax.custom_vjp
def low_back(v):
    return v

def low_keep(v):
    return (low(v), None)

def low_pass(kept, grad):
    return (grad,)

def back_keep(v):
    return (v, None)

def back_low(kept, grad):
    return (low(grad),)
low.defvjp(low_keep, low_pass)
low_back.defvjp(back_keep, back_low)
EPS = 1e-05

def matmul(left, right):
    return jnp.einsum('...i,ij->...j', left, right, precision=lax.Precision.HIGHEST)

def layer_norm(values, gain, shift):
    center = values - lax.optimization_barrier(jnp.mean(values, -1, keepdims=True))
    return center * lax.rsqrt(lax.optimization_barrier(jnp.mean(center * center, -1, keepdims=True)) + EPS) * gain + shift

def noise_weight(timesteps):
    frac = (timesteps.astype(jnp.float32) / 1000.0 + 0.008) / 1.008
    kept = jnp.cos(frac * (0.5 * jnp.pi)) ** 2
    return jnp.minimum(1.0, 5.0 * (1.0 - kept) / kept)

def attend(block):
    queries, keys, values = block
    scale = queries.shape[-1] ** (-0.5)
    scores = low_back(jnp.einsum('bqhd,bkhd->bhqk', queries, keys, precision=lax.Precision.HIGHEST) * scale)
    probs = low(jax.nn.softmax(scores, -1))
    return jnp.einsum('bhqk,bkhd->bqhd', probs, values, precision=lax.Precision.HIGHEST)

def forward(weights, target, tokens, skip_tokens, extra_tokens, extra_skip, w_skip, b_skip, norm1_gain, norm1_shift, w_qkv, w_out, b_out, norm2_gain, norm2_shift, w_up, b_up, w_down, b_down, final_gain, final_shift, w_head, b_head, w_conv, b_conv):
    items = tokens.shape[0]
    side = tokens.shape[1]
    width = tokens.shape[3]
    body_count = side * side
    span = body_count + EXTRA
    flat = tokens.reshape(items, body_count, width)
    flat_skip = skip_tokens.reshape(items, body_count, width)
    joined = jnp.concatenate([jnp.concatenate([flat, flat_skip], 2), jnp.concatenate([extra_tokens, extra_skip], 2)], 1)
    hidden0 = low_back(matmul(joined, w_skip) + b_skip)
    normed1 = low(layer_norm(hidden0, norm1_gain, norm1_shift))
    qkv = low_back(low(matmul(normed1, w_qkv)))
    head_dim = width // HEADS
    group = items // N_BATCH
    queries = qkv[:, :body_count, :width].reshape(N_BATCH, group, body_count, HEADS, head_dim)
    keys = qkv[:, :, width:2 * width].reshape(N_BATCH, group, span, HEADS, head_dim)
    values = qkv[:, :, 2 * width:].reshape(N_BATCH, group, span, HEADS, head_dim)
    mixed = lax.map(jax.checkpoint(attend), (queries, keys, values))
    mixed = low_back(low(mixed.reshape(items, body_count, width)))
    hidden1 = hidden0[:, :body_count] + low_back(matmul(mixed, w_out) + b_out)
    normed2 = low(layer_norm(hidden1, norm2_gain, norm2_shift))
    upper = low_back(matmul(normed2, w_up) + b_up)
    active = low(jax.nn.gelu(upper, approximate=False))
    hidden2 = hidden1 + low_back(matmul(active, w_down) + b_down)
    normedf = low(layer_norm(hidden2, final_gain, final_shift))
    patches = low_back(low(matmul(normedf, w_head) + b_head))
    chans = w_conv.shape[3]
    edge = side * PATCH
    latent = patches.reshape(items, side, side, PATCH, PATCH, chans).transpose(0, 1, 3, 2, 4, 5)
    latent = latent.reshape(items, edge, edge, chans)
    padded = jnp.pad(latent, ((0, 0), (1, 1), (1, 1), (0, 0)))
    result = jnp.zeros((items, edge, edge, chans), tokens.dtype) + b_conv
    for row_off in range(3):
        for col_off in range(3):
            window = padded[:, row_off:row_off + edge, col_off:col_off + edge]
            result = result + jnp.einsum('byxc,cd->byxd', window, w_conv[row_off, col_off], precision=lax.Precision.HIGHEST)
    result = low_back(result)
    loss = jnp.sum(weights[:, None, None, None] * 0.5 * (result - target) ** 2)
    return (loss, result)

def reference(tokens, skip_tokens, extra_tokens, extra_skip, timesteps, target, w_skip, b_skip, norm1_gain, norm1_shift, w_qkv, w_out, b_out, norm2_gain, norm2_shift, w_up, b_up, w_down, b_down, final_gain, final_shift, w_head, b_head, w_conv, b_conv):
    weights = noise_weight(timesteps)
    floats = [arr.astype(jnp.float32) for arr in (tokens, skip_tokens, extra_tokens, extra_skip, w_skip, b_skip, norm1_gain, norm1_shift, w_qkv, w_out, b_out, norm2_gain, norm2_shift, w_up, b_up, w_down, b_down, final_gain, final_shift, w_head, b_head, w_conv, b_conv)]
    loss, pullback, result = jax.vjp(partial(forward, weights, target.astype(jnp.float32)), *floats, has_aux=True)
    grads = pullback(jnp.ones((), jnp.float32))
    half = jnp.bfloat16
    return (result.astype(half), grads[0].astype(half), grads[1].astype(half), grads[2].astype(half), grads[3].astype(half), grads[4], grads[5], grads[6], grads[7], grads[8], grads[9], grads[10], grads[11], grads[12], grads[13], grads[14], grads[15], grads[16], grads[17], grads[18], grads[19], grads[20], grads[21], grads[22])
```

```python
import functools

import jax
import jax.numpy as jnp
import numpy as np
from jax import lax
from jax.experimental import pallas as pl
from jax.experimental.pallas import tpu as pltpu
from jax.sharding import PartitionSpec as P

HEADS = 12
PATCH = 2
EXTRA_PAD = 8
EPS = 1e-05
BF = jnp.bfloat16
F32 = jnp.float32
PLANE = ("ty", "tx")
ALL = ("batch", "ty", "tx")
MIB = 1024 * 1024


def dot(left, right, left_dim, right_dim):
    return lax.dot_general(
        left, right, (((left_dim,), (right_dim,)), ((), ())), preferred_element_type=F32
    )


def norm_parts(values):
    center = values - jnp.mean(values, -1, keepdims=True)
    scaled = lax.rsqrt(jnp.mean(center * center, -1, keepdims=True) + EPS)
    return center * scaled, scaled


def norm_back(inner, normed, scaled):
    return scaled * (
        inner
        - jnp.mean(inner, -1, keepdims=True)
        - normed * jnp.mean(inner * normed, -1, keepdims=True)
    )


def row_sum(values):
    return jnp.sum(values, 0, keepdims=True)


def gelu_parts(upper):
    spread = 0.5 + 0.5 * lax.erf(upper * np.float32(0.5**0.5))
    bell = jnp.exp(upper * upper * -0.5) * np.float32((2 * np.pi) ** -0.5)
    return upper * spread, spread + upper * bell


def noise_weight(timesteps):
    frac = (timesteps.astype(F32) / 1000.0 + 0.008) / 1.008
    kept = jnp.cos(frac * (0.5 * jnp.pi)) ** 2
    return jnp.minimum(1.0, 5.0 * (1.0 - kept) / kept)


def attend_kernel(
    hidden_ref,
    key_extra_ref,
    value_extra_ref,
    gain_ref,
    shift_ref,
    w_qkv_t_ref,
    w_out_ref,
    b_out_ref,
    normed_ref,
    qkv_ref,
    probs_ref,
    probs_extra_ref,
    mixed_ref,
    hidden1_ref,
):
    width = w_out_ref.shape[0]
    head_dim = width // HEADS
    scale = head_dim ** (-0.5)
    rows = hidden_ref.shape[0] * hidden_ref.shape[2]
    hidden = hidden_ref[...].reshape(rows, width).astype(F32)
    unit, _ = norm_parts(hidden)
    normed = (unit * gain_ref[...] + shift_ref[...]).astype(BF)
    normed_ref[0] = normed
    qkv_ref[0] = dot(w_qkv_t_ref[...], normed, 1, 1).astype(BF)
    live = lax.broadcasted_iota(jnp.int32, (EXTRA_PAD, rows), 0) < 2
    for head in range(HEADS):
        low = head * head_dim
        query = qkv_ref[0, low : low + head_dim, :]
        key = qkv_ref[0, width + low : width + low + head_dim, :]
        value = qkv_ref[0, 2 * width + low : 2 * width + low + head_dim, :]
        scores = dot(key, query, 0, 0) * scale
        scores_extra = jnp.where(live, dot(key_extra_ref[0, head], query, 1, 0) * scale, -1e30)
        top = jnp.maximum(
            jnp.max(scores, 0, keepdims=True), jnp.max(scores_extra, 0, keepdims=True)
        )
        raised = jnp.exp(scores - top)
        raised_extra = jnp.exp(scores_extra - top)
        share = 1.0 / (row_sum(raised) + row_sum(raised_extra))
        probs = (raised * share).astype(BF)
        probs_extra = (raised_extra * share).astype(BF)
        probs_ref[0, head] = probs
        probs_extra_ref[0, head] = probs_extra
        mixed = dot(value, probs, 1, 0) + dot(value_extra_ref[0, head], probs_extra, 0, 0)
        mixed_ref[0, low : low + head_dim, :] = mixed.astype(BF)
    hidden1_ref[0] = hidden + (dot(mixed_ref[0], w_out_ref[...], 0, 0) + b_out_ref[...])


def middle_kernel(
    tile_rows,
    tile_cols,
    tiles_x,
    hidden1_ref,
    gain2_ref,
    shift2_ref,
    w_up_ref,
    b_up_ref,
    w_down_ref,
    b_down_ref,
    gainf_ref,
    shiftf_ref,
    w_head_ref,
    b_head_ref,
    w_conv_ref,
    b_conv_ref,
    weight_ref,
    target_ref,
    active_ref,
    slope_ref,
    normed2_ref,
    result_ref,
    grad_hidden2_ref,
    grad_down_ref,
    grad_head_ref,
    sums_ref,
    head_sum_ref,
    conv_sum_ref,
    conv_bias_ref,
    total,
):
    step = pl.program_id(0)

    @pl.when(step == 0)
    def _():
        unit, _ = norm_parts(hidden1_ref[...])
        normed2_ref[...] = (unit * gain2_ref[...] + shift2_ref[...]).astype(BF)

    upper = dot(normed2_ref[...], w_up_ref[...], 1, 0) + b_up_ref[...]
    active, slope = gelu_parts(upper)
    active = active.astype(BF)
    active_ref[...] = active
    slope_ref[...] = slope.astype(BF)
    part = dot(active, w_down_ref[...], 1, 0)

    @pl.when(step == 0)
    def _():
        total[...] = part

    @pl.when(step > 0)
    def _():
        total[...] += part

    @pl.when(step == pl.num_programs(0) - 1)
    def _():
        items = w_head_ref.shape[0]
        per_item = target_ref.shape[0]
        hidden2 = hidden1_ref[...] + (total[...] + b_down_ref[...])
        unit, scaled = norm_parts(hidden2)
        total[...] = unit
        normedf = (unit * gainf_ref[...] + shiftf_ref[...]).astype(BF)
        normed2_final = [normedf[i * per_item : (i + 1) * per_item] for i in range(items)]
        patches = b_head_ref[...]
        for i in range(items):
            patches = patches + dot(normed2_final[i], w_head_ref[i], 1, 1)
        patches = patches.astype(BF)

        def place(position):
            tile = position // (tile_rows * tile_cols)
            row = (tile // tiles_x) * tile_rows + (position // tile_cols) % tile_rows
            col = (tile % tiles_x) * tile_cols + position % tile_cols
            return row * 1024 + col

        own = place(lax.broadcasted_iota(jnp.int32, (per_item, 1), 0))
        other = place(lax.broadcasted_iota(jnp.int32, (1, per_item), 1))
        shifts = []
        for row_off in range(3):
            for col_off in range(3):
                wanted = own + ((row_off - 1) * 1024 + (col_off - 1))
                shifts.append(jnp.where(wanted == other, 1.0, 0.0).astype(BF))
        windows = [dot(shift, patches, 1, 0).astype(BF) for shift in shifts]
        result = b_conv_ref[...]
        for k in range(9):
            result = result + dot(windows[k], w_conv_ref[k], 1, 0)
        result_ref[...] = result.astype(BF)
        grad_result = (weight_ref[...] * (result - target_ref[...])).astype(BF)
        conv_bias_ref[...] = row_sum(grad_result.astype(F32))
        grad_patches = jnp.zeros(target_ref.shape, F32)
        for k in range(9):
            conv_sum_ref[k] = dot(windows[k], grad_result, 0, 0)
            moved = dot(shifts[8 - k], grad_result, 1, 0).astype(BF)
            grad_patches = grad_patches + dot(moved, w_conv_ref[k], 1, 1)
        grad_patches = grad_patches.astype(BF)
        grad_head_ref[...] = row_sum(grad_patches.astype(F32))
        sum_gain = jnp.zeros((1, unit.shape[1]), F32)
        sum_shift = sum_gain
        sum_down = sum_gain
        for i in range(items):
            rows = slice(i * per_item, (i + 1) * per_item)
            head_sum_ref[i] = dot(grad_patches, normed2_final[i], 0, 0)
            grad_normedf = dot(grad_patches, w_head_ref[i], 1, 0)
            unit_part = total[rows]
            sum_gain = sum_gain + row_sum(grad_normedf * unit_part)
            sum_shift = sum_shift + row_sum(grad_normedf)
            grad_hidden2 = norm_back(grad_normedf * gainf_ref[...], unit_part, scaled[rows])
            grad_hidden2_ref[rows] = grad_hidden2
            grad_down = grad_hidden2.astype(BF)
            grad_down_ref[rows] = grad_down
            sum_down = sum_down + row_sum(grad_down.astype(F32))
        sums_ref[0:1] = sum_gain
        sums_ref[1:2] = sum_shift
        sums_ref[2:3] = sum_down


def down_kernel(active_ref, grad_down_ref, grad_w_ref):
    grad_w_ref[...] = dot(active_ref[...], grad_down_ref[...], 0, 0).astype(BF)


def up_kernel(
    slope_ref,
    grad_down_ref,
    w_down_ref,
    w_up_ref,
    normed2_ref,
    hidden1_ref,
    gain2_ref,
    grad_hidden2_ref,
    grad_w_up_ref,
    grad_b_up_ref,
    grad_hidden1_ref,
    sums_ref,
    total,
):
    step = pl.program_id(0)
    grad_active = dot(grad_down_ref[...], w_down_ref[...], 1, 1)
    grad_upper = (grad_active * slope_ref[...].astype(F32)).astype(BF)
    grad_b_up_ref[...] = row_sum(grad_upper.astype(F32))
    grad_w_up_ref[...] = dot(normed2_ref[...], grad_upper, 0, 0).astype(BF)
    part = dot(grad_upper, w_up_ref[...], 1, 1)

    @pl.when(step == 0)
    def _():
        total[...] = part

    @pl.when(step > 0)
    def _():
        total[...] += part

    @pl.when(step == pl.num_programs(0) - 1)
    def _():
        unit, scaled = norm_parts(hidden1_ref[...])
        grad_normed2 = total[...]
        sums_ref[0:1] = row_sum(grad_normed2 * unit)
        sums_ref[1:2] = row_sum(grad_normed2)
        grad_hidden1 = grad_hidden2_ref[...] + norm_back(
            grad_normed2 * gain2_ref[...], unit, scaled
        )
        grad_hidden1_ref[...] = grad_hidden1
        sums_ref[2:3] = row_sum(grad_hidden1.astype(BF).astype(F32))


def attend_back_kernel(
    hidden_ref,
    grad_hidden1_ref,
    mixed_ref,
    qkv_ref,
    probs_ref,
    probs_extra_ref,
    key_extra_ref,
    value_extra_ref,
    gain_ref,
    w_qkv_t_ref,
    w_out_ref,
    grad_qkv_ref,
    grad_key_extra_ref,
    grad_value_extra_ref,
    grad_hidden0_ref,
    grad_w_out_ref,
    sums_ref,
    grad_mixed_ref,
    out_total,
):
    step = pl.program_id(0)
    width = w_out_ref.shape[0]
    head_dim = width // HEADS
    scale = head_dim ** (-0.5)
    rows = hidden_ref.shape[0] * hidden_ref.shape[2]
    grad_hidden1 = grad_hidden1_ref[0]
    grad_branch = grad_hidden1.astype(BF)
    part = dot(mixed_ref[0], grad_branch, 1, 0)

    @pl.when(step == 0)
    def _():
        out_total[...] = part
        sums_ref[...] = jnp.zeros_like(sums_ref)

    @pl.when(step > 0)
    def _():
        out_total[...] += part

    @pl.when(step == pl.num_programs(0) - 1)
    def _():
        grad_w_out_ref[...] = out_total[...].astype(BF)

    grad_mixed_ref[...] = dot(w_out_ref[...], grad_branch, 1, 1).astype(BF)
    for head in range(HEADS):
        low = head * head_dim
        query = qkv_ref[0, low : low + head_dim, :]
        key = qkv_ref[0, width + low : width + low + head_dim, :]
        value = qkv_ref[0, 2 * width + low : 2 * width + low + head_dim, :]
        grad_mixed = grad_mixed_ref[low : low + head_dim, :]
        probs_low = probs_ref[0, head]
        probs_extra_low = probs_extra_ref[0, head]
        probs = probs_low.astype(F32)
        probs_extra = probs_extra_low.astype(F32)
        grad_probs = dot(value, grad_mixed, 0, 0)
        grad_probs_extra = dot(value_extra_ref[0, head], grad_mixed, 1, 0)
        common = row_sum(grad_probs * probs) + row_sum(grad_probs_extra * probs_extra)
        grad_scores = (probs * (grad_probs - common)).astype(BF)
        grad_scores_extra = (probs_extra * (grad_probs_extra - common)).astype(BF)
        grad_query = dot(key, grad_scores, 1, 0) + dot(
            key_extra_ref[0, head], grad_scores_extra, 0, 0
        )
        grad_key = dot(query, grad_scores, 1, 1)
        grad_value = dot(grad_mixed, probs_low, 1, 1)
        grad_key_extra_ref[0, head] = dot(grad_scores_extra, query, 1, 1) * scale
        grad_value_extra_ref[0, head] = dot(probs_extra_low, grad_mixed, 1, 1)
        grad_qkv_ref[0, low : low + head_dim, :] = (grad_query * scale).astype(BF)
        grad_qkv_ref[0, width + low : width + low + head_dim, :] = (grad_key * scale).astype(BF)
        grad_qkv_ref[0, 2 * width + low : 2 * width + low + head_dim, :] = grad_value.astype(BF)
    grad_normed = dot(grad_qkv_ref[0], w_qkv_t_ref[...], 0, 0)
    unit, scaled = norm_parts(hidden_ref[...].reshape(rows, width).astype(F32))
    sums_ref[0:1] += row_sum(grad_normed * unit)
    sums_ref[1:2] += row_sum(grad_normed)
    grad_hidden0 = grad_hidden1 + norm_back(grad_normed * gain_ref[...], unit, scaled)
    grad_low = grad_hidden0.astype(BF)
    sums_ref[2:3] += row_sum(grad_low.astype(F32))
    grad_hidden0_ref[...] = grad_low.reshape(grad_hidden0_ref.shape)


def qkv_weight_kernel(normed_ref, grad_qkv_ref, normed_extra_ref, grad_extra_ref, grad_w_ref):
    total = dot(normed_extra_ref[...], grad_extra_ref[...], 0, 0)
    for item in range(normed_ref.shape[0]):
        total = total + dot(normed_ref[item], grad_qkv_ref[item], 0, 1)
    grad_w_ref[...] = total.astype(BF)


def skip_weight_kernel(joined_ref, grad_ref, joined_extra_ref, grad_extra_ref, grad_w_ref):
    total = dot(joined_extra_ref[...], grad_extra_ref[...], 0, 0)
    grad_w_ref[...] = (total + dot(joined_ref[...], grad_ref[...], 0, 0)).astype(BF)


def whole(shape):
    return pl.BlockSpec(shape, lambda *_: (0,) * len(shape), pipeline_mode=pl.Buffered(1))


def params(mib):
    return pltpu.CompilerParams(vmem_limit_bytes=mib * MIB)


def cost(flops, moved, transcendentals=0):
    return pl.CostEstimate(
        flops=int(flops), bytes_accessed=int(moved), transcendentals=int(transcendentals)
    )


def sds(shape, dtype):
    return jax.ShapeDtypeStruct(shape, dtype)


def swap(block, axis, gap):
    count = lax.axis_size(axis)
    return lax.ppermute(block, axis, [(i, i ^ gap) for i in range(count)])


def halve(parts, axis, gap, dim, place):
    send = lax.dynamic_index_in_dim(parts, 1 - place, dim, keepdims=False)
    keep = lax.dynamic_index_in_dim(parts, place, dim, keepdims=False)
    return keep + swap(send, axis, gap)


def scatter_sum(grad, order):
    batch = lax.axis_size("batch")
    down, across = lax.axis_size("ty"), lax.axis_size("tx")
    at_y, at_x = lax.axis_index("ty"), lax.axis_index("tx")
    rows = grad.shape[0] // (batch * down * across)
    parts = grad.reshape(batch, down, across // 2, 2, rows, grad.shape[1])
    parts = halve(parts, "tx", 1, 3, at_x % 2)
    if order == "xy":
        parts = halve(parts, "tx", 2, 2, at_x // 2)
        parts = halve(parts, "ty", 1, 1, at_y)
    else:
        parts = halve(parts, "ty", 1, 1, at_y)
        parts = halve(parts, "tx", 2, 1, at_x // 2)
    parts = lax.all_to_all(parts, "batch", split_axis=0, concat_axis=0, tiled=True)
    return jnp.sum(parts.astype(F32), 0)


def scatter_sum_halves(grad):
    half = grad.shape[1] // 2
    return jnp.concatenate(
        [scatter_sum(grad[:, :half], "xy"), scatter_sum(grad[:, half:], "yx")], 1
    )


def conv_map():
    table = np.zeros((9, 9, 4, 4), np.float32)
    for row_off in range(3):
        for col_off in range(3):
            for p in range(4):
                for q in range(4):
                    i = 2 * (row_off - 1) + p // 2 - q // 2 + 1
                    j = 2 * (col_off - 1) + p % 2 - q % 2 + 1
                    if 0 <= i < 3 and 0 <= j < 3:
                        table[i * 3 + j, row_off * 3 + col_off, p, q] = 1.0
    return table


def per_device(
    tokens,
    skip_tokens,
    extra_tokens,
    extra_skip,
    timesteps,
    target,
    w_skip,
    b_skip,
    norm1_gain,
    norm1_shift,
    w_qkv,
    w_out,
    b_out,
    norm2_gain,
    norm2_shift,
    w_up,
    b_up,
    w_down,
    b_down,
    final_gain,
    final_shift,
    w_head,
    b_head,
    w_conv,
    b_conv,
):
    items, rows, cols, width = tokens.shape
    hidden_units = w_up.shape[1]
    local = rows * cols
    patch_values = w_head.shape[1]
    chans = w_conv.shape[3]
    devices = lax.axis_size(ALL)
    groups = lax.axis_size(PLANE)
    place = lax.axis_index(PLANE)
    share = items // groups
    per_item = groups * local
    count = share * per_item
    head_dim = width // HEADS
    height, breadth = rows * PATCH, cols * PATCH

    def row(vector):
        return vector.astype(F32).reshape(1, -1)

    def to_items(array):
        return lax.all_to_all(array, PLANE, split_axis=0, concat_axis=0, tiled=True)

    body = tokens.reshape(items * local, width)
    body_skip = skip_tokens.reshape(items * local, width)
    hidden0 = (
        dot(body, w_skip[:width], 1, 0) + dot(body_skip, w_skip[width:], 1, 0) + row(b_skip)
    ).astype(BF)
    hidden0 = to_items(hidden0.reshape(items, local, width)).reshape(groups, share, local, width)

    start = place * share
    joined_extra = jnp.concatenate(
        [
            lax.dynamic_slice_in_dim(extra_tokens, start, share, 0),
            lax.dynamic_slice_in_dim(extra_skip, start, share, 0),
        ],
        2,
    ).reshape(share * 2, 2 * width)
    hidden_extra = dot(joined_extra, w_skip, 1, 0) + row(b_skip)
    unit_extra, scaled_extra = norm_parts(hidden_extra)
    normed_extra = (unit_extra * row(norm1_gain) + row(norm1_shift)).astype(BF)
    pairs_extra = dot(normed_extra, w_qkv[:, width:], 1, 0).astype(BF)

    def by_head(block):
        block = block.reshape(share, 2, HEADS, head_dim).transpose(0, 2, 1, 3)
        return jnp.pad(block, ((0, 0), (0, 0), (0, EXTRA_PAD - 2), (0, 0)))

    key_extra = by_head(pairs_extra[:, :width])
    value_extra = by_head(pairs_extra[:, width:])

    target_patches = (
        target.reshape(items, rows, PATCH, cols, PATCH, chans)
        .transpose(0, 1, 3, 2, 4, 5)
        .reshape(items, local, patch_values)
    )
    target_own = (
        to_items(target_patches)
        .reshape(groups, share, local, patch_values)
        .transpose(0, 2, 1, 3)
        .reshape(per_item, share * patch_values)
    )
    weight = lax.dynamic_slice_in_dim(noise_weight(timesteps), start, share, 0)
    weight_lanes = jnp.repeat(weight, patch_values).reshape(1, -1)
    table = jnp.asarray(conv_map())
    kernel = jnp.einsum(
        "tkpq,tcd->kpcqd",
        table,
        w_conv.astype(F32).reshape(9, chans, chans),
        precision=lax.Precision.HIGHEST,
    ).reshape(9, patch_values, patch_values)
    eye = jnp.eye(share, dtype=F32)
    kernel = (
        (eye[None, :, None, :, None] * kernel[:, None, :, None, :])
        .reshape(9, share * patch_values, share * patch_values)
        .astype(BF)
    )
    head_lanes = (eye[:, :, None, None] * w_head.T.astype(F32)[None, None]).reshape(
        share, share * patch_values, width
    ).astype(BF)
    lanes = share * patch_values
    b_head_lanes = jnp.tile(row(b_head), (1, share))
    b_conv_lanes = jnp.tile(row(b_conv), (1, lanes // chans))

    w_qkv_t = w_qkv.T
    item_block = pl.BlockSpec((groups, 1, local, width), lambda i: (0, i, 0, 0))

    def per_share(*shape):
        return pl.BlockSpec((1,) + shape, lambda i: (i,) + (0,) * len(shape))

    normed1, qkv, probs, probs_extra, mixed, hidden1 = pl.pallas_call(
        attend_kernel,
        grid=(share,),
        in_specs=[
            item_block,
            per_share(HEADS, EXTRA_PAD, head_dim),
            per_share(HEADS, EXTRA_PAD, head_dim),
            whole((1, width)),
            whole((1, width)),
            whole((3 * width, width)),
            whole((width, width)),
            whole((1, width)),
        ],
        out_specs=[
            per_share(per_item, width),
            per_share(3 * width, per_item),
            per_share(HEADS, per_item, per_item),
            per_share(HEADS, EXTRA_PAD, per_item),
            per_share(width, per_item),
            per_share(per_item, width),
        ],
        out_shape=[
            sds((share, per_item, width), BF),
            sds((share, 3 * width, per_item), BF),
            sds((share, HEADS, per_item, per_item), BF),
            sds((share, HEADS, EXTRA_PAD, per_item), BF),
            sds((share, width, per_item), BF),
            sds((share, per_item, width), F32),
        ],
        compiler_params=params(48),
        cost_estimate=cost(count * (8 * width * width + 16 * per_item * width), 25e6, 3e6),
        name="attend",
    )(
        hidden0,
        key_extra,
        value_extra,
        row(norm1_gain),
        row(norm1_shift),
        w_qkv_t,
        w_out,
        row(b_out),
    )
    hidden1 = hidden1.reshape(count, width)

    chunk = 512
    chunks = hidden_units // chunk
    by_col = pl.BlockSpec((count, chunk), lambda j: (0, j))
    (
        active,
        slope,
        normed2,
        result,
        grad_hidden2,
        grad_down,
        grad_head,
        sums_final,
        head_sum,
        conv_sum,
        conv_bias,
    ) = pl.pallas_call(
        functools.partial(middle_kernel, rows, cols, lax.axis_size("tx")),
        grid=(chunks,),
        in_specs=[
            whole((count, width)),
            whole((1, width)),
            whole((1, width)),
            pl.BlockSpec((width, chunk), lambda j: (0, j)),
            pl.BlockSpec((1, chunk), lambda j: (0, j)),
            pl.BlockSpec((chunk, width), lambda j: (j, 0)),
            whole((1, width)),
            whole((1, width)),
            whole((1, width)),
            whole((share, lanes, width)),
            whole((1, lanes)),
            whole((9, lanes, lanes)),
            whole((1, lanes)),
            whole((1, lanes)),
            whole((per_item, lanes)),
        ],
        out_specs=[
            by_col,
            by_col,
            whole((count, width)),
            whole((per_item, lanes)),
            whole((count, width)),
            whole((count, width)),
            whole((1, lanes)),
            whole((8, width)),
            whole((share, lanes, width)),
            whole((9, lanes, lanes)),
            whole((1, lanes)),
        ],
        out_shape=[
            sds((count, hidden_units), BF),
            sds((count, hidden_units), BF),
            sds((count, width), BF),
            sds((per_item, lanes), BF),
            sds((count, width), F32),
            sds((count, width), BF),
            sds((1, lanes), F32),
            sds((8, width), F32),
            sds((share, lanes, width), F32),
            sds((9, lanes, lanes), F32),
            sds((1, lanes), F32),
        ],
        scratch_shapes=[pltpu.VMEM((count, width), F32)],
        compiler_params=params(48),
        cost_estimate=cost(count * 4 * width * hidden_units, 25e6, 5e6),
        name="middle",
    )(
        hidden1,
        row(norm2_gain),
        row(norm2_shift),
        w_up,
        row(b_up),
        w_down,
        row(b_down),
        row(final_gain),
        row(final_shift),
        head_lanes,
        b_head_lanes,
        kernel,
        b_conv_lanes,
        weight_lanes,
        target_own,
    )

    latent = (
        result.reshape(groups, local, share, patch_values)
        .transpose(0, 2, 1, 3)
        .reshape(items, local, patch_values)
    )
    latent = to_items(latent)
    latent_out = (
        latent.reshape(items, rows, cols, PATCH, PATCH, chans)
        .transpose(0, 1, 3, 2, 4, 5)
        .reshape(items, height, breadth, chans)
    )

    grad_w_down = pl.pallas_call(
        down_kernel,
        grid=(chunks,),
        in_specs=[by_col, whole((count, width))],
        out_specs=pl.BlockSpec((chunk, width), lambda j: (j, 0)),
        out_shape=sds((hidden_units, width), BF),
        compiler_params=params(48),
        cost_estimate=cost(count * 2 * width * hidden_units, 11e6),
        name="down_weight",
    )(active, grad_down)

    grad_w_up, grad_b_up, grad_hidden1, sums_up = pl.pallas_call(
        up_kernel,
        grid=(chunks,),
        in_specs=[
            by_col,
            whole((count, width)),
            pl.BlockSpec((chunk, width), lambda j: (j, 0)),
            pl.BlockSpec((width, chunk), lambda j: (0, j)),
            whole((count, width)),
            whole((count, width)),
            whole((1, width)),
            whole((count, width)),
        ],
        out_specs=[
            pl.BlockSpec((width, chunk), lambda j: (0, j)),
            pl.BlockSpec((1, chunk), lambda j: (0, j)),
            whole((count, width)),
            whole((8, width)),
        ],
        out_shape=[
            sds((width, hidden_units), BF),
            sds((1, hidden_units), F32),
            sds((count, width), F32),
            sds((8, width), F32),
        ],
        scratch_shapes=[pltpu.VMEM((count, width), F32)],
        compiler_params=params(48),
        cost_estimate=cost(count * 6 * width * hidden_units, 25e6),
        name="up_weight",
    )(slope, grad_down, w_down, w_up, normed2, hidden1, row(norm2_gain), grad_hidden2)

    grad_qkv, grad_key_extra, grad_value_extra, grad_hidden0, grad_w_out, sums_attend = (
        pl.pallas_call(
            attend_back_kernel,
            grid=(share,),
            in_specs=[
                item_block,
                per_share(per_item, width),
                per_share(width, per_item),
                per_share(3 * width, per_item),
                per_share(HEADS, per_item, per_item),
                per_share(HEADS, EXTRA_PAD, per_item),
                per_share(HEADS, EXTRA_PAD, head_dim),
                per_share(HEADS, EXTRA_PAD, head_dim),
                whole((1, width)),
                whole((3 * width, width)),
                whole((width, width)),
            ],
            out_specs=[
                per_share(3 * width, per_item),
                per_share(HEADS, EXTRA_PAD, head_dim),
                per_share(HEADS, EXTRA_PAD, head_dim),
                item_block,
                whole((width, width)),
                whole((8, width)),
            ],
            out_shape=[
                sds((share, 3 * width, per_item), BF),
                sds((share, HEADS, EXTRA_PAD, head_dim), F32),
                sds((share, HEADS, EXTRA_PAD, head_dim), F32),
                sds((groups, share, local, width), BF),
                sds((width, width), BF),
                sds((8, width), F32),
            ],
            scratch_shapes=[pltpu.VMEM((width, per_item), BF), pltpu.VMEM((width, width), F32)],
            compiler_params=params(56),
            cost_estimate=cost(count * (10 * width * width + 32 * per_item * width), 30e6),
            name="attend_back",
        )(
            hidden0,
            grad_hidden1.reshape(share, per_item, width),
            mixed,
            qkv,
            probs,
            probs_extra,
            key_extra,
            value_extra,
            row(norm1_gain),
            w_qkv_t,
            w_out,
        )
    )
    grad_hidden_tile = to_items(grad_hidden0.reshape(items, local, width))

    def from_head(block):
        return block[:, :, :2].transpose(0, 2, 1, 3).reshape(share * 2, width)

    grad_pairs = jnp.concatenate(
        [from_head(grad_key_extra), from_head(grad_value_extra)], 1
    ).astype(BF)
    grad_normed_extra = dot(grad_pairs, w_qkv[:, width:], 1, 1)
    grad_extra = norm_back(grad_normed_extra * row(norm1_gain), unit_extra, scaled_extra)
    grad_extra = grad_extra.astype(BF)
    grad_joined_extra = dot(grad_extra, w_skip, 1, 1).astype(BF)
    grad_joined_extra = to_items(
        jnp.tile(grad_joined_extra.reshape(1, share * 2, 2 * width), (groups, 1, 1))
    ).reshape(items, 2, 2 * width)

    grad_qkv_extra = jnp.concatenate([jnp.zeros((share * 2, width), BF), grad_pairs], 1)
    pad_extra = (-2 * share) % 16
    normed_extra_pad = jnp.pad(normed_extra, ((0, pad_extra), (0, 0)))
    grad_qkv_extra_pad = jnp.pad(grad_qkv_extra, ((0, pad_extra), (0, 0)))
    block = 384
    grad_w_qkv = pl.pallas_call(
        qkv_weight_kernel,
        grid=(3 * width // block,),
        in_specs=[
            whole((share, per_item, width)),
            pl.BlockSpec((share, block, per_item), lambda j: (0, j, 0)),
            whole(normed_extra_pad.shape),
            pl.BlockSpec((normed_extra_pad.shape[0], block), lambda j: (0, j)),
        ],
        out_specs=pl.BlockSpec((width, block), lambda j: (0, j)),
        out_shape=sds((width, 3 * width), BF),
        compiler_params=params(40),
        cost_estimate=cost(count * 6 * width * width, 9e6),
        name="qkv_weight",
    )(normed1, grad_qkv, normed_extra_pad, grad_qkv_extra_pad)

    joined_extra_pad = jnp.pad(joined_extra, ((0, pad_extra), (0, 0)))
    grad_extra_pad = jnp.pad(grad_extra, ((0, pad_extra), (0, 0)))
    grad_tile = grad_hidden_tile.reshape(items * local, width)

    def skip_weight(side, extra_side):
        return pl.pallas_call(
            skip_weight_kernel,
            grid=(2,),
            in_specs=[
                pl.BlockSpec((items * local, width // 2), lambda j: (0, j)),
                whole((items * local, width)),
                pl.BlockSpec((joined_extra_pad.shape[0], width // 2), lambda j: (0, j)),
                whole(grad_extra_pad.shape),
            ],
            out_specs=pl.BlockSpec((width // 2, width), lambda j: (j, 0)),
            out_shape=sds((width, width), BF),
            compiler_params=params(40),
            cost_estimate=cost(count * 2 * width * width, 4e6),
            name="skip_weight",
        )(side, grad_tile, extra_side, grad_extra_pad)

    grad_w_skip = jnp.concatenate(
        [
            skip_weight(body, joined_extra_pad[:, :width]),
            skip_weight(body_skip, joined_extra_pad[:, width:]),
        ],
        0,
    )
    grad_tokens = dot(grad_tile, w_skip[:width], 1, 1).astype(BF).reshape(tokens.shape)
    grad_skip_tokens = dot(grad_tile, w_skip[width:], 1, 1).astype(BF).reshape(tokens.shape)

    sum_down = scatter_sum_halves(grad_w_down)
    sum_up = scatter_sum_halves(grad_w_up)
    sum_out = scatter_sum(grad_w_out, "xy")
    sum_qkv = scatter_sum_halves(grad_w_qkv)
    sum_skip = scatter_sum_halves(grad_w_skip)

    shared = jnp.concatenate(
        [
            jnp.sum(grad_head.reshape(share, patch_values), 0),
            jnp.einsum(
                "tkpq,kpcqd->tcd",
                table,
                jnp.einsum(
                    "kicid->kcd",
                    conv_sum.reshape(9, share, patch_values, share, patch_values),
                ).reshape(9, PATCH * PATCH, chans, PATCH * PATCH, chans),
                precision=lax.Precision.HIGHEST,
            ).reshape(-1),
            jnp.sum(conv_bias.reshape(-1, chans), 0),
        ]
    )
    grad_w_head = sum(
        head_sum[i, i * patch_values : (i + 1) * patch_values] for i in range(share)
    )
    vectors = [
        sums_attend[2] + row_sum(grad_extra.astype(F32))[0],
        sums_attend[0] + row_sum(grad_normed_extra * unit_extra)[0],
        sums_attend[1] + row_sum(grad_normed_extra)[0],
        sums_up[2],
        sums_up[0],
        sums_up[1],
        grad_b_up[0],
        sums_final[2],
        sums_final[0],
        sums_final[1],
    ]
    pieces = [vector.reshape(devices, -1) for vector in vectors]
    pieces.append(grad_w_head.T.reshape(devices, -1))
    pieces.append(jnp.tile(shared.reshape(1, -1), (devices, 1)))
    packed = jnp.concatenate(pieces, 1)
    packed = jnp.pad(packed, ((0, 0), (0, (-packed.shape[1]) % 128)))
    packed = lax.all_to_all(packed, ALL, split_axis=0, concat_axis=0, tiled=True)
    summed = jnp.sum(packed, 0)
    small = []
    offset = 0
    for piece in pieces:
        small.append(summed[offset : offset + piece.shape[1]])
        offset = offset + piece.shape[1]
    shared = small[11]
    conv_size = 9 * chans * chans
    return (
        latent_out,
        grad_tokens,
        grad_skip_tokens,
        grad_joined_extra[..., :width],
        grad_joined_extra[..., width:],
        sum_skip,
        small[0],
        small[1],
        small[2],
        sum_qkv,
        sum_out,
        small[3],
        small[4],
        small[5],
        sum_up,
        small[6],
        sum_down,
        small[7],
        small[8],
        small[9],
        small[10].reshape(width // devices, patch_values),
        shared[:patch_values],
        shared[patch_values : patch_values + conv_size].reshape(w_conv.shape),
        shared[patch_values + conv_size :],
    )


def solution(mesh):
    tiles = P("batch", "ty", "tx", None)
    pairs = P("batch", None, None)
    matrix = P(ALL, None)
    vector = P(ALL)
    return jax.shard_map(
        per_device,
        mesh=mesh,
        in_specs=(tiles, tiles, pairs, pairs, P("batch"), tiles) + (P(),) * 19,
        out_specs=(
            tiles,
            tiles,
            tiles,
            pairs,
            pairs,
            matrix,
            vector,
            vector,
            vector,
            matrix,
            matrix,
            vector,
            vector,
            vector,
            matrix,
            vector,
            matrix,
            vector,
            vector,
            vector,
            matrix,
            P(),
            P(),
            P(),
        ),
        check_vma=False,
    )
```

```python
import functools

import jax
import jax.numpy as jnp
import numpy as np
from jax import lax
from jax.experimental import pallas as pl
from jax.experimental.pallas import tpu as pltpu
from jax.sharding import PartitionSpec as P

HEADS = 12
PATCH = 2
EXTRA_PAD = 8
EPS = 1e-05
BF = jnp.bfloat16
F32 = jnp.float32
PLANE = ("ty", "tx")
ALL = ("batch", "ty", "tx")
MIB = 1024 * 1024


def dot(left, right, left_dim, right_dim):
    return lax.dot_general(
        left, right, (((left_dim,), (right_dim,)), ((), ())), preferred_element_type=F32
    )


def norm_parts(values):
    center = values - jnp.mean(values, -1, keepdims=True)
    scaled = lax.rsqrt(jnp.mean(center * center, -1, keepdims=True) + EPS)
    return center * scaled, scaled


def norm_back(inner, normed, scaled):
    return scaled * (
        inner
        - jnp.mean(inner, -1, keepdims=True)
        - normed * jnp.mean(inner * normed, -1, keepdims=True)
    )


def row_sum(values):
    return jnp.sum(values, 0, keepdims=True)


def gelu_parts(upper):
    spread = 0.5 + 0.5 * lax.erf(upper * np.float32(0.5**0.5))
    bell = jnp.exp(upper * upper * -0.5) * np.float32((2 * np.pi) ** -0.5)
    return upper * spread, spread + upper * bell


def noise_weight(timesteps):
    frac = (timesteps.astype(F32) / 1000.0 + 0.008) / 1.008
    kept = jnp.cos(frac * (0.5 * jnp.pi)) ** 2
    return jnp.minimum(1.0, 5.0 * (1.0 - kept) / kept)


def can_split(own):
    return own % 8 == 0


def store_split(value, own, lane_refs):
    if len(lane_refs) == 1:
        lane_refs[0][...] = value.astype(BF)
        return
    keep_ref, send_ref, core_ref = lane_refs
    pairs = value.reshape(value.shape[0] // (2 * own), 2, own, value.shape[1])
    first = core_ref[0] == 0
    keep = jnp.where(first, pairs[:, 0], pairs[:, 1])
    send = jnp.where(first, pairs[:, 1], pairs[:, 0])
    keep_ref[...] = keep.astype(BF)
    send_ref[...] = send.astype(BF)


def merge_kernel(tokens_ref, skip_ref, w_skip_ref, b_skip_ref, hidden_ref, body_ref, body_skip_ref):
    width = w_skip_ref.shape[1]
    local = tokens_ref.shape[1] * tokens_ref.shape[2]
    body = tokens_ref[...].reshape(-1, width)
    body_skip = skip_ref[...].reshape(-1, width)
    hidden = (
        dot(body, w_skip_ref[:width], 1, 0)
        + dot(body_skip, w_skip_ref[width:], 1, 0)
        + b_skip_ref[...].astype(F32).reshape(1, width)
    )
    hidden_ref[...] = hidden.astype(BF).reshape(-1, local, width)
    body_ref[...] = body.reshape(-1, local, width)
    body_skip_ref[...] = body_skip.reshape(-1, local, width)


def attend_kernel(
    hidden_ref,
    key_extra_ref,
    value_extra_ref,
    vectors_ref,
    w_qkv_t_ref,
    w_out_ref,
    normed_ref,
    qkv_ref,
    probs_ref,
    probs_extra_ref,
    mixed_ref,
    hidden1_ref,
):
    width = w_out_ref.shape[0]
    head_dim = width // HEADS
    scale = head_dim ** (-0.5)
    rows = hidden_ref.shape[0] * hidden_ref.shape[2]
    hidden = hidden_ref[...].reshape(rows, width).astype(F32)
    unit, _ = norm_parts(hidden)
    normed = (unit * vectors_ref[0:1] + vectors_ref[1:2]).astype(BF)
    normed_ref[0] = normed
    qkv_ref[0] = dot(w_qkv_t_ref[...], normed, 1, 1).astype(BF)
    live = lax.broadcasted_iota(jnp.int32, (EXTRA_PAD, rows), 0) < 2
    for head in range(HEADS):
        low = head * head_dim
        query = qkv_ref[0, low : low + head_dim, :]
        key = qkv_ref[0, width + low : width + low + head_dim, :]
        value = qkv_ref[0, 2 * width + low : 2 * width + low + head_dim, :]
        scores = dot(key, query, 0, 0) * scale
        scores_extra = jnp.where(live, dot(key_extra_ref[0, head], query, 1, 0) * scale, -1e30)
        top = jnp.maximum(
            jnp.max(scores, 0, keepdims=True), jnp.max(scores_extra, 0, keepdims=True)
        )
        raised = jnp.exp(scores - top)
        raised_extra = jnp.exp(scores_extra - top)
        share = 1.0 / (row_sum(raised) + row_sum(raised_extra))
        probs = (raised * share).astype(BF)
        probs_extra = (raised_extra * share).astype(BF)
        probs_ref[0, head] = probs
        probs_extra_ref[0, head] = probs_extra
        mixed = dot(value, probs, 1, 0) + dot(value_extra_ref[0, head], probs_extra, 0, 0)
        mixed_ref[0, low : low + head_dim, :] = mixed.astype(BF)
    hidden1_ref[0] = hidden + (dot(mixed_ref[0], w_out_ref[...], 0, 0) + vectors_ref[2:3])


def middle_kernel(
    tile_rows,
    tile_cols,
    tiles_x,
    hidden1_ref,
    vectors_ref,
    w_up_ref,
    w_down_ref,
    w_head_ref,
    w_conv_ref,
    lanes_ref,
    target_ref,
    active_ref,
    slope_ref,
    normed2_ref,
    result_ref,
    grad_hidden2_ref,
    grad_down_ref,
    grad_head_ref,
    sums_ref,
    head_sum_ref,
    conv_sum_ref,
    conv_bias_ref,
    total,
):
    step = pl.program_id(0)

    @pl.when(step == 0)
    def _():
        unit, _ = norm_parts(hidden1_ref[...])
        normed2_ref[...] = (unit * vectors_ref[3:4] + vectors_ref[4:5]).astype(BF)

    upper = dot(normed2_ref[...], w_up_ref[...], 1, 0) + vectors_ref[pl.ds(8 + step, 1)]
    active, slope = gelu_parts(upper)
    active = active.astype(BF)
    active_ref[...] = active
    slope_ref[...] = slope.astype(BF)
    part = dot(active, w_down_ref[...], 1, 0)

    @pl.when(step == 0)
    def _():
        total[...] = part

    @pl.when(step > 0)
    def _():
        total[...] += part

    @pl.when(step == pl.num_programs(0) - 1)
    def _():
        per_item, lanes = target_ref.shape
        patch_values, width = w_head_ref.shape
        items = lanes // patch_values

        def head_of(i):
            parts = [w_head_ref[...]]
            if i > 0:
                parts = [jnp.zeros((i * patch_values, width), BF)] + parts
            if i < items - 1:
                parts = parts + [jnp.zeros((lanes - (i + 1) * patch_values, width), BF)]
            return jnp.concatenate(parts, 0)

        heads = [head_of(i) for i in range(items)]
        hidden2 = hidden1_ref[...] + (total[...] + vectors_ref[5:6])
        unit, scaled = norm_parts(hidden2)
        total[...] = unit
        normedf = (unit * vectors_ref[6:7] + vectors_ref[7:8]).astype(BF)
        normed2_final = [normedf[i * per_item : (i + 1) * per_item] for i in range(items)]
        patches = lanes_ref[0:1]
        for i in range(items):
            patches = patches + dot(normed2_final[i], heads[i], 1, 1)
        patches = patches.astype(BF)

        def place(position):
            tile = position // (tile_rows * tile_cols)
            row = (tile // tiles_x) * tile_rows + (position // tile_cols) % tile_rows
            col = (tile % tiles_x) * tile_cols + position % tile_cols
            return row * 1024 + col

        own = place(lax.broadcasted_iota(jnp.int32, (per_item, 1), 0))
        other = place(lax.broadcasted_iota(jnp.int32, (1, per_item), 1))
        shifts = []
        for row_off in range(3):
            for col_off in range(3):
                wanted = own + ((row_off - 1) * 1024 + (col_off - 1))
                shifts.append(jnp.where(wanted == other, 1.0, 0.0).astype(BF))
        windows = [dot(shift, patches, 1, 0).astype(BF) for shift in shifts]
        result = lanes_ref[1:2]
        for k in range(9):
            result = result + dot(windows[k], w_conv_ref[k], 1, 0)
        result_ref[...] = result.astype(BF)
        grad_result = (lanes_ref[2:3] * (result - target_ref[...])).astype(BF)
        conv_bias_ref[...] = row_sum(grad_result.astype(F32))
        grad_patches = jnp.zeros(target_ref.shape, F32)
        for k in range(9):
            conv_sum_ref[k] = dot(windows[k], grad_result, 0, 0)
            moved = dot(shifts[8 - k], grad_result, 1, 0).astype(BF)
            grad_patches = grad_patches + dot(moved, w_conv_ref[k], 1, 1)
        grad_patches = grad_patches.astype(BF)
        grad_head_ref[...] = row_sum(grad_patches.astype(F32))
        sum_gain = jnp.zeros((1, unit.shape[1]), F32)
        sum_shift = sum_gain
        sum_down = sum_gain
        for i in range(items):
            rows = slice(i * per_item, (i + 1) * per_item)
            head_sum_ref[i] = dot(grad_patches, normed2_final[i], 0, 0)
            grad_normedf = dot(grad_patches, heads[i], 1, 0)
            unit_part = total[rows]
            sum_gain = sum_gain + row_sum(grad_normedf * unit_part)
            sum_shift = sum_shift + row_sum(grad_normedf)
            grad_hidden2 = norm_back(grad_normedf * vectors_ref[6:7], unit_part, scaled[rows])
            grad_hidden2_ref[rows] = grad_hidden2
            grad_down = grad_hidden2.astype(BF)
            grad_down_ref[rows] = grad_down
            sum_down = sum_down + row_sum(grad_down.astype(F32))
        sums_ref[0:1] = sum_gain
        sums_ref[1:2] = sum_shift
        sums_ref[2:3] = sum_down


def core_and_outs(refs, split):
    return (refs[-2], refs[-1], refs[0]) if split else (refs[-1],)


def down_kernel(own, active_ref, grad_down_ref, *refs):
    value = dot(active_ref[...], grad_down_ref[...], 0, 0)
    store_split(value, own, core_and_outs(refs, can_split(own)))


def up_kernel(
    own,
    slope_ref,
    grad_down_ref,
    w_down_ref,
    w_up_ref,
    normed2_ref,
    hidden1_ref,
    vectors_ref,
    grad_hidden2_ref,
    mixed_ref,
    core_ref,
    after_ref,
    grad_b_up_ref,
    grad_hidden1_ref,
    grad_branch_ref,
    sums_ref,
    *rest,
):
    total = rest[-1]
    rest = rest[:-1]
    step = pl.program_id(0)
    steps = pl.num_programs(0)

    def store(value):
        half = value.shape[1] // 2
        for side in range(2):
            piece = value[:, side * half : (side + 1) * half]
            if can_split(own):
                store_split(piece, own, (rest[0].at[side], rest[1].at[side], core_ref))
            else:
                store_split(piece, own, (rest[0].at[side],))

    @pl.when(step < steps - 1)
    def _():
        grad_active = dot(grad_down_ref[...], w_down_ref[...], 1, 1)
        grad_upper = (grad_active * slope_ref[...].astype(F32)).astype(BF)
        grad_b_up_ref[0, 0:1] = row_sum(grad_upper.astype(F32))
        store(dot(normed2_ref[...], grad_upper, 0, 0))
        part = dot(grad_upper, w_up_ref[...], 1, 1)

        @pl.when(step == 0)
        def _():
            total[...] = part

        @pl.when(step > 0)
        def _():
            total[...] += part

    @pl.when(step == steps - 1)
    def _():
        unit, scaled = norm_parts(hidden1_ref[...])
        grad_normed2 = total[...]
        sums_ref[0:1] = row_sum(grad_normed2 * unit)
        sums_ref[1:2] = row_sum(grad_normed2)
        grad_hidden1 = grad_hidden2_ref[...] + norm_back(
            grad_normed2 * vectors_ref[3:4], unit, scaled
        )
        grad_hidden1_ref[...] = grad_hidden1
        grad_branch = grad_hidden1.astype(BF)
        grad_branch_ref[...] = grad_branch
        sums_ref[2:3] = row_sum(grad_branch.astype(F32))
        items, _, per_item = mixed_ref.shape
        value = dot(mixed_ref[0], grad_branch[:per_item], 1, 0)
        for item in range(1, items):
            rows = slice(item * per_item, (item + 1) * per_item)
            value = value + dot(mixed_ref[item], grad_branch[rows], 1, 0)
        store(value)


def attend_back_kernel(
    hidden_ref,
    grad_hidden1_ref,
    grad_branch_ref,
    qkv_ref,
    probs_ref,
    probs_extra_ref,
    key_extra_ref,
    value_extra_ref,
    vectors_ref,
    w_qkv_t_ref,
    w_out_ref,
    sums_in_ref,
    *rest,
):
    (
        grad_qkv_ref,
        grad_key_extra_ref,
        grad_value_extra_ref,
        grad_hidden0_ref,
        sums_ref,
        grad_mixed_ref,
    ) = rest[-6:]
    width = w_out_ref.shape[0]
    head_dim = width // HEADS
    scale = head_dim ** (-0.5)
    rows = hidden_ref.shape[0] * hidden_ref.shape[2]
    grad_mixed_ref[...] = dot(w_out_ref[...], grad_branch_ref[0], 1, 1).astype(BF)
    for head in range(HEADS):
        low = head * head_dim
        query = qkv_ref[0, low : low + head_dim, :]
        key = qkv_ref[0, width + low : width + low + head_dim, :]
        value = qkv_ref[0, 2 * width + low : 2 * width + low + head_dim, :]
        grad_mixed = grad_mixed_ref[low : low + head_dim, :]
        probs_low = probs_ref[0, head]
        probs_extra_low = probs_extra_ref[0, head]
        probs = probs_low.astype(F32)
        probs_extra = probs_extra_low.astype(F32)
        grad_probs = dot(value, grad_mixed, 0, 0)
        grad_probs_extra = dot(value_extra_ref[0, head], grad_mixed, 1, 0)
        common = row_sum(grad_probs * probs) + row_sum(grad_probs_extra * probs_extra)
        grad_scores = (probs * (grad_probs - common)).astype(BF)
        grad_scores_extra = (probs_extra * (grad_probs_extra - common)).astype(BF)
        grad_query = dot(key, grad_scores, 1, 0) + dot(
            key_extra_ref[0, head], grad_scores_extra, 0, 0
        )
        grad_key = dot(query, grad_scores, 1, 1)
        grad_value = dot(grad_mixed, probs_low, 1, 1)
        grad_key_extra_ref[head] = dot(grad_scores_extra, query, 1, 1) * scale
        grad_value_extra_ref[head] = dot(probs_extra_low, grad_mixed, 1, 1)
        grad_qkv_ref[low : low + head_dim, :] = (grad_query * scale).astype(BF)
        grad_qkv_ref[width + low : width + low + head_dim, :] = (grad_key * scale).astype(BF)
        grad_qkv_ref[2 * width + low : 2 * width + low + head_dim, :] = grad_value.astype(BF)
    grad_normed = dot(grad_qkv_ref[...], w_qkv_t_ref[...], 0, 0)
    unit, scaled = norm_parts(hidden_ref[...].reshape(rows, width).astype(F32))
    sums_ref[0:1] = sums_in_ref[0:1] + row_sum(grad_normed * unit)
    sums_ref[1:2] = sums_in_ref[1:2] + row_sum(grad_normed)
    grad_hidden0 = grad_hidden1_ref[0] + norm_back(grad_normed * vectors_ref[0:1], unit, scaled)
    grad_low = grad_hidden0.astype(BF)
    sums_ref[2:3] = sums_in_ref[2:3] + row_sum(grad_low.astype(F32))
    grad_hidden0_ref[...] = grad_low.reshape(grad_hidden0_ref.shape)


def late_weight_kernel(
    own,
    normed_ref,
    normed_extra_ref,
    grad_extra_ref,
    grad_qkv_0_ref,
    grad_qkv_1_ref,
    grad_qkv_2_ref,
    core_ref,
    *rest,
):
    total = dot(normed_extra_ref[...], grad_extra_ref[...], 0, 0)
    for item, ref in enumerate((grad_qkv_0_ref, grad_qkv_1_ref, grad_qkv_2_ref)):
        total = total + dot(normed_ref[item], ref[...], 0, 1)
    if can_split(own):
        store_split(total, own, (rest[-2].at[0], rest[-1].at[0], core_ref))
    else:
        store_split(total, own, (rest[-1].at[0],))


def skip_weight_kernel(
    own, body_ref, body_skip_ref, grad_ref, joined_extra_ref, grad_extra_ref, core_ref, *rest
):
    def store(joined):
        total = dot(joined_extra_ref[...], grad_extra_ref[...], 0, 0)
        total = total + dot(joined, grad_ref[...], 0, 0)
        if can_split(own):
            store_split(total, own, (rest[-2], rest[-1], core_ref))
        else:
            store_split(total, own, (rest[-1],))

    half = pl.num_programs(0) // 2

    @pl.when(pl.program_id(0) < half)
    def _():
        store(body_ref[...])

    @pl.when(pl.program_id(0) >= half)
    def _():
        store(body_skip_ref[...])


def token_kernel(grad_ref, w_skip_ref, *rest):
    tokens_ref, skip_ref = rest[-2:]
    width = w_skip_ref.shape[1]
    grad = grad_ref[...].reshape(-1, width)
    tokens_ref[...] = dot(grad, w_skip_ref[:width], 1, 1).astype(BF).reshape(tokens_ref.shape)
    skip_ref[...] = dot(grad, w_skip_ref[width:], 1, 1).astype(BF).reshape(skip_ref.shape)


def fold_matrix(shape, low, wide, period):
    row = lax.broadcasted_iota(jnp.int32, shape, 0)
    col = lax.broadcasted_iota(jnp.int32, shape, 1)
    return jnp.where((col >= low) & (col < low + wide) & (row % period == col - low), 1.0, 0.0)


def pack_kernel(
    sums_attend_ref,
    sums_extra_ref,
    sums_up_ref,
    sums_final_ref,
    head_sum_ref,
    grad_head_ref,
    conv_sum_ref,
    conv_bias_ref,
    table_ref,
    *rest,
):
    stacked_ref, shared_ref = rest[-2:]
    items, lanes, _ = head_sum_ref.shape
    values = lanes // items
    exact = functools.partial(
        jnp.dot, precision=lax.Precision.HIGHEST, preferred_element_type=F32
    )
    stacked_ref[0:1] = sums_attend_ref[2:3] + sums_extra_ref[2:3]
    stacked_ref[1:2] = sums_attend_ref[0:1] + sums_extra_ref[0:1]
    stacked_ref[2:3] = sums_attend_ref[1:2] + sums_extra_ref[1:2]
    stacked_ref[3:4] = sums_up_ref[2:3]
    stacked_ref[4:6] = sums_up_ref[0:2]
    stacked_ref[6:7] = sums_final_ref[2:3]
    stacked_ref[7:9] = sums_final_ref[0:2]
    head = head_sum_ref[0, 0:values]
    for item in range(1, items):
        head = head + head_sum_ref[item, item * values : (item + 1) * values]
    stacked_ref[9 : 9 + values] = head
    row = lax.broadcasted_iota(jnp.int32, (8, lanes), 0)
    col = lax.broadcasted_iota(jnp.int32, (8, lanes), 1)
    left = jnp.where(col % 4 == row, 1.0, 0.0)
    shared = jnp.zeros((8, 128), F32)
    for tap in range(9):
        picked = conv_sum_ref[0] * table_ref[0, tap].astype(F32)
        for k in range(1, 9):
            picked = picked + conv_sum_ref[k] * table_ref[k, tap].astype(F32)
        shared = shared + exact(exact(left, picked), fold_matrix((lanes, 128), 4 * tap, 4, 4))
    bias = exact(grad_head_ref[...], fold_matrix((lanes, 128), 64, values, values))
    bias = bias + exact(conv_bias_ref[...], fold_matrix((lanes, 128), 96, 4, 4))
    first = lax.broadcasted_iota(jnp.int32, (8, 128), 0) == 0
    shared_ref[...] = shared + jnp.where(first, bias, 0.0)


def whole(shape):
    return pl.BlockSpec(shape, lambda *_: (0,) * len(shape), pipeline_mode=pl.Buffered(1))


def params():
    return pltpu.CompilerParams(vmem_limit_bytes=60 * MIB)


def cost(flops, moved, transcendentals=0):
    del flops, moved, transcendentals
    return pl.CostEstimate(flops=1024, bytes_accessed=1024, transcendentals=0)


def sds(shape, dtype):
    return jax.ShapeDtypeStruct(shape, dtype)


def swap(block, axis, gap):
    count = lax.axis_size(axis)
    return lax.ppermute(block, axis, [(i, i ^ gap) for i in range(count)])


def serve_kernel(tasks, places_ref, *refs):
    del places_ref
    inputs = sum(len(parts) for task in tasks for parts in task["sides"])
    outs = refs[len(refs) - sum(len(task["outs"]) for task in tasks) :]
    at, out_at = 0, 0
    del inputs
    for task in tasks:
        values = []
        for parts in task["sides"]:
            total = refs[at][...].astype(F32)
            for k in range(1, len(parts)):
                total = total + refs[at + k][...].astype(F32)
            at += len(parts)
            values.append(total)
        task["emit"](values, outs[out_at : out_at + len(task["outs"])])
        out_at += len(task["outs"])


def serve(tasks, after, name):
    places, arrays, specs = [], [], []
    for task in tasks:
        for parts in task["sides"]:
            for array, starts, sizes in parts:
                index = []
                for start, size in zip(starts, sizes, strict=True):
                    if isinstance(start, int):
                        index.append(start // size)
                    else:
                        index.append((len(places),))
                        places.append(start)

                def where(_, ref, index=tuple(index)):
                    return tuple(ref[i[0]] if isinstance(i, tuple) else i for i in index)

                arrays.append(array)
                specs.append(pl.BlockSpec(tuple(sizes), where))
    outs = [out for task in tasks for out in task["outs"]]
    moved = sum(2 * int(np.prod(spec.block_shape)) for spec in specs)
    return pl.pallas_call(
        functools.partial(serve_kernel, tasks),
        grid_spec=pltpu.PrefetchScalarGridSpec(
            num_scalar_prefetch=1,
            grid=(1,),
            in_specs=specs + [pl.BlockSpec(memory_space=pl.ANY)] * len(after),
            out_specs=[
                pl.BlockSpec(out.shape, lambda _, ref, n=len(out.shape): (0,) * n) for out in outs
            ],
        ),
        out_shape=outs,
        compiler_params=params(),
        cost_estimate=cost(moved, 2 * moved),
        name=name,
    )(jnp.stack(places).astype(jnp.int32), *arrays, *after)


def emit_low(values, outs):
    for value, out in zip(values, outs, strict=True):
        out[...] = value.astype(BF)


class Sum:
    def __init__(self, grads, units, inner, columns):
        batch = lax.axis_size("batch")
        bits = batch.bit_length() - 1
        rows = sum(grad.size for grad in grads) // (units * columns)
        self.own = rows // lax.axis_size(ALL) // inner
        self.columns = columns
        self.dims = [units] + [2] * bits + [2, 2, 2, inner, self.own, columns]
        self.moves = {"y": bits + 1, "x": bits + 2, "c": bits + 3}
        self.places = {
            "y": lax.axis_index("ty"),
            "x": lax.axis_index("tx") // 2,
            "c": lax.axis_index("tx") % 2,
        }
        self.links = {"y": ("ty", 1), "x": ("tx", 2), "c": ("tx", 1)}
        for bit in range(bits):
            self.moves[bit] = bits - bit
            self.places[bit] = (lax.axis_index("batch") >> bit) % 2
            self.links[bit] = ("batch", 1 << bit)
        self.cut = 0 if units > 1 else len(self.dims) - 3
        self.half = self.dims[self.cut] // 2
        tail = list(range(bits))
        self.orders = [["x", "y"] + tail, ["y", "x"] + tail]
        at = self.moves["c"]
        if len(grads) == 1:
            grad = grads[0].reshape(self.dims)
            keep = lax.dynamic_slice_in_dim(grad, self.places["c"], 1, at)
            send = lax.dynamic_slice_in_dim(grad, 1 - self.places["c"], 1, at)
        else:
            halved = list(self.dims)
            halved[at] = 1
            keep, send = grads[0].reshape(halved), grads[1].reshape(halved)
        self.sent = [send]
        received = swap(send, *self.links["c"])
        self.parts = [[(keep, ("c",)), (received, ("c",))] for _ in range(2)]
        self.done = [["c"], ["c"]]

    def pick(self, part, chosen, side):
        array, fixed = part
        starts, sizes = [0] * array.ndim, list(array.shape)
        for move, where in chosen.items():
            if move not in fixed:
                starts[self.moves[move]] = where
                sizes[self.moves[move]] = 1
        if "side" not in fixed:
            starts[self.cut], sizes[self.cut] = side * self.half, self.half
        return array, starts, sizes

    def task(self):
        sides, outs = [], []
        for side in range(2):
            move = self.orders[side][0]
            chosen = {m: self.places[m] for m in self.done[side]}
            chosen[move] = 1 - self.places[move]
            parts = [self.pick(part, chosen, side) for part in self.parts[side]]
            sides.append(parts)
            outs.append(sds(tuple(parts[0][2]), BF))
        return {"sides": sides, "outs": outs, "emit": emit_low}

    def accept(self, sent):
        for side in range(2):
            move = self.orders[side].pop(0)
            self.done[side].append(move)
            received = swap(sent[side], *self.links[move])
            self.parts[side].append((received, ("side",) + tuple(self.done[side])))

    def last_task(self, layout):
        sides = []
        for side in range(2):
            chosen = {m: self.places[m] for m in self.done[side]}
            sides.append([self.pick(part, chosen, side) for part in self.parts[side]])
        shapes, units = layout
        own, columns, half = self.own, self.columns, self.half

        def emit(values, outs):
            for side in range(2):
                value = values[side].reshape(half, own, columns)
                for k in range(half):
                    out, row, col = units[side * half + k]
                    outs[out][
                        row * own : (row + 1) * own, col * columns : (col + 1) * columns
                    ] = value[k]

        outs = [sds((r * own, c * columns), F32) for r, c in shapes]
        return {"sides": sides, "outs": outs, "emit": emit}


def run_tasks(sums, after, name):
    tasks = []
    for sum_, layout in sums:
        tasks.append(sum_.task() if sum_.orders[0] else sum_.last_task(layout))
    outs = serve(tasks, after, name)
    results, at = [], 0
    for (sum_, _), task in zip(sums, tasks, strict=True):
        got = outs[at : at + len(task["outs"])]
        at += len(task["outs"])
        if sum_.orders[0]:
            sum_.accept(got)
        else:
            results.append(got)
    return outs, results


def conv_map():
    table = np.zeros((9, 9, 4, 4), np.float32)
    for row_off in range(3):
        for col_off in range(3):
            for p in range(4):
                for q in range(4):
                    i = 2 * (row_off - 1) + p // 2 - q // 2 + 1
                    j = 2 * (col_off - 1) + p % 2 - q % 2 + 1
                    if 0 <= i < 3 and 0 <= j < 3:
                        table[i * 3 + j, row_off * 3 + col_off, p, q] = 1.0
    return table


def conv_lanes(share):
    table = conv_map().transpose(1, 0, 2, 3)
    wide = np.kron(np.eye(share, dtype=np.float32), np.ones((16, 16), np.float32))
    small = np.repeat(np.repeat(table, 4, 2), 4, 3)
    return np.tile(small, (1, 1, share, share)) * wide


def per_device(
    tokens,
    skip_tokens,
    extra_tokens,
    extra_skip,
    timesteps,
    target,
    w_skip,
    b_skip,
    norm1_gain,
    norm1_shift,
    w_qkv,
    w_out,
    b_out,
    norm2_gain,
    norm2_shift,
    w_up,
    b_up,
    w_down,
    b_down,
    final_gain,
    final_shift,
    w_head,
    b_head,
    w_conv,
    b_conv,
):
    items, rows, cols, width = tokens.shape
    hidden_units = w_up.shape[1]
    local = rows * cols
    patch_values = w_head.shape[1]
    chans = w_conv.shape[3]
    devices = lax.axis_size(ALL)
    groups = lax.axis_size(PLANE)
    place = lax.axis_index(PLANE)
    share = items // groups
    per_item = groups * local
    count = share * per_item
    head_dim = width // HEADS
    height, breadth = rows * PATCH, cols * PATCH

    def row(vector):
        return vector.astype(F32).reshape(1, -1)

    def to_items(array):
        return lax.all_to_all(array, PLANE, split_axis=0, concat_axis=0, tiled=True)

    some = 4
    tile_block = pl.BlockSpec((some, rows, cols, width), lambda i: (i, 0, 0, 0))
    flat_block = pl.BlockSpec((some, local, width), lambda i: (i, 0, 0))
    hidden0, body, body_skip = pl.pallas_call(
        merge_kernel,
        grid=(items // some,),
        in_specs=[tile_block, tile_block, whole((2 * width, width)), whole((width,))],
        out_specs=[flat_block] * 3,
        out_shape=[sds((items, local, width), BF)] * 3,
        compiler_params=params(),
        cost_estimate=cost(items * local * 4 * width * width, 11e6),
        name="merge",
    )(tokens, skip_tokens, w_skip, b_skip)
    target, _ = lax.optimization_barrier((target, hidden0))
    hidden0 = to_items(hidden0)
    hidden0 = hidden0.reshape(groups, share, local, width)
    body = body.reshape(items * local, width)
    body_skip = body_skip.reshape(items * local, width)

    start = place * share
    joined_extra = jnp.concatenate(
        [
            lax.dynamic_slice_in_dim(extra_tokens, start, share, 0),
            lax.dynamic_slice_in_dim(extra_skip, start, share, 0),
        ],
        2,
    ).reshape(share * 2, 2 * width)
    hidden_extra = dot(joined_extra, w_skip, 1, 0) + row(b_skip)
    unit_extra, scaled_extra = norm_parts(hidden_extra)
    normed_extra = (unit_extra * row(norm1_gain) + row(norm1_shift)).astype(BF)
    pairs_extra = dot(normed_extra, w_qkv[:, width:], 1, 0).astype(BF)

    def by_head(block):
        block = block.reshape(share, 2, HEADS, head_dim).transpose(0, 2, 1, 3)
        return jnp.pad(block, ((0, 0), (0, 0), (0, EXTRA_PAD - 2), (0, 0)))

    key_extra = by_head(pairs_extra[:, :width])
    value_extra = by_head(pairs_extra[:, width:])

    target_patches = (
        target.reshape(items, rows, PATCH, cols, PATCH, chans)
        .transpose(0, 1, 3, 2, 4, 5)
        .reshape(items, local, patch_values)
    )
    target_own = (
        to_items(target_patches)
        .reshape(groups, share, local, patch_values)
        .transpose(0, 2, 1, 3)
        .reshape(per_item, share * patch_values)
    )
    weight = lax.dynamic_slice_in_dim(noise_weight(timesteps), start, share, 0)
    table = jnp.asarray(conv_map())
    lanes = share * patch_values
    spread = jnp.tile(w_conv.reshape(9, chans, chans), (1, lanes // chans, lanes // chans))
    kernel = jnp.sum(jnp.asarray(conv_lanes(share)) * spread[None].astype(F32), 1).astype(BF)
    lane_rows = jnp.concatenate(
        [
            jnp.tile(b_head.astype(F32), share),
            jnp.tile(b_conv.astype(F32), lanes // chans),
            jnp.repeat(weight, patch_values),
        ]
    ).reshape(3, lanes)
    vectors = jnp.concatenate(
        [
            norm1_gain,
            norm1_shift,
            b_out,
            norm2_gain,
            norm2_shift,
            b_down,
            final_gain,
            final_shift,
            b_up,
        ]
    )
    vectors = vectors.astype(F32).reshape(-1, width)

    w_qkv_t = w_qkv.T
    item_block = pl.BlockSpec((groups, 1, local, width), lambda i: (0, i, 0, 0))

    def per_share(*shape):
        return pl.BlockSpec((1,) + shape, lambda i: (i,) + (0,) * len(shape))

    normed1, qkv, probs, probs_extra, mixed, hidden1 = pl.pallas_call(
        attend_kernel,
        grid=(share,),
        in_specs=[
            item_block,
            per_share(HEADS, EXTRA_PAD, head_dim),
            per_share(HEADS, EXTRA_PAD, head_dim),
            whole(vectors.shape),
            whole((3 * width, width)),
            whole((width, width)),
        ],
        out_specs=[
            per_share(per_item, width),
            per_share(3 * width, per_item),
            per_share(HEADS, per_item, per_item),
            per_share(HEADS, EXTRA_PAD, per_item),
            per_share(width, per_item),
            per_share(per_item, width),
        ],
        out_shape=[
            sds((share, per_item, width), BF),
            sds((share, 3 * width, per_item), BF),
            sds((share, HEADS, per_item, per_item), BF),
            sds((share, HEADS, EXTRA_PAD, per_item), BF),
            sds((share, width, per_item), BF),
            sds((share, per_item, width), F32),
        ],
        compiler_params=params(),
        cost_estimate=cost(count * (8 * width * width + 16 * per_item * width), 25e6, 3e6),
        name="attend",
    )(
        hidden0,
        key_extra,
        value_extra,
        vectors,
        w_qkv_t,
        w_out,
    )
    hidden1 = hidden1.reshape(count, width)

    chunk = width
    chunks = hidden_units // chunk
    by_col = pl.BlockSpec((count, chunk), lambda j: (0, j))
    (
        active,
        slope,
        normed2,
        result,
        grad_hidden2,
        grad_down,
        grad_head,
        sums_final,
        head_sum,
        conv_sum,
        conv_bias,
    ) = pl.pallas_call(
        functools.partial(middle_kernel, rows, cols, lax.axis_size("tx")),
        grid=(chunks,),
        in_specs=[
            whole((count, width)),
            whole(vectors.shape),
            pl.BlockSpec((width, chunk), lambda j: (0, j)),
            pl.BlockSpec((chunk, width), lambda j: (j, 0)),
            whole((patch_values, width)),
            whole((9, lanes, lanes)),
            whole((3, lanes)),
            whole((per_item, lanes)),
        ],
        out_specs=[
            by_col,
            by_col,
            whole((count, width)),
            whole((per_item, lanes)),
            whole((count, width)),
            whole((count, width)),
            whole((1, lanes)),
            whole((8, width)),
            whole((share, lanes, width)),
            whole((9, lanes, lanes)),
            whole((1, lanes)),
        ],
        out_shape=[
            sds((count, hidden_units), BF),
            sds((count, hidden_units), BF),
            sds((count, width), BF),
            sds((per_item, lanes), BF),
            sds((count, width), F32),
            sds((count, width), BF),
            sds((1, lanes), F32),
            sds((8, width), F32),
            sds((share, lanes, width), F32),
            sds((9, lanes, lanes), F32),
            sds((1, lanes), F32),
        ],
        scratch_shapes=[pltpu.VMEM((count, width), F32)],
        compiler_params=params(),
        cost_estimate=cost(count * 4 * width * hidden_units, 25e6, 5e6),
        name="middle",
    )(
        hidden1,
        vectors,
        w_up,
        w_down,
        w_head.T,
        kernel,
        lane_rows,
        target_own,
    )

    any_place = pl.BlockSpec(memory_space=pl.ANY)
    core = lax.axis_index("tx") % 2
    core = core.astype(jnp.int32).reshape(1)
    core_spec = pl.BlockSpec(memory_space=pltpu.SMEM)

    def split_outs(units, rows, block_rows, own, cols, index):
        if can_split(own):
            spec = pl.BlockSpec(
                (units, block_rows // (2 * own), own, cols), lambda j: index(j) + (0, 0)
            )
            return spec, lambda n: sds((n, rows // (2 * own), own, cols), BF), 2
        spec = pl.BlockSpec((units, block_rows, cols), lambda j: index(j) + (0,))
        return spec, lambda n: sds((n, rows, cols), BF), 1

    own_down = hidden_units // devices
    if can_split(own_down):
        down_spec = pl.BlockSpec((chunk // (2 * own_down), own_down, width), lambda j: (j, 0, 0))
        down_shapes = [sds((hidden_units // (2 * own_down), own_down, width), BF)] * 2
    else:
        down_spec = pl.BlockSpec((chunk, width), lambda j: (j, 0))
        down_shapes = [sds((hidden_units, width), BF)]
    grad_w_down = pl.pallas_call(
        functools.partial(down_kernel, own_down),
        grid=(chunks,),
        in_specs=[by_col, whole((count, width)), core_spec],
        out_specs=[down_spec] * len(down_shapes),
        out_shape=down_shapes,
        compiler_params=params(),
        cost_estimate=cost(count * 2 * width * hidden_units, 11e6),
        name="down_weight",
    )(active, grad_down, core)
    sum_down = Sum(grad_w_down, 1, 4, width)
    down_layout = ([(4, 1)], [(0, k, 0) for k in range(4)])

    own = width // devices
    up_spec, up_shape, up_outs = split_outs(2, width, width, own, width // 2, lambda j: (j, 0))

    def held_col(j):
        return jnp.minimum(j, chunks - 1)

    grad_b_up, grad_hidden1, grad_branch, sums_up, *grad_w_up = pl.pallas_call(
        functools.partial(up_kernel, own),
        grid=(chunks + 1,),
        in_specs=[
            pl.BlockSpec((count, chunk), lambda j: (0, held_col(j))),
            whole((count, width)),
            pl.BlockSpec((chunk, width), lambda j: (held_col(j), 0)),
            pl.BlockSpec((width, chunk), lambda j: (0, held_col(j))),
            whole((count, width)),
            whole((count, width)),
            whole(vectors.shape),
            whole((count, width)),
            whole((share, width, per_item)),
            core_spec,
            any_place,
        ],
        out_specs=[
            pl.BlockSpec((1, 8, chunk), lambda j: (held_col(j), 0, 0)),
            whole((count, width)),
            whole((count, width)),
            whole((8, width)),
        ]
        + [up_spec] * up_outs,
        out_shape=[
            sds((chunks, 8, chunk), F32),
            sds((count, width), F32),
            sds((count, width), BF),
            sds((8, width), F32),
        ]
        + [up_shape(2 * chunks + 2)] * up_outs,
        scratch_shapes=[pltpu.VMEM((count, width), F32)],
        compiler_params=params(),
        cost_estimate=cost(count * (6 * hidden_units + 2 * width) * width, 25e6),
        name="up_weight",
    )(
        slope,
        grad_down,
        w_down,
        w_up,
        normed2,
        hidden1,
        vectors,
        grad_hidden2,
        mixed,
        core,
        sum_down.sent[0],
    )
    sum_up = Sum(grad_w_up, 2 * chunks + 2, 1, width // 2)
    up_layout = (
        [(1, 2 * chunks), (1, 2)],
        [(0, 0, k) for k in range(2 * chunks)] + [(1, 0, 0), (1, 0, 1)],
    )
    late_layout = ([(1, 6)], [(0, 0, k) for k in range(6)])
    skip_layout = ([(2, 1)], [(0, k, 0) for k in range(2)])

    after, _ = run_tasks([(sum_down, None)], [sum_up.sent[0]], "serve_1")
    grad_qkv, grad_key_extra, grad_value_extra = [], [], []
    sums_attend = jnp.zeros((8, width), F32)
    grad_hidden0 = None
    for item in range(share):

        def one(*shape, item=item):
            return pl.BlockSpec(
                (1,) + shape, lambda *_: (item,) + (0,) * len(shape), pipeline_mode=pl.Buffered(1)
            )

        one_block = pl.BlockSpec(
            (groups, 1, local, width), lambda *_, item=item: (0, item, 0, 0)
        )
        held = [grad_hidden0] if item else []
        outs = pl.pallas_call(
            attend_back_kernel,
            grid=(1,),
            in_specs=[
                one_block,
                one(per_item, width),
                one(per_item, width),
                one(3 * width, per_item),
                one(HEADS, per_item, per_item),
                one(HEADS, EXTRA_PAD, per_item),
                one(HEADS, EXTRA_PAD, head_dim),
                one(HEADS, EXTRA_PAD, head_dim),
                whole(vectors.shape),
                whole((3 * width, width)),
                whole((width, width)),
                whole((8, width)),
            ]
            + [any_place] * (len(held) + len(after)),
            out_specs=[
                whole((3 * width, per_item)),
                whole((HEADS, EXTRA_PAD, head_dim)),
                whole((HEADS, EXTRA_PAD, head_dim)),
                one_block,
                whole((8, width)),
            ],
            out_shape=[
                sds((3 * width, per_item), BF),
                sds((HEADS, EXTRA_PAD, head_dim), F32),
                sds((HEADS, EXTRA_PAD, head_dim), F32),
                sds((groups, share, local, width), BF),
                sds((8, width), F32),
            ],
            input_output_aliases={12: 3} if item else {},
            scratch_shapes=[pltpu.VMEM((width, per_item), BF)],
            compiler_params=params(),
            cost_estimate=cost(
                per_item * (8 * width * width + 40 * per_item * width), 12e6
            ),
            name="attend_back",
        )(
            hidden0,
            grad_hidden1.reshape(share, per_item, width),
            grad_branch.reshape(share, per_item, width),
            qkv,
            probs,
            probs_extra,
            key_extra,
            value_extra,
            vectors,
            w_qkv_t,
            w_out,
            sums_attend,
            *held,
            *after,
        )
        grad_qkv.append(outs[0])
        grad_key_extra.append(outs[1])
        grad_value_extra.append(outs[2])
        grad_hidden0, sums_attend = outs[3], outs[4]
        after, _ = run_tasks(
            [(sum_down, None), (sum_up, None)], [sums_attend], "serve_" + str(item + 2)
        )
    grad_key_extra = jnp.stack(grad_key_extra)
    grad_value_extra = jnp.stack(grad_value_extra)
    grad_tile = to_items(grad_hidden0.reshape(items, local, width))

    def from_head(block):
        return block[:, :, :2].transpose(0, 2, 1, 3).reshape(share * 2, width)

    grad_pairs = jnp.concatenate(
        [from_head(grad_key_extra), from_head(grad_value_extra)], 1
    ).astype(BF)
    grad_qkv_extra = jnp.concatenate([jnp.zeros((share * 2, width), BF), grad_pairs], 1)
    pad_extra = (-2 * share) % 16
    normed_extra_pad = jnp.pad(normed_extra, ((0, pad_extra), (0, 0)))
    grad_qkv_extra_pad = jnp.pad(grad_qkv_extra, ((0, pad_extra), (0, 0)))

    half = width // 2
    late_spec, late_shape, late_outs = split_outs(1, width, width, own, half, lambda j: (j, 0))
    grad_late = pl.pallas_call(
        functools.partial(late_weight_kernel, own),
        grid=(6,),
        in_specs=[
            whole((share, per_item, width)),
            whole(normed_extra_pad.shape),
            pl.BlockSpec((normed_extra_pad.shape[0], half), lambda j: (0, j)),
        ]
        + [pl.BlockSpec((half, per_item), lambda j: (j, 0))] * share
        + [core_spec]
        + [any_place] * len(after),
        out_specs=[late_spec] * late_outs,
        out_shape=[late_shape(6)] * late_outs,
        compiler_params=params(),
        cost_estimate=cost(count * 6 * width * width, 12e6),
        name="late_weight",
    )(normed1, normed_extra_pad, grad_qkv_extra_pad, *grad_qkv, core, *after)
    sum_late = Sum(grad_late, 6, 1, half)

    def hold(values, *others):
        return lax.optimization_barrier((values, others))[0]

    grad_normed_extra = dot(hold(grad_pairs, sum_late.sent), w_qkv[:, width:], 1, 1)
    grad_extra = norm_back(grad_normed_extra * row(norm1_gain), unit_extra, scaled_extra)
    grad_extra = grad_extra.astype(BF)
    sums_extra = jnp.concatenate(
        [
            row_sum(grad_normed_extra * unit_extra),
            row_sum(grad_normed_extra),
            row_sum(grad_extra.astype(F32)),
        ],
        0,
    )
    grad_joined_extra = dot(grad_extra, w_skip, 1, 1).astype(BF)

    while sum_down.orders[0]:
        run_tasks([(sum_down, None), (sum_up, None)], [sum_late.sent[0]], "serve_more")
    after, results = run_tasks(
        [(sum_down, down_layout), (sum_up, None)], [sum_late.sent[0], grad_joined_extra], "serve_5"
    )
    out_down = results[0][0]
    while sum_up.orders[0]:
        after, _ = run_tasks([(sum_up, None)], after, "serve_more")
    after, results = run_tasks([(sum_late, None), (sum_up, up_layout)], after, "serve_6")
    out_up, out_out = results[0]

    joined_extra_pad = jnp.pad(joined_extra, ((0, pad_extra), (0, 0)))
    grad_extra_pad = jnp.pad(grad_extra, ((0, pad_extra), (0, 0)))
    own_skip_rows = 2 * own
    skip_block = width // 2
    if can_split(own_skip_rows):
        skip_spec = pl.BlockSpec(
            (skip_block // (2 * own_skip_rows), own_skip_rows, width), lambda j: (j, 0, 0)
        )
        skip_shapes = [sds((2 * width // (2 * own_skip_rows), own_skip_rows, width), BF)] * 2
    else:
        skip_spec = pl.BlockSpec((skip_block, width), lambda j: (j, 0))
        skip_shapes = [sds((2 * width, width), BF)]
    grad_w_skip = pl.pallas_call(
        functools.partial(skip_weight_kernel, own_skip_rows),
        grid=(4,),
        in_specs=[
            pl.BlockSpec((items * local, skip_block), lambda j: (0, jnp.minimum(j, 1))),
            pl.BlockSpec((items * local, skip_block), lambda j: (0, jnp.maximum(j - 2, 0))),
            whole((items * local, width)),
            pl.BlockSpec((joined_extra_pad.shape[0], skip_block), lambda j: (0, j)),
            whole(grad_extra_pad.shape),
            core_spec,
        ]
        + [any_place] * len(after),
        out_specs=[skip_spec] * len(skip_shapes),
        out_shape=skip_shapes,
        compiler_params=params(),
        cost_estimate=cost(count * 4 * width * width, 8e6),
        name="skip_weight",
    )(
        body,
        body_skip,
        grad_tile.reshape(items * local, width),
        joined_extra_pad,
        grad_extra_pad,
        core,
        *after,
    )
    sum_skip = Sum(grad_w_skip, 1, 2, width)
    grad_tokens, grad_skip_tokens = pl.pallas_call(
        token_kernel,
        grid=(items // some,),
        in_specs=[flat_block, whole((2 * width, width)), any_place],
        out_specs=[tile_block] * 2,
        out_shape=[sds(tokens.shape, BF)] * 2,
        compiler_params=params(),
        cost_estimate=cost(items * local * 4 * width * width, 8e6),
        name="tokens",
    )(grad_tile, w_skip, sum_skip.sent[0])
    after, _ = run_tasks(
        [(sum_late, None)], [sum_skip.sent[0], grad_tokens], "serve_7"
    )

    stacked_count = 9 + patch_values
    stacked, shared = pl.pallas_call(
        pack_kernel,
        in_specs=[pl.BlockSpec(memory_space=pltpu.VMEM)] * 9 + [any_place] * len(after),
        out_specs=[pl.BlockSpec(memory_space=pltpu.VMEM)] * 2,
        out_shape=[sds((stacked_count, width), F32), sds((8, 128), F32)],
        compiler_params=params(),
        cost_estimate=cost(1e6, 1e6),
        name="pack",
    )(
        sums_attend,
        sums_extra,
        sums_up,
        sums_final,
        head_sum,
        grad_head,
        conv_sum,
        conv_bias,
        jnp.asarray(conv_lanes(share), BF),
        *after,
    )
    packed = jnp.concatenate(
        [
            stacked.reshape(stacked_count, devices, own).transpose(1, 0, 2).reshape(devices, -1),
            grad_b_up[:, 0].reshape(devices, -1),
            jnp.broadcast_to(shared[:4].reshape(1, -1), (devices, 512)),
        ],
        1,
    )
    packed_size = packed.shape[1]
    packed = jnp.pad(packed, ((0, 0), (0, (-packed.shape[1]) % 128)))
    after, _ = run_tasks([(sum_skip, None), (sum_late, None)], [packed], "serve_8")
    packed = lax.all_to_all(packed, ALL, split_axis=0, concat_axis=0, tiled=True)
    summed = jnp.sum(packed, 0)
    small = [summed[k * own : (k + 1) * own] for k in range(9)]
    own_head = summed[9 * own : stacked_count * own].reshape(patch_values, own).T
    up_low = stacked_count * own
    own_b_up = summed[up_low : up_low + hidden_units // devices]
    shared = summed[up_low + hidden_units // devices : packed_size].reshape(4, 128)

    latent = (
        hold(result, after)
        .reshape(groups, local, share, patch_values)
        .transpose(0, 2, 1, 3)
        .reshape(items, local, patch_values)
    )
    after, _ = run_tasks([(sum_skip, None), (sum_late, None)], [latent], "serve_9")
    latent = to_items(latent)
    latent_out = (
        latent.reshape(items, rows, cols, PATCH, PATCH, chans)
        .transpose(0, 1, 3, 2, 4, 5)
        .reshape(items, height, breadth, chans)
    )
    grad_joined_extra = to_items(
        jnp.tile(grad_joined_extra.reshape(1, share * 2, 2 * width), (groups, 1, 1))
    ).reshape(items, 2, 2 * width)
    while sum_late.orders[0]:
        after, _ = run_tasks([(sum_skip, None), (sum_late, None)], after, "serve_more")
    after, results = run_tasks([(sum_skip, None), (sum_late, late_layout)], after, "serve_10")
    out_qkv = results[0][0]
    while sum_skip.orders[0]:
        after, _ = run_tasks([(sum_skip, None)], after, "serve_last")
    _, results = run_tasks([(sum_skip, skip_layout)], after, "serve_end")
    out_skip = results[0][0]
    return (
        latent_out,
        grad_tokens,
        grad_skip_tokens,
        grad_joined_extra[..., :width],
        grad_joined_extra[..., width:],
        out_skip,
        small[0],
        small[1],
        small[2],
        out_qkv,
        out_out,
        small[3],
        small[4],
        small[5],
        out_up,
        own_b_up,
        out_down,
        small[6],
        small[7],
        small[8],
        own_head,
        shared[0, 64 : 64 + patch_values],
        shared[:, : 9 * chans].reshape(chans, 3, 3, chans).transpose(1, 2, 0, 3),
        shared[0, 96 : 96 + chans],
    )


def solution(mesh):
    tiles = P("batch", "ty", "tx", None)
    pairs = P("batch", None, None)
    matrix = P(ALL, None)
    vector = P(ALL)
    return jax.shard_map(
        per_device,
        mesh=mesh,
        in_specs=(tiles, tiles, pairs, pairs, P("batch"), tiles) + (P(),) * 19,
        out_specs=(
            tiles,
            tiles,
            tiles,
            pairs,
            pairs,
            matrix,
            vector,
            vector,
            vector,
            matrix,
            matrix,
            vector,
            vector,
            vector,
            matrix,
            vector,
            matrix,
            vector,
            vector,
            vector,
            matrix,
            P(),
            P(),
            P(),
        ),
        check_vma=False,
    )
```

```python
import functools

import jax
import jax.numpy as jnp
import numpy as np
from jax import lax
from jax.experimental import pallas as pl
from jax.experimental.pallas import tpu as pltpu
from jax.sharding import PartitionSpec as P

HEADS = 12
PATCH = 2
EXTRA_PAD = 8
EPS = 1e-05
BF = jnp.bfloat16
F32 = jnp.float32
PLANE = ("ty", "tx")
ALL = ("batch", "ty", "tx")
MIB = 1024 * 1024


def dot(left, right, left_dim, right_dim):
    return lax.dot_general(
        left, right, (((left_dim,), (right_dim,)), ((), ())), preferred_element_type=F32
    )


def norm_parts(values):
    center = values - jnp.mean(values, -1, keepdims=True)
    scaled = lax.rsqrt(jnp.mean(center * center, -1, keepdims=True) + EPS)
    return center * scaled, scaled


def norm_back(inner, normed, scaled):
    return scaled * (
        inner
        - jnp.mean(inner, -1, keepdims=True)
        - normed * jnp.mean(inner * normed, -1, keepdims=True)
    )


def flat(ref):
    return ref[...].astype(F32).reshape(1, -1)


def row_sum(values):
    return jnp.sum(values, 0, keepdims=True)


def gelu_parts(upper):
    spread = 0.5 + 0.5 * lax.erf(upper * np.float32(0.5**0.5))
    bell = jnp.exp(upper * upper * -0.5) * np.float32((2 * np.pi) ** -0.5)
    return upper * spread, spread + upper * bell


def noise_weight(timesteps):
    frac = (timesteps.astype(F32) / 1000.0 + 0.008) / 1.008
    kept = jnp.cos(frac * (0.5 * jnp.pi)) ** 2
    return jnp.minimum(1.0, 5.0 * (1.0 - kept) / kept)


def can_split(own):
    return own % 8 == 0


def store_split(value, own, lane_refs):
    if len(lane_refs) == 1:
        lane_refs[0][...] = value.astype(BF)
        return
    keep_ref, send_ref, core_ref = lane_refs
    pairs = value.reshape(value.shape[0] // (2 * own), 2, own, value.shape[1])
    first = core_ref[0] == 0
    keep = jnp.where(first, pairs[:, 0], pairs[:, 1])
    send = jnp.where(first, pairs[:, 1], pairs[:, 0])
    keep_ref[...] = keep.astype(BF)
    send_ref[...] = send.astype(BF)


def merge_kernel(tokens_ref, skip_ref, w_skip_ref, b_skip_ref, hidden_ref, joined_ref):
    width = w_skip_ref.shape[1]
    local = tokens_ref.shape[1] * tokens_ref.shape[2]
    body = tokens_ref[...].reshape(-1, width)
    body_skip = skip_ref[...].reshape(-1, width)
    hidden = (
        dot(body, w_skip_ref[:width], 1, 0)
        + dot(body_skip, w_skip_ref[width:], 1, 0)
        + b_skip_ref[...].astype(F32).reshape(1, width)
    )
    hidden_ref[...] = hidden.astype(BF).reshape(-1, local, width)
    joined_ref[:, :local] = body.reshape(-1, local, width)
    joined_ref[:, local : 2 * local] = body_skip.reshape(-1, local, width)


def attend_kernel(
    hidden_ref,
    key_extra_ref,
    value_extra_ref,
    gain_ref,
    shift_ref,
    b_out_ref,
    w_qkv_ref,
    w_out_ref,
    normed_ref,
    qkv_ref,
    probs_ref,
    probs_extra_ref,
    mixed_ref,
    hidden1_ref,
):
    width = w_out_ref.shape[0]
    head_dim = width // HEADS
    scale = head_dim ** (-0.5)
    rows = hidden_ref.shape[0] * hidden_ref.shape[2]
    hidden = hidden_ref[...].reshape(rows, width).astype(F32)
    unit, _ = norm_parts(hidden)
    normed = (unit * flat(gain_ref) + flat(shift_ref)).astype(BF)
    normed_ref[0] = normed
    qkv_ref[0] = dot(w_qkv_ref[...], normed, 0, 1).astype(BF)
    live = lax.broadcasted_iota(jnp.int32, (EXTRA_PAD, rows), 0) < 2
    for head in range(HEADS):
        low = head * head_dim
        query = qkv_ref[0, low : low + head_dim, :]
        key = qkv_ref[0, width + low : width + low + head_dim, :]
        value = qkv_ref[0, 2 * width + low : 2 * width + low + head_dim, :]
        scores = dot(key, query, 0, 0) * scale
        scores_extra = jnp.where(live, dot(key_extra_ref[0, head], query, 1, 0) * scale, -1e30)
        top = jnp.maximum(
            jnp.max(scores, 0, keepdims=True), jnp.max(scores_extra, 0, keepdims=True)
        )
        raised = jnp.exp(scores - top)
        raised_extra = jnp.exp(scores_extra - top)
        share = 1.0 / (row_sum(raised) + row_sum(raised_extra))
        probs = (raised * share).astype(BF)
        probs_extra = (raised_extra * share).astype(BF)
        probs_ref[0, head] = probs
        probs_extra_ref[0, head] = probs_extra
        mixed = dot(value, probs, 1, 0) + dot(value_extra_ref[0, head], probs_extra, 0, 0)
        mixed_ref[0, low : low + head_dim, :] = mixed.astype(BF)
    hidden1_ref[0] = hidden + (dot(mixed_ref[0], w_out_ref[...], 0, 0) + flat(b_out_ref))


def forward_kernel(
    hidden1_ref,
    gain2_ref,
    shift2_ref,
    b_up_ref,
    w_up_ref,
    w_down_ref,
    active_ref,
    slope_ref,
    normed2_ref,
    total,
    up_rows,
):
    step = pl.program_id(0)

    @pl.when(step == 0)
    def _():
        unit, _ = norm_parts(hidden1_ref[...])
        b_up = flat(b_up_ref)
        width = up_rows.shape[1]
        for j in range(up_rows.shape[0]):
            up_rows[j : j + 1] = b_up[:, j * width : (j + 1) * width]
        normed2_ref[...] = (unit * flat(gain2_ref) + flat(shift2_ref)).astype(BF)

    upper = dot(normed2_ref[...], w_up_ref[...], 1, 0) + up_rows[pl.ds(step, 1)]
    active, slope = gelu_parts(upper)
    active = active.astype(BF)
    active_ref[0] = active
    slope_ref[0] = slope.astype(BF)
    part = dot(active, w_down_ref[...], 1, 0)

    @pl.when(step == 0)
    def _():
        total[...] = part

    @pl.when(step > 0)
    def _():
        total[...] += part


def turn_kernel(
    tile_rows,
    tile_cols,
    tiles_x,
    hidden1_ref,
    change_ref,
    b_down_ref,
    gainf_ref,
    shiftf_ref,
    w_head_ref,
    w_conv_ref,
    lanes_ref,
    target_ref,
    after_ref,
    result_ref,
    grad_hidden2_ref,
    grad_down_ref,
    grad_head_ref,
    sums_ref,
    head_sum_ref,
    conv_sum_ref,
    conv_bias_ref,
    total,
):
    per_item, lanes = target_ref.shape
    patch_values, width = w_head_ref.shape
    items = lanes // patch_values

    def head_of(i):
        parts = [w_head_ref[...]]
        if i > 0:
            parts = [jnp.zeros((i * patch_values, width), BF)] + parts
        if i < items - 1:
            parts = parts + [jnp.zeros((lanes - (i + 1) * patch_values, width), BF)]
        return jnp.concatenate(parts, 0)

    heads = [head_of(i) for i in range(items)]
    hidden2 = hidden1_ref[...] + (change_ref[...] + flat(b_down_ref))
    unit, scaled = norm_parts(hidden2)
    total[...] = unit
    normedf = (unit * flat(gainf_ref) + flat(shiftf_ref)).astype(BF)
    normed2_final = [normedf[i * per_item : (i + 1) * per_item] for i in range(items)]
    patches = lanes_ref[0:1]
    for i in range(items):
        patches = patches + dot(normed2_final[i], heads[i], 1, 1)
    patches = patches.astype(BF)

    def place(position):
        tile = position // (tile_rows * tile_cols)
        row = (tile // tiles_x) * tile_rows + (position // tile_cols) % tile_rows
        col = (tile % tiles_x) * tile_cols + position % tile_cols
        return row * 1024 + col

    own = place(lax.broadcasted_iota(jnp.int32, (per_item, 1), 0))
    other = place(lax.broadcasted_iota(jnp.int32, (1, per_item), 1))
    shifts = []
    for row_off in range(3):
        for col_off in range(3):
            wanted = own + ((row_off - 1) * 1024 + (col_off - 1))
            shifts.append(jnp.where(wanted == other, 1.0, 0.0).astype(BF))
    windows = [dot(shift, patches, 1, 0).astype(BF) for shift in shifts]
    result = lanes_ref[1:2]
    for k in range(9):
        result = result + dot(windows[k], w_conv_ref[k], 1, 0)
    result_ref[...] = result.astype(BF)
    grad_result = (lanes_ref[2:3] * (result - target_ref[...])).astype(BF)
    conv_bias_ref[...] = row_sum(grad_result.astype(F32))
    grad_patches = jnp.zeros(target_ref.shape, F32)
    for k in range(9):
        conv_sum_ref[k] = dot(windows[k], grad_result, 0, 0)
        moved = dot(shifts[8 - k], grad_result, 1, 0).astype(BF)
        grad_patches = grad_patches + dot(moved, w_conv_ref[k], 1, 1)
    grad_patches = grad_patches.astype(BF)
    grad_head_ref[...] = row_sum(grad_patches.astype(F32))
    sum_gain = jnp.zeros((1, unit.shape[1]), F32)
    sum_shift = sum_gain
    sum_down = sum_gain
    for i in range(items):
        rows = slice(i * per_item, (i + 1) * per_item)
        head_sum_ref[i] = dot(grad_patches, normed2_final[i], 0, 0)
        grad_normedf = dot(grad_patches, heads[i], 1, 0)
        unit_part = total[rows]
        sum_gain = sum_gain + row_sum(grad_normedf * unit_part)
        sum_shift = sum_shift + row_sum(grad_normedf)
        grad_hidden2 = norm_back(grad_normedf * flat(gainf_ref), unit_part, scaled[rows])
        grad_hidden2_ref[rows] = grad_hidden2
        grad_down = grad_hidden2.astype(BF)
        grad_down_ref[rows] = grad_down
        sum_down = sum_down + row_sum(grad_down.astype(F32))
    sums_ref[0:1] = sum_gain
    sums_ref[1:2] = sum_shift
    sums_ref[2:3] = sum_down


def down_kernel(active_ref, grad_down_ref, grad_w_ref):
    grad_w_ref[...] = dot(active_ref[0], grad_down_ref[...], 0, 0).astype(BF)


def up_kernel(
    own,
    slope_ref,
    grad_down_ref,
    w_down_ref,
    w_up_ref,
    normed2_ref,
    hidden1_ref,
    gain2_ref,
    grad_hidden2_ref,
    mixed_ref,
    core_ref,
    after_ref,
    grad_b_up_ref,
    grad_hidden1_ref,
    grad_branch_ref,
    sums_ref,
    *rest,
):
    total = rest[-1]
    rest = rest[:-1]
    step = pl.program_id(0)
    steps = pl.num_programs(0)

    def store(value):
        half = value.shape[1] // 2
        for side in range(2):
            piece = value[:, side * half : (side + 1) * half]
            if can_split(own):
                store_split(piece, own, (rest[0].at[side], rest[1].at[side], core_ref))
            else:
                store_split(piece, own, (rest[0].at[side],))

    @pl.when(step < steps - 1)
    def _():
        grad_active = dot(grad_down_ref[...], w_down_ref[...], 1, 1)
        grad_upper = (grad_active * slope_ref[0].astype(F32)).astype(BF)
        grad_b_up_ref[0, 0:1] = row_sum(grad_upper.astype(F32))
        store(dot(normed2_ref[...], grad_upper, 0, 0))
        part = dot(grad_upper, w_up_ref[...], 1, 1)

        @pl.when(step == 0)
        def _():
            total[...] = part

        @pl.when(step > 0)
        def _():
            total[...] += part

    @pl.when(step == steps - 1)
    def _():
        unit, scaled = norm_parts(hidden1_ref[...])
        grad_normed2 = total[...]
        sums_ref[0:1] = row_sum(grad_normed2 * unit)
        sums_ref[1:2] = row_sum(grad_normed2)
        grad_hidden1 = grad_hidden2_ref[...] + norm_back(
            grad_normed2 * flat(gain2_ref), unit, scaled
        )
        grad_hidden1_ref[...] = grad_hidden1
        grad_branch = grad_hidden1.astype(BF)
        grad_branch_ref[...] = grad_branch
        sums_ref[2:3] = row_sum(grad_branch.astype(F32))
        items, _, per_item = mixed_ref.shape
        value = dot(mixed_ref[0], grad_branch[:per_item], 1, 0)
        for item in range(1, items):
            rows = slice(item * per_item, (item + 1) * per_item)
            value = value + dot(mixed_ref[item], grad_branch[rows], 1, 0)
        store(value)


def attend_back_kernel(
    hidden_ref,
    grad_hidden1_ref,
    grad_branch_ref,
    qkv_ref,
    probs_ref,
    probs_extra_ref,
    key_extra_ref,
    value_extra_ref,
    gain_ref,
    w_qkv_ref,
    w_out_ref,
    sums_in_ref,
    *rest,
):
    (
        grad_qkv_ref,
        grad_key_extra_ref,
        grad_value_extra_ref,
        grad_hidden0_ref,
        sums_ref,
        grad_mixed_ref,
    ) = rest[-6:]
    width = w_out_ref.shape[0]
    head_dim = width // HEADS
    scale = head_dim ** (-0.5)
    rows = hidden_ref.shape[0] * hidden_ref.shape[2]
    grad_mixed_ref[...] = dot(w_out_ref[...], grad_branch_ref[0], 1, 1).astype(BF)
    for head in range(HEADS):
        low = head * head_dim
        query = qkv_ref[0, low : low + head_dim, :]
        key = qkv_ref[0, width + low : width + low + head_dim, :]
        value = qkv_ref[0, 2 * width + low : 2 * width + low + head_dim, :]
        grad_mixed = grad_mixed_ref[low : low + head_dim, :]
        probs_low = probs_ref[0, head]
        probs_extra_low = probs_extra_ref[0, head]
        probs = probs_low.astype(F32)
        probs_extra = probs_extra_low.astype(F32)
        grad_probs = dot(value, grad_mixed, 0, 0)
        grad_probs_extra = dot(value_extra_ref[0, head], grad_mixed, 1, 0)
        common = row_sum(grad_probs * probs) + row_sum(grad_probs_extra * probs_extra)
        grad_scores = (probs * (grad_probs - common)).astype(BF)
        grad_scores_extra = (probs_extra * (grad_probs_extra - common)).astype(BF)
        grad_query = dot(key, grad_scores, 1, 0) + dot(
            key_extra_ref[0, head], grad_scores_extra, 0, 0
        )
        grad_key = dot(query, grad_scores, 1, 1)
        grad_value = dot(grad_mixed, probs_low, 1, 1)
        grad_key_extra_ref[head] = dot(grad_scores_extra, query, 1, 1) * scale
        grad_value_extra_ref[head] = dot(probs_extra_low, grad_mixed, 1, 1)
        grad_qkv_ref[low : low + head_dim, :] = (grad_query * scale).astype(BF)
        grad_qkv_ref[width + low : width + low + head_dim, :] = (grad_key * scale).astype(BF)
        grad_qkv_ref[2 * width + low : 2 * width + low + head_dim, :] = grad_value.astype(BF)
    grad_normed = dot(grad_qkv_ref[...], w_qkv_ref[...], 0, 1)
    unit, scaled = norm_parts(hidden_ref[...].reshape(rows, width).astype(F32))
    sums_ref[0:1] = sums_in_ref[0:1] + row_sum(grad_normed * unit)
    sums_ref[1:2] = sums_in_ref[1:2] + row_sum(grad_normed)
    grad_hidden0 = grad_hidden1_ref[0] + norm_back(grad_normed * flat(gain_ref), unit, scaled)
    grad_low = grad_hidden0.astype(BF)
    sums_ref[2:3] = sums_in_ref[2:3] + row_sum(grad_low.astype(F32))
    grad_hidden0_ref[...] = grad_low.reshape(grad_hidden0_ref.shape)


def extra_back_kernel(
    share,
    hidden_ref,
    gain_ref,
    w_key_ref,
    w_value_ref,
    latent_ref,
    sums_in_ref,
    *rest,
):
    keys, values = rest[:share], rest[share : 2 * share]
    pairs_ref, grad_ref, sums_ref, back_ref = rest[-4:]
    width = hidden_ref.shape[1]

    def rows_of(refs):
        return jnp.concatenate(
            [jnp.concatenate([ref[head] for ref in refs], 0) for head in range(HEADS)], 1
        ).astype(BF)

    grad_key, grad_value = rows_of(keys), rows_of(values)
    pairs_ref[0] = grad_key
    pairs_ref[1] = grad_value
    grad_normed = dot(grad_key, w_key_ref[...], 1, 1) + dot(grad_value, w_value_ref[...], 1, 1)
    unit, scaled = norm_parts(hidden_ref[...])
    grad = norm_back(grad_normed * flat(gain_ref), unit, scaled).astype(BF)
    grad_ref[...] = grad
    wide = grad.astype(F32)
    sums_ref[0:1] = sums_in_ref[0:1] + row_sum(grad_normed * unit)
    sums_ref[1:2] = sums_in_ref[1:2] + row_sum(grad_normed)
    sums_ref[2:3] = sums_in_ref[2:3] + row_sum(wide)
    real = [wide[i * EXTRA_PAD : i * EXTRA_PAD + 2] for i in range(share)]
    fill = back_ref.shape[1] - 2 * share - latent_ref.shape[1]
    for group in range(back_ref.shape[0]):
        block = real + [latent_ref[group].astype(F32), jnp.zeros((fill, width), F32)]
        back_ref[group] = jnp.concatenate(block, 0).astype(BF)


def late_weight_kernel(
    own,
    normed_ref,
    normed_extra_ref,
    pairs_ref,
    joined_ref,
    grad_ref,
    joined_extra_ref,
    grad_extra_ref,
    grad_qkv_0_ref,
    grad_qkv_1_ref,
    grad_qkv_2_ref,
    core_ref,
    *rest,
):
    step = pl.program_id(0)
    split = can_split(own)
    groups, items, _, width = joined_ref.shape
    local = (grad_ref.shape[1] - 16) // items

    @pl.when(step < 3)
    def _():
        total = dot(normed_extra_ref[...], pairs_ref[0], 0, 0)
        total = total * jnp.where(step == 0, 0.0, 1.0)
        for item, ref in enumerate((grad_qkv_0_ref, grad_qkv_1_ref, grad_qkv_2_ref)):
            total = total + dot(normed_ref[item], ref[...], 0, 1)
        half = width // 2
        for side in range(2):
            piece = total[:, side * half : (side + 1) * half]
            if split:
                store_split(piece, own, (rest[-2].at[side], rest[-1].at[side], core_ref))
            else:
                store_split(piece, own, (rest[-1].at[side],))

    @pl.when(step >= 3)
    def _():
        grad = grad_ref[:, : items * local].reshape(groups * items * local, -1)
        for side in range(2):
            joined = joined_ref[:, :, side * local : (side + 1) * local]
            joined = joined.reshape(groups * items * local, width)
            extra = joined_extra_ref[:, side * width : (side + 1) * width]
            total = dot(joined, grad, 0, 0) + dot(extra, grad_extra_ref[...], 0, 0)
            if not split:
                rest[-1][side] = total.astype(BF)
                continue
            pairs = total.reshape(width // (4 * own), 2, 2, own, total.shape[1])
            first = core_ref[0] == 0
            count = pairs.shape[0]
            for part in range(2):
                low, high = pairs[:, 0, part], pairs[:, 1, part]
                where = pl.ds(side * count, count)
                rest[-2][part, where] = jnp.where(first, low, high).astype(BF)
                rest[-1][part, where] = jnp.where(first, high, low).astype(BF)


def token_kernel(back_ref, w_skip_ref, tokens_ref, skip_ref, extra_ref):
    width = w_skip_ref.shape[1]
    items = tokens_ref.shape[0]
    local = tokens_ref.shape[1] * tokens_ref.shape[2]
    body = items // back_ref.shape[0] * local
    grad = back_ref[:, :body].reshape(items * local, width)
    tokens_ref[...] = dot(grad, w_skip_ref[:width], 1, 1).astype(BF).reshape(tokens_ref.shape)
    skip_ref[...] = dot(grad, w_skip_ref[width:], 1, 1).astype(BF).reshape(skip_ref.shape)
    extra = back_ref[:, body:].reshape(-1, width)
    extra_ref[...] = dot(extra, w_skip_ref[...], 1, 1).astype(BF).reshape(extra_ref.shape)


def fold_matrix(shape, low, wide, period):
    row = lax.broadcasted_iota(jnp.int32, shape, 0)
    col = lax.broadcasted_iota(jnp.int32, shape, 1)
    return jnp.where((col >= low) & (col < low + wide) & (row % period == col - low), 1.0, 0.0)


def pack_kernel(
    sums_attend_ref,
    sums_up_ref,
    sums_final_ref,
    head_sum_ref,
    grad_head_ref,
    conv_sum_ref,
    conv_bias_ref,
    table_ref,
    *rest,
):
    stacked_ref, shared_ref = rest[-2:]
    items, lanes, _ = head_sum_ref.shape
    values = lanes // items
    exact = functools.partial(
        jnp.dot, precision=lax.Precision.HIGHEST, preferred_element_type=F32
    )
    stacked_ref[0:1] = sums_attend_ref[2:3]
    stacked_ref[1:2] = sums_attend_ref[0:1]
    stacked_ref[2:3] = sums_attend_ref[1:2]
    stacked_ref[3:4] = sums_up_ref[2:3]
    stacked_ref[4:6] = sums_up_ref[0:2]
    stacked_ref[6:7] = sums_final_ref[2:3]
    stacked_ref[7:9] = sums_final_ref[0:2]
    head = head_sum_ref[0, 0:values]
    for item in range(1, items):
        head = head + head_sum_ref[item, item * values : (item + 1) * values]
    stacked_ref[9 : 9 + values] = head
    row = lax.broadcasted_iota(jnp.int32, (8, lanes), 0)
    col = lax.broadcasted_iota(jnp.int32, (8, lanes), 1)
    left = jnp.where(col % 4 == row, 1.0, 0.0)
    shared = jnp.zeros((8, 128), F32)
    for tap in range(9):
        picked = conv_sum_ref[0] * table_ref[0, tap].astype(F32)
        for k in range(1, 9):
            picked = picked + conv_sum_ref[k] * table_ref[k, tap].astype(F32)
        shared = shared + exact(exact(left, picked), fold_matrix((lanes, 128), 4 * tap, 4, 4))
    bias = exact(grad_head_ref[...], fold_matrix((lanes, 128), 64, values, values))
    bias = bias + exact(conv_bias_ref[...], fold_matrix((lanes, 128), 96, 4, 4))
    first = lax.broadcasted_iota(jnp.int32, (8, 128), 0) == 0
    shared_ref[...] = shared + jnp.where(first, bias, 0.0)


def whole(shape):
    return pl.BlockSpec(shape, lambda *_: (0,) * len(shape), pipeline_mode=pl.Buffered(1))


def params():
    return pltpu.CompilerParams(vmem_limit_bytes=60 * MIB)


def cost(flops, moved, transcendentals=0):
    del flops, moved, transcendentals
    return pl.CostEstimate(flops=1024, bytes_accessed=1024, transcendentals=0)


def sds(shape, dtype):
    return jax.ShapeDtypeStruct(shape, dtype)


def swap(block, axis, gap):
    count = lax.axis_size(axis)
    return lax.ppermute(block, axis, [(i, i ^ gap) for i in range(count)])


def serve_kernel(tasks, places_ref, *refs):
    del places_ref
    inputs = sum(len(parts) for task in tasks for parts in task["sides"])
    outs = refs[len(refs) - sum(len(task["outs"]) for task in tasks) :]
    at, out_at = 0, 0
    del inputs
    for task in tasks:
        values = []
        for parts in task["sides"]:
            total = refs[at][...].astype(F32)
            for k in range(1, len(parts)):
                total = total + refs[at + k][...].astype(F32)
            at += len(parts)
            values.append(total)
        task["emit"](values, outs[out_at : out_at + len(task["outs"])])
        out_at += len(task["outs"])


def serve(tasks, after, name, places):
    arrays, specs = [], []
    for task in tasks:
        for parts in task["sides"]:
            for array, starts, sizes in parts:
                index = tuple(
                    start // size if isinstance(start, int) else start
                    for start, size in zip(starts, sizes, strict=True)
                )

                def where(_, ref, index=index):
                    return tuple(i if isinstance(i, int) else ref[i[0]] for i in index)

                arrays.append(array)
                specs.append(pl.BlockSpec(tuple(sizes), where))
    outs = [out for task in tasks for out in task["outs"]]
    moved = sum(2 * int(np.prod(spec.block_shape)) for spec in specs)
    return pl.pallas_call(
        functools.partial(serve_kernel, tasks),
        grid_spec=pltpu.PrefetchScalarGridSpec(
            num_scalar_prefetch=1,
            grid=(1,),
            in_specs=specs + [pl.BlockSpec(memory_space=pl.ANY)] * len(after),
            out_specs=[
                pl.BlockSpec(out.shape, lambda _, ref, n=len(out.shape): (0,) * n) for out in outs
            ],
        ),
        out_shape=outs,
        compiler_params=params(),
        cost_estimate=cost(moved, 2 * moved),
        name=name,
    )(places, *arrays, *after)


def emit_low(values, outs):
    for value, out in zip(values, outs, strict=True):
        out[...] = value.astype(BF)


def place_table():
    own = [lax.axis_index("ty"), lax.axis_index("tx") // 2]
    batch = lax.axis_size("batch")
    own += [(lax.axis_index("batch") >> bit) % 2 for bit in range(batch.bit_length() - 1)]
    return jnp.stack([v for place in own for v in (place, 1 - place)]).astype(jnp.int32)


class Sum:
    def __init__(self, grads, units, inner, columns, table):
        batch = lax.axis_size("batch")
        bits = batch.bit_length() - 1
        rows = sum(grad.size for grad in grads) // (units * columns)
        self.own = rows // lax.axis_size(ALL) // inner
        self.columns = columns
        self.table = table
        self.dims = [units] + [2] * bits + [2, 2, 2, inner, self.own, columns]
        self.moves = {"y": bits + 1, "x": bits + 2, "c": bits + 3}
        self.places = {"y": (0, 1), "x": (2, 3)}
        self.links = {"y": ("ty", 1), "x": ("tx", 2), "c": ("tx", 1)}
        for bit in range(bits):
            self.moves[bit] = bits - bit
            self.places[bit] = (4 + 2 * bit, 5 + 2 * bit)
            self.links[bit] = ("batch", 1 << bit)
        self.cut = 0 if units > 1 else len(self.dims) - 3
        self.half = self.dims[self.cut] // 2
        tail = list(range(bits))
        self.orders = [["x", "y"] + tail, ["y", "x"] + tail]
        at = self.moves["c"]
        if len(grads) == 1:
            grad = grads[0].reshape(self.dims)
            core = lax.axis_index("tx") % 2
            keep = lax.dynamic_slice_in_dim(grad, core, 1, at)
            send = lax.dynamic_slice_in_dim(grad, 1 - core, 1, at)
        else:
            halved = list(self.dims)
            halved[at] = 1
            keep, send = grads[0].reshape(halved), grads[1].reshape(halved)
        self.sent = [send]
        received = swap(send, *self.links["c"])
        self.parts = [[(keep, ("c",)), (received, ("c",))] for _ in range(2)]
        self.done = [["c"], ["c"]]

    def pick(self, part, chosen, side):
        array, fixed = part
        starts, sizes = [0] * array.ndim, list(array.shape)
        for move, where in chosen.items():
            if move not in fixed:
                starts[self.moves[move]] = where
                sizes[self.moves[move]] = 1
        if "side" not in fixed:
            starts[self.cut], sizes[self.cut] = side * self.half, self.half
        return array, starts, sizes

    def task(self):
        if self.orders[0][0] == self.orders[1][0]:
            return self.joint_task()
        sides, outs = [], []
        for side in range(2):
            move = self.orders[side][0]
            chosen = {m: self.places[m][:1] for m in self.done[side] if m != "c"}
            chosen[move] = self.places[move][1:]
            parts = [self.pick(part, chosen, side) for part in self.parts[side]]
            sides.append(parts)
            outs.append(sds(tuple(parts[0][2]), BF))
        return {"sides": sides, "outs": outs, "emit": emit_low}

    def joint_task(self):
        move = self.orders[0][0]
        sides = []
        for side in range(2):
            chosen = {m: self.places[m][:1] for m in self.done[side] if m != "c"}
            chosen[move] = self.places[move][1:]
            sides.append([self.pick(part, chosen, side) for part in self.parts[side]])
        shape = list(sides[0][0][2])
        shape[self.cut] = 2 * self.half
        cut, half = self.cut, self.half

        def emit(values, outs):
            for side in range(2):
                index = [slice(None)] * len(shape)
                index[cut] = slice(side * half, (side + 1) * half)
                outs[0][tuple(index)] = values[side].astype(BF)

        return {"sides": sides, "outs": [sds(tuple(shape), BF)], "emit": emit}

    def accept(self, sent):
        if len(sent) == 1:
            move = self.orders[0][0]
            received = swap(sent[0], *self.links[move])
            for side in range(2):
                self.orders[side].pop(0)
                self.done[side].append(move)
                self.parts[side].append((received, tuple(self.done[side])))
            return
        for side in range(2):
            move = self.orders[side].pop(0)
            self.done[side].append(move)
            received = swap(sent[side], *self.links[move])
            self.parts[side].append((received, ("side",) + tuple(self.done[side])))

    def last_task(self, layout):
        sides = []
        for side in range(2):
            chosen = {m: self.places[m][:1] for m in self.done[side] if m != "c"}
            sides.append([self.pick(part, chosen, side) for part in self.parts[side]])
        shapes, units = layout
        own, columns, half = self.own, self.columns, self.half

        def emit(values, outs):
            for side in range(2):
                value = values[side].reshape(half, own, columns)
                for k in range(half):
                    out, row, col = units[side * half + k]
                    outs[out][
                        row * own : (row + 1) * own, col * columns : (col + 1) * columns
                    ] = value[k]

        outs = [sds((r * own, c * columns), F32) for r, c in shapes]
        return {"sides": sides, "outs": outs, "emit": emit}


def run_tasks(sums, after, name):
    places = sums[0][0].table
    tasks = []
    for sum_, layout in sums:
        tasks.append(sum_.task() if sum_.orders[0] else sum_.last_task(layout))
    outs = serve(tasks, after, name, places)
    results, at = [], 0
    for (sum_, _), task in zip(sums, tasks, strict=True):
        got = outs[at : at + len(task["outs"])]
        at += len(task["outs"])
        if sum_.orders[0]:
            sum_.accept(got)
        else:
            results.append(got)
    return outs, results


def conv_map():
    table = np.zeros((9, 9, 4, 4), np.float32)
    for row_off in range(3):
        for col_off in range(3):
            for p in range(4):
                for q in range(4):
                    i = 2 * (row_off - 1) + p // 2 - q // 2 + 1
                    j = 2 * (col_off - 1) + p % 2 - q % 2 + 1
                    if 0 <= i < 3 and 0 <= j < 3:
                        table[i * 3 + j, row_off * 3 + col_off, p, q] = 1.0
    return table


def conv_lanes(share):
    table = conv_map().transpose(1, 0, 2, 3)
    wide = np.kron(np.eye(share, dtype=np.float32), np.ones((16, 16), np.float32))
    small = np.repeat(np.repeat(table, 4, 2), 4, 3)
    return np.tile(small, (1, 1, share, share)) * wide


def per_device(
    tokens,
    skip_tokens,
    extra_tokens,
    extra_skip,
    timesteps,
    target,
    w_skip,
    b_skip,
    norm1_gain,
    norm1_shift,
    w_qkv,
    w_out,
    b_out,
    norm2_gain,
    norm2_shift,
    w_up,
    b_up,
    w_down,
    b_down,
    final_gain,
    final_shift,
    w_head,
    b_head,
    w_conv,
    b_conv,
):
    items, rows, cols, width = tokens.shape
    hidden_units = w_up.shape[1]
    local = rows * cols
    patch_values = w_head.shape[1]
    chans = w_conv.shape[3]
    devices = lax.axis_size(ALL)
    groups = lax.axis_size(PLANE)
    place = lax.axis_index(PLANE)
    share = items // groups
    per_item = groups * local
    count = share * per_item
    head_dim = width // HEADS
    height, breadth = rows * PATCH, cols * PATCH

    def row(vector):
        return vector.astype(F32).reshape(1, -1)

    def to_items(array):
        return lax.all_to_all(array, PLANE, split_axis=0, concat_axis=0, tiled=True)

    some = 8
    joined_rows = 2 * local + 8
    tile_block = pl.BlockSpec((some, rows, cols, width), lambda i: (i, 0, 0, 0))
    flat_block = pl.BlockSpec((some, local, width), lambda i: (i, 0, 0))
    hidden0, joined = pl.pallas_call(
        merge_kernel,
        grid=(items // some,),
        in_specs=[tile_block, tile_block, whole((2 * width, width)), whole((width,))],
        out_specs=[flat_block, pl.BlockSpec((some, joined_rows, width), lambda i: (i, 0, 0))],
        out_shape=[sds((items, local, width), BF), sds((items, joined_rows, width), BF)],
        compiler_params=params(),
        cost_estimate=cost(items * local * 4 * width * width, 11e6),
        name="merge",
    )(tokens, skip_tokens, w_skip, b_skip)
    hidden0 = to_items(hidden0)
    hidden0 = hidden0.reshape(groups, share, local, width)
    target_patches = (
        target.reshape(items, rows, PATCH, cols, PATCH, chans)
        .transpose(0, 1, 3, 2, 4, 5)
        .reshape(items, local * patch_values)
    )
    high = lax.reduce_precision(target_patches, 8, 7)
    middle = lax.reduce_precision(target_patches - high, 8, 7)
    low = target_patches - high - middle
    thirds = jnp.concatenate([high, middle, low], 1).astype(BF).reshape(items, -1, width)
    joined = lax.dynamic_update_slice(joined, thirds, (0, 2 * local, 0))

    start = place * share
    joined_extra = jnp.concatenate(
        [
            lax.dynamic_slice_in_dim(extra_tokens, start, share, 0),
            lax.dynamic_slice_in_dim(extra_skip, start, share, 0),
        ],
        2,
    )
    extra_rows = share * EXTRA_PAD
    joined_extra = jnp.pad(joined_extra, ((0, 0), (0, EXTRA_PAD - 2), (0, 0)))
    joined_extra = joined_extra.reshape(extra_rows, 2 * width)
    hidden_extra = dot(joined_extra, w_skip, 1, 0) + row(b_skip)
    unit_extra, _ = norm_parts(hidden_extra)
    normed_extra = (unit_extra * row(norm1_gain) + row(norm1_shift)).astype(BF)
    pairs_extra = dot(normed_extra, w_qkv[:, width:], 1, 0).astype(BF)

    def by_head(block):
        return block.reshape(share, EXTRA_PAD, HEADS, head_dim).transpose(0, 2, 1, 3)

    key_extra = by_head(pairs_extra[:, :width])
    value_extra = by_head(pairs_extra[:, width:])

    weight = lax.dynamic_slice_in_dim(noise_weight(timesteps), start, share, 0)
    lanes = share * patch_values
    spread = jnp.tile(w_conv.reshape(9, chans, chans), (1, lanes // chans, lanes // chans))
    kernel = jnp.sum(jnp.asarray(conv_lanes(share)) * spread[None].astype(F32), 1).astype(BF)
    lane_rows = jnp.concatenate(
        [
            jnp.tile(b_head.astype(F32), share),
            jnp.tile(b_conv.astype(F32), lanes // chans),
            jnp.repeat(weight, patch_values),
        ]
    ).reshape(3, lanes)
    joined = lax.optimization_barrier(
        (joined, key_extra, value_extra, kernel, lane_rows, normed_extra)
    )[0]
    joined = to_items(joined).reshape(groups, share, joined_rows, width)
    thirds = joined[:, :, 2 * local : 2 * local + thirds.shape[1]].astype(F32)
    thirds = thirds.reshape(groups, share, 3, local, patch_values)
    target_own = (
        (thirds[:, :, 0] + thirds[:, :, 1] + thirds[:, :, 2])
        .transpose(0, 2, 1, 3)
        .reshape(per_item, share * patch_values)
    )

    vec = whole((width,))
    item_block = pl.BlockSpec((groups, 1, local, width), lambda i: (0, i, 0, 0))

    def per_share(*shape):
        return pl.BlockSpec((1,) + shape, lambda i: (i,) + (0,) * len(shape))

    normed1, qkv, probs, probs_extra, mixed, hidden1 = pl.pallas_call(
        attend_kernel,
        grid=(share,),
        in_specs=[
            item_block,
            per_share(HEADS, EXTRA_PAD, head_dim),
            per_share(HEADS, EXTRA_PAD, head_dim),
            vec,
            vec,
            vec,
            whole((width, 3 * width)),
            whole((width, width)),
        ],
        out_specs=[
            per_share(per_item, width),
            per_share(3 * width, per_item),
            per_share(HEADS, per_item, per_item),
            per_share(HEADS, EXTRA_PAD, per_item),
            per_share(width, per_item),
            per_share(per_item, width),
        ],
        out_shape=[
            sds((share, per_item, width), BF),
            sds((share, 3 * width, per_item), BF),
            sds((share, HEADS, per_item, per_item), BF),
            sds((share, HEADS, EXTRA_PAD, per_item), BF),
            sds((share, width, per_item), BF),
            sds((share, per_item, width), F32),
        ],
        compiler_params=params(),
        cost_estimate=cost(count * (8 * width * width + 16 * per_item * width), 25e6, 3e6),
        name="attend",
    )(
        hidden0,
        key_extra,
        value_extra,
        norm1_gain,
        norm1_shift,
        b_out,
        w_qkv,
        w_out,
    )
    hidden1 = hidden1.reshape(count, width)

    chunk = width
    chunks = hidden_units // chunk
    by_col = pl.BlockSpec((1, count, chunk), lambda j: (j, 0, 0))
    active, slope, normed2, change = pl.pallas_call(
        forward_kernel,
        grid=(chunks,),
        in_specs=[
            whole((count, width)),
            vec,
            vec,
            whole((hidden_units,)),
            pl.BlockSpec((width, chunk), lambda j: (0, j)),
            pl.BlockSpec((chunk, width), lambda j: (j, 0)),
        ],
        out_specs=[by_col, by_col, whole((count, width)), whole((count, width))],
        out_shape=[
            sds((chunks, count, chunk), BF),
            sds((chunks, count, chunk), BF),
            sds((count, width), BF),
            sds((count, width), F32),
        ],
        scratch_shapes=[pltpu.VMEM((chunks, chunk), F32)],
        compiler_params=params(),
        cost_estimate=cost(count * 4 * width * hidden_units, 25e6, 5e6),
        name="forward",
    )(hidden1, norm2_gain, norm2_shift, b_up, w_up, w_down)
    (
        result,
        grad_hidden2,
        grad_down,
        grad_head,
        sums_final,
        head_sum,
        conv_sum,
        conv_bias,
    ) = pl.pallas_call(
        functools.partial(turn_kernel, rows, cols, lax.axis_size("tx")),
        grid=(1,),
        in_specs=[
            whole((count, width)),
            whole((count, width)),
            vec,
            vec,
            vec,
            whole((patch_values, width)),
            whole((9, lanes, lanes)),
            whole((3, lanes)),
            whole((per_item, lanes)),
            pl.BlockSpec(memory_space=pl.ANY),
        ],
        out_specs=[
            whole((per_item, lanes)),
            whole((count, width)),
            whole((count, width)),
            whole((1, lanes)),
            whole((8, width)),
            whole((share, lanes, width)),
            whole((9, lanes, lanes)),
            whole((1, lanes)),
        ],
        out_shape=[
            sds((per_item, lanes), BF),
            sds((count, width), F32),
            sds((count, width), BF),
            sds((1, lanes), F32),
            sds((8, width), F32),
            sds((share, lanes, width), F32),
            sds((9, lanes, lanes), F32),
            sds((1, lanes), F32),
        ],
        scratch_shapes=[pltpu.VMEM((count, width), F32)],
        compiler_params=params(),
        cost_estimate=cost(1e9, 10e6),
        name="turn",
    )(
        hidden1,
        change,
        b_down,
        final_gain,
        final_shift,
        w_head.T,
        kernel,
        lane_rows,
        target_own,
        joined,
    )

    any_place = pl.BlockSpec(memory_space=pl.ANY)
    table = place_table()
    core = lax.axis_index("tx") % 2
    core = core.astype(jnp.int32).reshape(1)
    core_spec = pl.BlockSpec(memory_space=pltpu.SMEM)

    def split_outs(units, rows, block_rows, own, cols, index):
        if can_split(own):
            spec = pl.BlockSpec(
                (units, block_rows // (2 * own), own, cols), lambda j: index(j) + (0, 0)
            )
            return spec, lambda n: sds((n, rows // (2 * own), own, cols), BF), 2
        spec = pl.BlockSpec((units, block_rows, cols), lambda j: index(j) + (0,))
        return spec, lambda n: sds((n, rows, cols), BF), 1

    grad_w_down = pl.pallas_call(
        down_kernel,
        grid=(chunks,),
        in_specs=[by_col, whole((count, width))],
        out_specs=pl.BlockSpec((chunk, width), lambda j: (j, 0)),
        out_shape=sds((hidden_units, width), BF),
        compiler_params=params(),
        cost_estimate=cost(count * 2 * width * hidden_units, 11e6),
        name="down_weight",
    )(active, grad_down)
    out_down = lax.psum_scatter(grad_w_down, ALL, scatter_dimension=0, tiled=True).astype(F32)

    own = width // devices
    up_spec, up_shape, up_outs = split_outs(2, width, width, own, width // 2, lambda j: (j, 0))

    def held_col(j):
        return jnp.minimum(j, chunks - 1)

    grad_b_up, grad_hidden1, grad_branch, sums_up, *grad_w_up = pl.pallas_call(
        functools.partial(up_kernel, own),
        grid=(chunks + 1,),
        in_specs=[
            pl.BlockSpec((1, count, chunk), lambda j: (held_col(j), 0, 0)),
            whole((count, width)),
            pl.BlockSpec((chunk, width), lambda j: (held_col(j), 0)),
            pl.BlockSpec((width, chunk), lambda j: (0, held_col(j))),
            whole((count, width)),
            whole((count, width)),
            vec,
            whole((count, width)),
            whole((share, width, per_item)),
            core_spec,
            any_place,
        ],
        out_specs=[
            pl.BlockSpec((1, 8, chunk), lambda j: (held_col(j), 0, 0)),
            whole((count, width)),
            whole((count, width)),
            whole((8, width)),
        ]
        + [up_spec] * up_outs,
        out_shape=[
            sds((chunks, 8, chunk), F32),
            sds((count, width), F32),
            sds((count, width), BF),
            sds((8, width), F32),
        ]
        + [up_shape(2 * chunks + 2)] * up_outs,
        scratch_shapes=[pltpu.VMEM((count, width), F32)],
        compiler_params=params(),
        cost_estimate=cost(count * (6 * hidden_units + 2 * width) * width, 25e6),
        name="up_weight",
    )(
        slope,
        grad_down,
        w_down,
        w_up,
        normed2,
        hidden1,
        norm2_gain,
        grad_hidden2,
        mixed,
        core,
        grad_w_down,
    )
    if can_split(own):
        sum_up = Sum(grad_w_up, 2 * chunks + 2, 1, width // 2, table)
    up_layout = (
        [(1, 2 * chunks), (1, 2)],
        [(0, 0, k) for k in range(2 * chunks)] + [(1, 0, 0), (1, 0, 1)],
    )
    late_layout = (
        [(1, 6), (2, 2)],
        [(0, 0, k) for k in range(6)] + [(1, 0, 0), (1, 1, 0), (1, 0, 1), (1, 1, 1)],
    )

    after = sum_up.sent if can_split(own) else []
    grad_qkv, grad_key_extra, grad_value_extra = [], [], []
    sums_attend = jnp.zeros((8, width), F32)
    grad_hidden0 = None
    back_rows = share * local + 16
    for item in range(share):

        def one(*shape, item=item):
            return pl.BlockSpec(
                (1,) + shape, lambda *_: (item,) + (0,) * len(shape), pipeline_mode=pl.Buffered(1)
            )

        one_block = pl.BlockSpec(
            (groups, 1, local, width), lambda *_, item=item: (0, item, 0, 0)
        )
        held = [grad_hidden0] if item else []
        outs = pl.pallas_call(
            attend_back_kernel,
            grid=(1,),
            in_specs=[
                one_block,
                one(per_item, width),
                one(per_item, width),
                one(3 * width, per_item),
                one(HEADS, per_item, per_item),
                one(HEADS, EXTRA_PAD, per_item),
                one(HEADS, EXTRA_PAD, head_dim),
                one(HEADS, EXTRA_PAD, head_dim),
                vec,
                whole((width, 3 * width)),
                whole((width, width)),
                whole((8, width)),
            ]
            + [any_place] * (len(held) + len(after)),
            out_specs=[
                whole((3 * width, per_item)),
                whole((HEADS, EXTRA_PAD, head_dim)),
                whole((HEADS, EXTRA_PAD, head_dim)),
                pl.BlockSpec((groups, local, width), lambda *_, item=item: (0, item, 0)),
                whole((8, width)),
            ],
            out_shape=[
                sds((3 * width, per_item), BF),
                sds((HEADS, EXTRA_PAD, head_dim), F32),
                sds((HEADS, EXTRA_PAD, head_dim), F32),
                sds((groups, back_rows, width), BF),
                sds((8, width), F32),
            ],
            input_output_aliases={12: 3} if item else {},
            scratch_shapes=[pltpu.VMEM((width, per_item), BF)],
            compiler_params=params(),
            cost_estimate=cost(
                per_item * (8 * width * width + 40 * per_item * width), 12e6
            ),
            name="attend_back",
        )(
            hidden0,
            grad_hidden1.reshape(share, per_item, width),
            grad_branch.reshape(share, per_item, width),
            qkv,
            probs,
            probs_extra,
            key_extra,
            value_extra,
            norm1_gain,
            w_qkv,
            w_out,
            sums_attend,
            *held,
            *after,
        )
        grad_qkv.append(outs[0])
        grad_key_extra.append(outs[1])
        grad_value_extra.append(outs[2])
        grad_hidden0, sums_attend = outs[3], outs[4]
        if can_split(own):
            after, _ = run_tasks([(sum_up, None)], [sums_attend], "serve_" + str(item + 2))
    latent = result.reshape(groups, local * share * patch_values // width, width)
    pairs_extra, grad_extra, sums_attend, grad_back = pl.pallas_call(
        functools.partial(extra_back_kernel, share),
        grid=(1,),
        in_specs=[
            whole((extra_rows, width)),
            vec,
            pl.BlockSpec((width, width), lambda *_: (0, 1)),
            pl.BlockSpec((width, width), lambda *_: (0, 2)),
            whole(latent.shape),
            whole((8, width)),
        ]
        + [whole((HEADS, EXTRA_PAD, head_dim))] * (2 * share)
        + [any_place] * (1 + len(after)),
        out_specs=[
            whole((2, extra_rows, width)),
            whole((extra_rows, width)),
            whole((8, width)),
            pl.BlockSpec((groups, 16, width), lambda *_: (0, share * local // 16, 0)),
        ],
        out_shape=[
            sds((2, extra_rows, width), BF),
            sds((extra_rows, width), BF),
            sds((8, width), F32),
            sds((groups, back_rows, width), BF),
        ],
        input_output_aliases={6 + 2 * share: 3},
        compiler_params=params(),
        cost_estimate=cost(1e8, 5e6),
        name="extra_back",
    )(
        hidden_extra,
        norm1_gain,
        w_qkv,
        w_qkv,
        latent,
        sums_attend,
        *grad_key_extra,
        *grad_value_extra,
        grad_hidden0,
        *after,
    )
    back = to_items(grad_back)

    late_spec, late_shape, late_outs = split_outs(
        2, width, width, own, width // 2, lambda j: (j, 0)
    )

    def skip_col(j):
        return jnp.maximum(j - 3, 0)

    def qkv_row(j):
        return jnp.minimum(j, 2)

    half = width // 2
    grad_late = pl.pallas_call(
        functools.partial(late_weight_kernel, own),
        grid=(5,),
        in_specs=[
            whole((share, per_item, width)),
            whole((extra_rows, width)),
            pl.BlockSpec(
                (1, extra_rows, width), lambda j: (jnp.clip(j - 1, 0, 1), 0, 0)
            ),
            whole(joined.shape),
            pl.BlockSpec((groups, back_rows, half), lambda j: (0, 0, skip_col(j))),
            whole((extra_rows, 2 * width)),
            pl.BlockSpec((extra_rows, half), lambda j: (0, skip_col(j))),
        ]
        + [pl.BlockSpec((width, per_item), lambda j: (qkv_row(j), 0))] * share
        + [core_spec],
        out_specs=[late_spec] * late_outs,
        out_shape=[late_shape(10)] * late_outs,
        compiler_params=params(),
        cost_estimate=cost(count * 10 * width * width, 12e6),
        name="late_weight",
    )(
        normed1,
        normed_extra,
        pairs_extra,
        joined,
        grad_back,
        joined_extra,
        grad_extra,
        *grad_qkv,
        core,
    )

    def hold(values, *others):
        return lax.optimization_barrier((values, others))[0]

    stacked_count = 9 + patch_values
    stacked, shared = pl.pallas_call(
        pack_kernel,
        in_specs=[pl.BlockSpec(memory_space=pltpu.VMEM)] * 8 + [any_place],
        out_specs=[pl.BlockSpec(memory_space=pltpu.VMEM)] * 2,
        out_shape=[sds((stacked_count, width), F32), sds((8, 128), F32)],
        compiler_params=params(),
        cost_estimate=cost(1e6, 1e6),
        name="pack",
    )(
        sums_attend,
        sums_up,
        sums_final,
        head_sum,
        grad_head,
        conv_sum,
        conv_bias,
        jnp.asarray(conv_lanes(share), BF),
        grad_late[0],
    )
    packed = jnp.concatenate(
        [
            stacked.reshape(stacked_count, devices, own).transpose(1, 0, 2).reshape(devices, -1),
            grad_b_up[:, 0].reshape(devices, -1),
            jnp.broadcast_to(shared[:4].reshape(1, -1), (devices, 512)),
        ],
        1,
    )
    packed_size = packed.shape[1]
    packed = jnp.pad(packed, ((0, 0), (0, (-packed.shape[1]) % 128)))
    if not can_split(own):
        wide = grad_w_up[0].transpose(1, 0, 2).reshape(width, -1)
        wide = lax.psum_scatter(wide, ALL, scatter_dimension=0, tiled=True).astype(F32)
        out_up, out_out = wide[:, :hidden_units], wide[:, hidden_units:]
        wide = grad_late[0][:6].transpose(1, 0, 2).reshape(width, -1)
        out_qkv = lax.psum_scatter(wide, ALL, scatter_dimension=0, tiled=True).astype(F32)
        tall = grad_late[0][6:].reshape(2, 2, width, half).transpose(1, 2, 0, 3)
        tall = tall.reshape(2 * width, width)
        out_skip = lax.psum_scatter(tall, ALL, scatter_dimension=0, tiled=True).astype(F32)
    else:
        sum_late = Sum(grad_late, 10, 1, half, table)
        after, _ = run_tasks([(sum_late, None)], [packed], "serve_5")
    some_groups = max(groups // 2, 1)
    token_block = pl.BlockSpec(
        (some_groups * share, rows, cols, width), lambda i: (i, 0, 0, 0)
    )
    grad_tokens, grad_skip_tokens, grad_extra_all = pl.pallas_call(
        token_kernel,
        grid=(groups // some_groups,),
        in_specs=[
            pl.BlockSpec((some_groups, back_rows, width), lambda i: (i, 0, 0)),
            whole((2 * width, width)),
        ],
        out_specs=[
            token_block,
            token_block,
            pl.BlockSpec((some_groups, 16, 2 * width), lambda i: (i, 0, 0)),
        ],
        out_shape=[sds(tokens.shape, BF)] * 2 + [sds((groups, 16, 2 * width), BF)],
        compiler_params=params(),
        cost_estimate=cost(items * local * 4 * width * width, 8e6),
        name="tokens",
    )(hold(back, after), w_skip)
    if can_split(own):
        while len(sum_up.orders[0]) > 1:
            after, _ = run_tasks([(sum_up, None)], after, "serve_more")
        after, _ = run_tasks([(sum_late, None), (sum_up, None)], [grad_tokens], "serve_6")
        after, results = run_tasks([(sum_late, None), (sum_up, up_layout)], after, "serve_7")
        out_up, out_out = results[0]
    exchanged = lax.all_to_all(hold(packed, back), ALL, split_axis=0, concat_axis=0, tiled=True)
    if can_split(own):
        while sum_late.orders[0]:
            after, _ = run_tasks([(sum_late, None)], after, "serve_8")
    summed = jnp.sum(hold(exchanged, after), 0)
    small = [summed[k * own : (k + 1) * own] for k in range(9)]
    own_head = summed[9 * own : stacked_count * own].reshape(patch_values, own).T
    up_low = stacked_count * own
    own_b_up = summed[up_low : up_low + hidden_units // devices]
    shared = summed[up_low + hidden_units // devices : packed_size].reshape(4, 128)

    latent_row = share * local + 2 * share
    latent = back[:, latent_row : latent_row + latent.shape[1]]
    latent_out = (
        hold(latent, after)
        .reshape(groups, rows, cols, share, PATCH, PATCH, chans)
        .transpose(0, 3, 1, 4, 2, 5, 6)
        .reshape(items, height, breadth, chans)
    )
    grad_joined_extra = grad_extra_all[:, : 2 * share].reshape(items, 2, 2 * width)
    if can_split(own):
        _, results = run_tasks([(sum_late, late_layout)], after, "serve_9")
        out_qkv, out_skip = results[0]
    return (
        latent_out,
        grad_tokens,
        grad_skip_tokens,
        grad_joined_extra[..., :width],
        grad_joined_extra[..., width:],
        out_skip,
        small[0],
        small[1],
        small[2],
        out_qkv,
        out_out,
        small[3],
        small[4],
        small[5],
        out_up,
        own_b_up,
        out_down,
        small[6],
        small[7],
        small[8],
        own_head,
        shared[0, 64 : 64 + patch_values],
        shared[:, : 9 * chans].reshape(chans, 3, 3, chans).transpose(1, 2, 0, 3),
        shared[0, 96 : 96 + chans],
    )


def solution(mesh):
    tiles = P("batch", "ty", "tx", None)
    pairs = P("batch", None, None)
    matrix = P(ALL, None)
    vector = P(ALL)
    return jax.shard_map(
        per_device,
        mesh=mesh,
        in_specs=(tiles, tiles, pairs, pairs, P("batch"), tiles) + (P(),) * 19,
        out_specs=(
            tiles,
            tiles,
            tiles,
            pairs,
            pairs,
            matrix,
            vector,
            vector,
            vector,
            matrix,
            matrix,
            vector,
            vector,
            vector,
            matrix,
            vector,
            matrix,
            vector,
            vector,
            vector,
            matrix,
            P(),
            P(),
            P(),
        ),
        check_vma=False,
    )
```

```python
import functools

import jax
import jax.numpy as jnp
import numpy as np
from jax import lax
from jax.experimental import pallas as pl
from jax.experimental.pallas import tpu as pltpu
from jax.sharding import PartitionSpec as P

HEADS = 12
PATCH = 2
EXTRA_PAD = 8
CHAIN_DOWN = True
EPS = 1e-05
BF = jnp.bfloat16
F32 = jnp.float32
PLANE = ("ty", "tx")
ALL = ("batch", "ty", "tx")
MIB = 1024 * 1024


def dot(left, right, left_dim, right_dim):
    return lax.dot_general(
        left, right, (((left_dim,), (right_dim,)), ((), ())), preferred_element_type=F32
    )


def norm_parts(values):
    center = values - jnp.mean(values, -1, keepdims=True)
    scaled = lax.rsqrt(jnp.mean(center * center, -1, keepdims=True) + EPS)
    return center * scaled, scaled


def norm_back(inner, normed, scaled):
    return scaled * (
        inner
        - jnp.mean(inner, -1, keepdims=True)
        - normed * jnp.mean(inner * normed, -1, keepdims=True)
    )


def flat(ref):
    return ref[...].astype(F32).reshape(1, -1)


def row_sum(values):
    return jnp.sum(values, 0, keepdims=True)


def gelu_parts(upper):
    spread = 0.5 + 0.5 * lax.erf(upper * np.float32(0.5**0.5))
    bell = jnp.exp(upper * upper * -0.5) * np.float32((2 * np.pi) ** -0.5)
    return upper * spread, spread + upper * bell


def noise_weight(timesteps):
    frac = (timesteps.astype(F32) / 1000.0 + 0.008) / 1.008
    kept = jnp.cos(frac * (0.5 * jnp.pi)) ** 2
    return jnp.minimum(1.0, 5.0 * (1.0 - kept) / kept)


def can_split(own):
    return own % 8 == 0


def store_split(value, own, lane_refs):
    if len(lane_refs) == 1:
        lane_refs[0][...] = value.astype(BF)
        return
    keep_ref, send_ref, core_ref = lane_refs
    pairs = value.reshape(value.shape[0] // (2 * own), 2, own, value.shape[1])
    first = core_ref[0] == 0
    keep = jnp.where(first, pairs[:, 0], pairs[:, 1])
    send = jnp.where(first, pairs[:, 1], pairs[:, 0])
    keep_ref[...] = keep.astype(BF)
    send_ref[...] = send.astype(BF)


def merge_kernel(tokens_ref, skip_ref, w_skip_ref, b_skip_ref, hidden_ref, joined_ref):
    width = w_skip_ref.shape[1]
    local = tokens_ref.shape[1] * tokens_ref.shape[2]
    body = tokens_ref[...].reshape(-1, width)
    body_skip = skip_ref[...].reshape(-1, width)
    hidden = (
        dot(body, w_skip_ref[:width], 1, 0)
        + dot(body_skip, w_skip_ref[width:], 1, 0)
        + b_skip_ref[...].astype(F32).reshape(1, width)
    )
    hidden_ref[...] = hidden.astype(BF).reshape(-1, local, width)
    joined_ref[:, :local] = body.reshape(-1, local, width)
    joined_ref[:, local : 2 * local] = body_skip.reshape(-1, local, width)


def attend_kernel(
    hidden_ref,
    key_extra_ref,
    value_extra_ref,
    gain_ref,
    shift_ref,
    b_out_ref,
    w_qkv_ref,
    w_out_ref,
    normed_ref,
    qkv_ref,
    probs_ref,
    probs_extra_ref,
    mixed_ref,
    hidden1_ref,
    scores_ref,
    scores_extra_ref,
):
    width = w_out_ref.shape[0]
    head_dim = width // HEADS
    scale = head_dim ** (-0.5)
    rows = hidden_ref.shape[0] * hidden_ref.shape[2]
    hidden = hidden_ref[...].reshape(rows, width).astype(F32)
    unit, _ = norm_parts(hidden)
    normed = (unit * flat(gain_ref) + flat(shift_ref)).astype(BF)
    normed_ref[0] = normed
    qkv_ref[0] = dot(w_qkv_ref[...], normed, 0, 1).astype(BF)
    live = lax.broadcasted_iota(jnp.int32, (EXTRA_PAD, rows), 0) < 2
    for head in range(HEADS):
        low = head * head_dim
        query = qkv_ref[0, low : low + head_dim, :]
        key = qkv_ref[0, width + low : width + low + head_dim, :]
        scores_ref[head] = dot(key, query, 0, 0) * scale
        scores_extra = dot(key_extra_ref[0, head], query, 1, 0) * scale
        scores_extra_ref[head] = jnp.where(live, scores_extra, -1e30)
    for head in range(HEADS):
        scores, scores_extra = scores_ref[head], scores_extra_ref[head]
        top = jnp.maximum(
            jnp.max(scores, 0, keepdims=True), jnp.max(scores_extra, 0, keepdims=True)
        )
        raised = jnp.exp(scores - top)
        raised_extra = jnp.exp(scores_extra - top)
        share = 1.0 / (row_sum(raised) + row_sum(raised_extra))
        probs_ref[0, head] = (raised * share).astype(BF)
        probs_extra_ref[0, head] = (raised_extra * share).astype(BF)
    for head in range(HEADS):
        low = head * head_dim
        value = qkv_ref[0, 2 * width + low : 2 * width + low + head_dim, :]
        mixed = dot(value, probs_ref[0, head], 1, 0) + dot(
            value_extra_ref[0, head], probs_extra_ref[0, head], 0, 0
        )
        mixed_ref[0, low : low + head_dim, :] = mixed.astype(BF)
    hidden1_ref[0] = hidden + (dot(mixed_ref[0], w_out_ref[...], 0, 0) + flat(b_out_ref))


def forward_kernel(
    hidden1_ref,
    gain2_ref,
    shift2_ref,
    b_up_ref,
    b_down_ref,
    w_up_ref,
    w_down_ref,
    active_ref,
    slope_ref,
    normed2_ref,
    total,
    up_rows,
):
    step = pl.program_id(0)

    @pl.when(step == 0)
    def _():
        unit, _ = norm_parts(hidden1_ref[...])
        b_up = flat(b_up_ref)
        width = up_rows.shape[1]
        for j in range(up_rows.shape[0]):
            up_rows[j : j + 1] = b_up[:, j * width : (j + 1) * width]
        normed2_ref[...] = (unit * flat(gain2_ref) + flat(shift2_ref)).astype(BF)

    count = normed2_ref.shape[0]
    blocks = 3 if count % 48 == 0 else 1
    size = count // blocks
    rows = [slice(i * size, (i + 1) * size) for i in range(blocks)]

    def raise_rows(i):
        return dot(normed2_ref[rows[i]], w_up_ref[...], 1, 0) + up_rows[pl.ds(step, 1)]

    def activate(upper, i):
        active, slope = gelu_parts(upper)
        active = active.astype(BF)
        active_ref[0, rows[i]] = active
        slope_ref[0, rows[i]] = slope.astype(BF)
        return active

    def lower(active, i):
        part = dot(active, w_down_ref[...], 1, 0)
        base = jnp.where(step == 0, hidden1_ref[rows[i]] + flat(b_down_ref), total[rows[i]])
        total[rows[i]] = base + part

    upper = raise_rows(0)
    for i in range(blocks):
        following = raise_rows(i + 1) if i + 1 < blocks else None
        active = activate(upper, i)
        upper = following
        lower(active, i)


def turn_kernel(
    tile_rows,
    tile_cols,
    tiles_x,
    hidden2_ref,
    gainf_ref,
    shiftf_ref,
    w_head_ref,
    w_conv_ref,
    lanes_ref,
    target_ref,
    after_ref,
    result_ref,
    grad_hidden2_ref,
    grad_down_ref,
    grad_head_ref,
    sums_ref,
    head_sum_ref,
    conv_sum_ref,
    conv_bias_ref,
    total,
):
    per_item, lanes = target_ref.shape
    patch_values, width = w_head_ref.shape
    items = lanes // patch_values

    def head_of(i):
        parts = [w_head_ref[...]]
        if i > 0:
            parts = [jnp.zeros((i * patch_values, width), BF)] + parts
        if i < items - 1:
            parts = parts + [jnp.zeros((lanes - (i + 1) * patch_values, width), BF)]
        return jnp.concatenate(parts, 0)

    heads = [head_of(i) for i in range(items)]
    unit, scaled = norm_parts(hidden2_ref[...])
    total[...] = unit
    normedf = (unit * flat(gainf_ref) + flat(shiftf_ref)).astype(BF)
    normed2_final = [normedf[i * per_item : (i + 1) * per_item] for i in range(items)]
    patches = lanes_ref[0:1]
    for i in range(items):
        patches = patches + dot(normed2_final[i], heads[i], 1, 1)
    patches = patches.astype(BF)

    def place(position):
        tile = position // (tile_rows * tile_cols)
        row = (tile // tiles_x) * tile_rows + (position // tile_cols) % tile_rows
        col = (tile % tiles_x) * tile_cols + position % tile_cols
        return row * 1024 + col

    own = place(lax.broadcasted_iota(jnp.int32, (per_item, 1), 0))
    other = place(lax.broadcasted_iota(jnp.int32, (1, per_item), 1))
    shifts = []
    for row_off in range(3):
        for col_off in range(3):
            wanted = own + ((row_off - 1) * 1024 + (col_off - 1))
            shifts.append(jnp.where(wanted == other, 1.0, 0.0).astype(BF))
    windows = [dot(shift, patches, 1, 0).astype(BF) for shift in shifts]
    result = lanes_ref[1:2]
    for k in range(9):
        result = result + dot(windows[k], w_conv_ref[k], 1, 0)
    result_ref[...] = result.astype(BF)
    grad_result = (lanes_ref[2:3] * (result - target_ref[...])).astype(BF)
    conv_bias_ref[...] = row_sum(grad_result.astype(F32))
    grad_patches = jnp.zeros(target_ref.shape, F32)
    for k in range(9):
        conv_sum_ref[k] = dot(windows[k], grad_result, 0, 0)
        moved = dot(shifts[8 - k], grad_result, 1, 0).astype(BF)
        grad_patches = grad_patches + dot(moved, w_conv_ref[k], 1, 1)
    grad_patches = grad_patches.astype(BF)
    grad_head_ref[...] = row_sum(grad_patches.astype(F32))
    sum_gain = jnp.zeros((1, unit.shape[1]), F32)
    sum_shift = sum_gain
    sum_down = sum_gain
    for i in range(items):
        rows = slice(i * per_item, (i + 1) * per_item)
        head_sum_ref[i] = dot(grad_patches, normed2_final[i], 0, 0)
        grad_normedf = dot(grad_patches, heads[i], 1, 0)
        unit_part = total[rows]
        sum_gain = sum_gain + row_sum(grad_normedf * unit_part)
        sum_shift = sum_shift + row_sum(grad_normedf)
        grad_hidden2 = norm_back(grad_normedf * flat(gainf_ref), unit_part, scaled[rows])
        grad_hidden2_ref[rows] = grad_hidden2
        grad_down = grad_hidden2.astype(BF)
        grad_down_ref[rows] = grad_down
        sum_down = sum_down + row_sum(grad_down.astype(F32))
    sums_ref[0:1] = sum_gain
    sums_ref[1:2] = sum_shift
    sums_ref[2:3] = sum_down


def down_kernel(own, split, active_ref, grad_down_ref, core_ref, *outs):
    total = dot(active_ref[0], grad_down_ref[...], 0, 0)
    if not split:
        outs[0][...] = total.astype(BF)
        return
    pairs = total.reshape(total.shape[0] // (8 * own), 2, 4, own, total.shape[1])
    first = core_ref[0] == 0
    half = total.shape[1] // 2
    for part in range(4):
        low, high = pairs[:, 0, part], pairs[:, 1, part]
        keep = jnp.where(first, low, high).astype(BF)
        send = jnp.where(first, high, low).astype(BF)
        for side in range(2):
            cols = slice(side * half, (side + 1) * half)
            outs[0][2 * part + side] = keep[:, :, cols]
            outs[1][2 * part + side] = send[:, :, cols]


def up_kernel(
    own,
    slope_ref,
    grad_down_ref,
    w_down_ref,
    w_up_ref,
    normed2_ref,
    hidden1_ref,
    gain2_ref,
    grad_hidden2_ref,
    mixed_ref,
    core_ref,
    *rest,
):
    total = rest[-1]
    rest = rest[-7 if can_split(own) else -6 : -1]
    grad_b_up_ref, grad_hidden1_ref, grad_branch_ref, sums_ref = rest[:4]
    rest = rest[4:]
    step = pl.program_id(0)
    steps = pl.num_programs(0)

    def store(value):
        half = value.shape[1] // 2
        for side in range(2):
            piece = value[:, side * half : (side + 1) * half]
            if can_split(own):
                store_split(piece, own, (rest[0].at[side], rest[1].at[side], core_ref))
            else:
                store_split(piece, own, (rest[0].at[side],))

    @pl.when(step < steps - 1)
    def _():
        grad_active = dot(grad_down_ref[...], w_down_ref[...], 1, 1)
        grad_upper = (grad_active * slope_ref[0].astype(F32)).astype(BF)
        grad_b_up_ref[0, 0:1] = row_sum(grad_upper.astype(F32))
        store(dot(normed2_ref[...], grad_upper, 0, 0))
        part = dot(grad_upper, w_up_ref[...], 1, 1)

        @pl.when(step == 0)
        def _():
            total[...] = part

        @pl.when(step > 0)
        def _():
            total[...] += part

    @pl.when(step == steps - 1)
    def _():
        unit, scaled = norm_parts(hidden1_ref[...])
        grad_normed2 = total[...]
        sums_ref[0:1] = row_sum(grad_normed2 * unit)
        sums_ref[1:2] = row_sum(grad_normed2)
        grad_hidden1 = grad_hidden2_ref[...] + norm_back(
            grad_normed2 * flat(gain2_ref), unit, scaled
        )
        grad_hidden1_ref[...] = grad_hidden1
        grad_branch = grad_hidden1.astype(BF)
        grad_branch_ref[...] = grad_branch
        sums_ref[2:3] = row_sum(grad_branch.astype(F32))
        items, _, per_item = mixed_ref.shape
        value = dot(mixed_ref[0], grad_branch[:per_item], 1, 0)
        for item in range(1, items):
            rows = slice(item * per_item, (item + 1) * per_item)
            value = value + dot(mixed_ref[item], grad_branch[rows], 1, 0)
        store(value)


def attend_back_kernel(
    hidden_ref,
    grad_hidden1_ref,
    grad_branch_ref,
    qkv_ref,
    probs_ref,
    probs_extra_ref,
    key_extra_ref,
    value_extra_ref,
    gain_ref,
    w_qkv_ref,
    w_out_ref,
    sums_in_ref,
    *rest,
):
    (
        grad_qkv_ref,
        grad_key_extra_ref,
        grad_value_extra_ref,
        grad_hidden0_ref,
        sums_ref,
        grad_mixed_ref,
        grad_probs_ref,
        grad_probs_extra_ref,
        grad_scores_ref,
        grad_scores_extra_ref,
    ) = rest[-10:]
    width = w_out_ref.shape[0]
    head_dim = width // HEADS
    scale = head_dim ** (-0.5)
    rows = hidden_ref.shape[0] * hidden_ref.shape[2]
    grad_mixed_ref[...] = dot(w_out_ref[...], grad_branch_ref[0], 1, 1).astype(BF)
    for head in range(HEADS):
        low = head * head_dim
        value = qkv_ref[0, 2 * width + low : 2 * width + low + head_dim, :]
        grad_mixed = grad_mixed_ref[low : low + head_dim, :]
        grad_probs_ref[head] = dot(value, grad_mixed, 0, 0)
        grad_probs_extra_ref[head] = dot(value_extra_ref[0, head], grad_mixed, 1, 0)
    for head in range(HEADS):
        probs = probs_ref[0, head].astype(F32)
        probs_extra = probs_extra_ref[0, head].astype(F32)
        grad_probs, grad_probs_extra = grad_probs_ref[head], grad_probs_extra_ref[head]
        common = row_sum(grad_probs * probs) + row_sum(grad_probs_extra * probs_extra)
        grad_scores_ref[head] = (probs * (grad_probs - common)).astype(BF)
        grad_scores_extra_ref[head] = (probs_extra * (grad_probs_extra - common)).astype(BF)
    for head in range(HEADS):
        low = head * head_dim
        query = qkv_ref[0, low : low + head_dim, :]
        key = qkv_ref[0, width + low : width + low + head_dim, :]
        grad_mixed = grad_mixed_ref[low : low + head_dim, :]
        grad_scores, grad_scores_extra = grad_scores_ref[head], grad_scores_extra_ref[head]
        grad_query = dot(key, grad_scores, 1, 0) + dot(
            key_extra_ref[0, head], grad_scores_extra, 0, 0
        )
        grad_key = dot(query, grad_scores, 1, 1)
        grad_value = dot(grad_mixed, probs_ref[0, head], 1, 1)
        grad_key_extra_ref[0, head] = dot(grad_scores_extra, query, 1, 1) * scale
        grad_value_extra_ref[0, head] = dot(probs_extra_ref[0, head], grad_mixed, 1, 1)
        grad_qkv_ref[0, low : low + head_dim, :] = (grad_query * scale).astype(BF)
        grad_qkv_ref[0, width + low : width + low + head_dim, :] = (grad_key * scale).astype(BF)
        grad_qkv_ref[0, 2 * width + low : 2 * width + low + head_dim, :] = grad_value.astype(BF)
    grad_normed = dot(grad_qkv_ref[0], w_qkv_ref[...], 0, 1)
    unit, scaled = norm_parts(hidden_ref[...].reshape(rows, width).astype(F32))

    @pl.when(pl.program_id(0) == 0)
    def _():
        sums_ref[...] = sums_in_ref[...]

    sums_ref[0:1] += row_sum(grad_normed * unit)
    sums_ref[1:2] += row_sum(grad_normed)
    grad_hidden0 = grad_hidden1_ref[0] + norm_back(grad_normed * flat(gain_ref), unit, scaled)
    grad_low = grad_hidden0.astype(BF)
    sums_ref[2:3] += row_sum(grad_low.astype(F32))
    grad_hidden0_ref[...] = grad_low.reshape(grad_hidden0_ref.shape)


def extra_back_kernel(
    share,
    hidden_ref,
    gain_ref,
    w_key_ref,
    w_value_ref,
    latent_ref,
    sums_in_ref,
    *rest,
):
    keys, values = rest[:share], rest[share : 2 * share]
    pairs_ref, grad_ref, sums_ref, back_ref = rest[-4:]
    width = hidden_ref.shape[1]

    def rows_of(refs):
        return jnp.concatenate(
            [jnp.concatenate([ref[0, head] for ref in refs], 0) for head in range(HEADS)], 1
        ).astype(BF)

    grad_key, grad_value = rows_of(keys), rows_of(values)
    pairs_ref[0] = grad_key
    pairs_ref[1] = grad_value
    grad_normed = dot(grad_key, w_key_ref[...], 1, 1) + dot(grad_value, w_value_ref[...], 1, 1)
    unit, scaled = norm_parts(hidden_ref[...])
    grad = norm_back(grad_normed * flat(gain_ref), unit, scaled).astype(BF)
    grad_ref[...] = grad
    wide = grad.astype(F32)
    sums_ref[0:1] = sums_in_ref[0:1] + row_sum(grad_normed * unit)
    sums_ref[1:2] = sums_in_ref[1:2] + row_sum(grad_normed)
    sums_ref[2:3] = sums_in_ref[2:3] + row_sum(wide)
    real = [wide[i * EXTRA_PAD : i * EXTRA_PAD + 2] for i in range(share)]
    fill = back_ref.shape[1] - 2 * share - latent_ref.shape[1]
    for group in range(back_ref.shape[0]):
        block = real + [latent_ref[group].astype(F32), jnp.zeros((fill, width), F32)]
        back_ref[group] = jnp.concatenate(block, 0).astype(BF)


def late_weight_kernel(
    own,
    normed_ref,
    normed_extra_ref,
    pairs_ref,
    joined_ref,
    grad_ref,
    joined_extra_ref,
    grad_extra_ref,
    grad_qkv_0_ref,
    grad_qkv_1_ref,
    grad_qkv_2_ref,
    core_ref,
    *rest,
):
    step = pl.program_id(0)
    split = can_split(own)
    groups, items, _, width = joined_ref.shape
    local = (grad_ref.shape[1] - 16) // items

    @pl.when(step < 3)
    def _():
        total = dot(normed_extra_ref[...], pairs_ref[0], 0, 0)
        total = total * jnp.where(step == 0, 0.0, 1.0)
        for item, ref in enumerate((grad_qkv_0_ref, grad_qkv_1_ref, grad_qkv_2_ref)):
            total = total + dot(normed_ref[item], ref[0], 0, 1)
        half = width // 2
        for side in range(2):
            piece = total[:, side * half : (side + 1) * half]
            if split:
                store_split(piece, own, (rest[-2].at[side], rest[-1].at[side], core_ref))
            else:
                store_split(piece, own, (rest[-1].at[side],))

    @pl.when(step >= 3)
    def _():
        grad = grad_ref[:, : items * local].reshape(groups * items * local, -1)
        for side in range(2):
            joined = joined_ref[:, :, side * local : (side + 1) * local]
            joined = joined.reshape(groups * items * local, width)
            extra = joined_extra_ref[:, side * width : (side + 1) * width]
            total = dot(joined, grad, 0, 0) + dot(extra, grad_extra_ref[...], 0, 0)
            if not split:
                rest[-1][side] = total.astype(BF)
                continue
            pairs = total.reshape(width // (4 * own), 2, 2, own, total.shape[1])
            first = core_ref[0] == 0
            count = pairs.shape[0]
            for part in range(2):
                low, high = pairs[:, 0, part], pairs[:, 1, part]
                where = pl.ds(side * count, count)
                rest[-2][part, where] = jnp.where(first, low, high).astype(BF)
                rest[-1][part, where] = jnp.where(first, high, low).astype(BF)


def token_kernel(back_ref, w_skip_ref, tokens_ref, skip_ref, extra_ref):
    width = w_skip_ref.shape[1]
    items = tokens_ref.shape[0]
    local = tokens_ref.shape[1] * tokens_ref.shape[2]
    body = items // back_ref.shape[0] * local
    grad = back_ref[:, :body].reshape(items * local, width)
    tokens_ref[...] = dot(grad, w_skip_ref[:width], 1, 1).astype(BF).reshape(tokens_ref.shape)
    skip_ref[...] = dot(grad, w_skip_ref[width:], 1, 1).astype(BF).reshape(skip_ref.shape)
    extra = back_ref[:, body:].reshape(-1, width)
    extra_ref[...] = dot(extra, w_skip_ref[...], 1, 1).astype(BF).reshape(extra_ref.shape)


def fold_matrix(shape, low, wide, period):
    row = lax.broadcasted_iota(jnp.int32, shape, 0)
    col = lax.broadcasted_iota(jnp.int32, shape, 1)
    return jnp.where((col >= low) & (col < low + wide) & (row % period == col - low), 1.0, 0.0)


def pack_kernel(
    sums_attend_ref,
    sums_up_ref,
    sums_final_ref,
    head_sum_ref,
    grad_head_ref,
    conv_sum_ref,
    conv_bias_ref,
    table_ref,
    *rest,
):
    stacked_ref, shared_ref = rest[-2:]
    items, lanes, _ = head_sum_ref.shape
    values = lanes // items
    exact = functools.partial(
        jnp.dot, precision=lax.Precision.HIGHEST, preferred_element_type=F32
    )
    stacked_ref[0:1] = sums_attend_ref[2:3]
    stacked_ref[1:2] = sums_attend_ref[0:1]
    stacked_ref[2:3] = sums_attend_ref[1:2]
    stacked_ref[3:4] = sums_up_ref[2:3]
    stacked_ref[4:6] = sums_up_ref[0:2]
    stacked_ref[6:7] = sums_final_ref[2:3]
    stacked_ref[7:9] = sums_final_ref[0:2]
    head = head_sum_ref[0, 0:values]
    for item in range(1, items):
        head = head + head_sum_ref[item, item * values : (item + 1) * values]
    stacked_ref[9 : 9 + values] = head
    row = lax.broadcasted_iota(jnp.int32, (8, lanes), 0)
    col = lax.broadcasted_iota(jnp.int32, (8, lanes), 1)
    left = jnp.where(col % 4 == row, 1.0, 0.0)
    shared = jnp.zeros((8, 128), F32)
    for tap in range(9):
        picked = conv_sum_ref[0] * table_ref[0, tap].astype(F32)
        for k in range(1, 9):
            picked = picked + conv_sum_ref[k] * table_ref[k, tap].astype(F32)
        shared = shared + exact(exact(left, picked), fold_matrix((lanes, 128), 4 * tap, 4, 4))
    bias = exact(grad_head_ref[...], fold_matrix((lanes, 128), 64, values, values))
    bias = bias + exact(conv_bias_ref[...], fold_matrix((lanes, 128), 96, 4, 4))
    first = lax.broadcasted_iota(jnp.int32, (8, 128), 0) == 0
    shared_ref[...] = shared + jnp.where(first, bias, 0.0)


def whole(shape):
    return pl.BlockSpec(shape, lambda *_: (0,) * len(shape), pipeline_mode=pl.Buffered(1))


def params():
    return pltpu.CompilerParams(vmem_limit_bytes=60 * MIB)


def cost(flops, moved, transcendentals=0):
    del flops, moved, transcendentals
    return pl.CostEstimate(flops=1024, bytes_accessed=1024, transcendentals=0)


def sds(shape, dtype):
    return jax.ShapeDtypeStruct(shape, dtype)


def swap(block, axis, gap):
    count = lax.axis_size(axis)
    return lax.ppermute(block, axis, [(i, i ^ gap) for i in range(count)])


def serve_kernel(tasks, places_ref, *refs):
    del places_ref
    inputs = sum(len(parts) for task in tasks for parts in task["sides"])
    outs = refs[len(refs) - sum(len(task["outs"]) for task in tasks) :]
    at, out_at = 0, 0
    del inputs
    for task in tasks:
        values = []
        for parts in task["sides"]:
            total = refs[at][...].astype(F32)
            for k in range(1, len(parts)):
                total = total + refs[at + k][...].astype(F32)
            at += len(parts)
            values.append(total)
        task["emit"](values, outs[out_at : out_at + len(task["outs"])])
        out_at += len(task["outs"])


def serve(tasks, after, name, places):
    arrays, specs = [], []
    for task in tasks:
        for parts in task["sides"]:
            for array, starts, sizes in parts:
                index = tuple(
                    start // size if isinstance(start, int) else start
                    for start, size in zip(starts, sizes, strict=True)
                )

                def where(_, ref, index=index):
                    return tuple(i if isinstance(i, int) else ref[i[0]] for i in index)

                arrays.append(array)
                specs.append(pl.BlockSpec(tuple(sizes), where))
    outs = [out for task in tasks for out in task["outs"]]
    moved = sum(2 * int(np.prod(spec.block_shape)) for spec in specs)
    return pl.pallas_call(
        functools.partial(serve_kernel, tasks),
        grid_spec=pltpu.PrefetchScalarGridSpec(
            num_scalar_prefetch=1,
            grid=(1,),
            in_specs=specs + [pl.BlockSpec(memory_space=pl.ANY)] * len(after),
            out_specs=[
                pl.BlockSpec(out.shape, lambda _, ref, n=len(out.shape): (0,) * n) for out in outs
            ],
        ),
        out_shape=outs,
        compiler_params=params(),
        cost_estimate=cost(moved, 2 * moved),
        name=name,
    )(places, *arrays, *after)


def emit_low(values, outs):
    for value, out in zip(values, outs, strict=True):
        out[...] = value.astype(BF)


def place_table():
    own = [lax.axis_index("ty"), lax.axis_index("tx") // 2]
    batch = lax.axis_size("batch")
    own += [(lax.axis_index("batch") >> bit) % 2 for bit in range(batch.bit_length() - 1)]
    return jnp.stack([v for place in own for v in (place, 1 - place)]).astype(jnp.int32)


class Sum:
    def __init__(self, grads, units, inner, columns, table):
        batch = lax.axis_size("batch")
        bits = batch.bit_length() - 1
        rows = sum(grad.size for grad in grads) // (units * columns)
        self.own = rows // lax.axis_size(ALL) // inner
        self.columns = columns
        self.table = table
        self.dims = [units] + [2] * bits + [2, 2, 2, inner, self.own, columns]
        self.moves = {"y": bits + 1, "x": bits + 2, "c": bits + 3}
        self.places = {"y": (0, 1), "x": (2, 3)}
        self.links = {"y": ("ty", 1), "x": ("tx", 2), "c": ("tx", 1)}
        for bit in range(bits):
            self.moves[bit] = bits - bit
            self.places[bit] = (4 + 2 * bit, 5 + 2 * bit)
            self.links[bit] = ("batch", 1 << bit)
        self.cut = 0 if units > 1 else len(self.dims) - 3
        self.half = self.dims[self.cut] // 2
        tail = list(range(bits))
        self.orders = [["x", "y"] + tail, ["y", "x"] + tail]
        at = self.moves["c"]
        if len(grads) == 1:
            grad = grads[0].reshape(self.dims)
            core = lax.axis_index("tx") % 2
            keep = lax.dynamic_slice_in_dim(grad, core, 1, at)
            send = lax.dynamic_slice_in_dim(grad, 1 - core, 1, at)
        else:
            halved = list(self.dims)
            halved[at] = 1
            keep, send = grads[0].reshape(halved), grads[1].reshape(halved)
        self.sent = [send]
        received = swap(send, *self.links["c"])
        self.parts = [[(keep, ("c",)), (received, ("c",))] for _ in range(2)]
        self.done = [["c"], ["c"]]

    def pick(self, part, chosen, side):
        array, fixed = part
        starts, sizes = [0] * array.ndim, list(array.shape)
        for move, where in chosen.items():
            if move not in fixed:
                starts[self.moves[move]] = where
                sizes[self.moves[move]] = 1
        if "side" not in fixed:
            starts[self.cut], sizes[self.cut] = side * self.half, self.half
        return array, starts, sizes

    def task(self):
        if self.orders[0][0] == self.orders[1][0]:
            return self.joint_task()
        sides, outs = [], []
        for side in range(2):
            move = self.orders[side][0]
            chosen = {m: self.places[m][:1] for m in self.done[side] if m != "c"}
            chosen[move] = self.places[move][1:]
            parts = [self.pick(part, chosen, side) for part in self.parts[side]]
            sides.append(parts)
            outs.append(sds(tuple(parts[0][2]), BF))
        return {"sides": sides, "outs": outs, "emit": emit_low}

    def joint_task(self):
        move = self.orders[0][0]
        sides = []
        for side in range(2):
            chosen = {m: self.places[m][:1] for m in self.done[side] if m != "c"}
            chosen[move] = self.places[move][1:]
            sides.append([self.pick(part, chosen, side) for part in self.parts[side]])
        shape = list(sides[0][0][2])
        shape[self.cut] = 2 * self.half
        cut, half = self.cut, self.half

        def emit(values, outs):
            for side in range(2):
                index = [slice(None)] * len(shape)
                index[cut] = slice(side * half, (side + 1) * half)
                outs[0][tuple(index)] = values[side].astype(BF)

        return {"sides": sides, "outs": [sds(tuple(shape), BF)], "emit": emit}

    def accept(self, sent):
        if len(sent) == 1:
            move = self.orders[0][0]
            received = swap(sent[0], *self.links[move])
            for side in range(2):
                self.orders[side].pop(0)
                self.done[side].append(move)
                self.parts[side].append((received, tuple(self.done[side])))
            return
        for side in range(2):
            move = self.orders[side].pop(0)
            self.done[side].append(move)
            received = swap(sent[side], *self.links[move])
            self.parts[side].append((received, ("side",) + tuple(self.done[side])))

    def last_task(self, layout):
        sides = []
        for side in range(2):
            chosen = {m: self.places[m][:1] for m in self.done[side] if m != "c"}
            sides.append([self.pick(part, chosen, side) for part in self.parts[side]])
        shapes, units = layout
        own, columns, half = self.own, self.columns, self.half

        def emit(values, outs):
            for side in range(2):
                value = values[side].reshape(half, own, columns)
                for k in range(half):
                    out, row, col = units[side * half + k]
                    outs[out][
                        row * own : (row + 1) * own, col * columns : (col + 1) * columns
                    ] = value[k]

        outs = [sds((r * own, c * columns), F32) for r, c in shapes]
        return {"sides": sides, "outs": outs, "emit": emit}


def run_tasks(sums, after, name):
    places = sums[0][0].table
    tasks = []
    for sum_, layout in sums:
        tasks.append(sum_.task() if sum_.orders[0] else sum_.last_task(layout))
    outs = serve(tasks, after, name, places)
    results, at = [], 0
    for (sum_, _), task in zip(sums, tasks, strict=True):
        got = outs[at : at + len(task["outs"])]
        at += len(task["outs"])
        if sum_.orders[0]:
            sum_.accept(got)
        else:
            results.append(got)
    return outs, results


def conv_map():
    table = np.zeros((9, 9, 4, 4), np.float32)
    for row_off in range(3):
        for col_off in range(3):
            for p in range(4):
                for q in range(4):
                    i = 2 * (row_off - 1) + p // 2 - q // 2 + 1
                    j = 2 * (col_off - 1) + p % 2 - q % 2 + 1
                    if 0 <= i < 3 and 0 <= j < 3:
                        table[i * 3 + j, row_off * 3 + col_off, p, q] = 1.0
    return table


def conv_lanes(share):
    table = conv_map().transpose(1, 0, 2, 3)
    wide = np.kron(np.eye(share, dtype=np.float32), np.ones((16, 16), np.float32))
    small = np.repeat(np.repeat(table, 4, 2), 4, 3)
    return np.tile(small, (1, 1, share, share)) * wide


def per_device(
    tokens,
    skip_tokens,
    extra_tokens,
    extra_skip,
    timesteps,
    target,
    w_skip,
    b_skip,
    norm1_gain,
    norm1_shift,
    w_qkv,
    w_out,
    b_out,
    norm2_gain,
    norm2_shift,
    w_up,
    b_up,
    w_down,
    b_down,
    final_gain,
    final_shift,
    w_head,
    b_head,
    w_conv,
    b_conv,
):
    items, rows, cols, width = tokens.shape
    hidden_units = w_up.shape[1]
    local = rows * cols
    patch_values = w_head.shape[1]
    chans = w_conv.shape[3]
    devices = lax.axis_size(ALL)
    groups = lax.axis_size(PLANE)
    place = lax.axis_index(PLANE)
    share = items // groups
    per_item = groups * local
    count = share * per_item
    head_dim = width // HEADS
    height, breadth = rows * PATCH, cols * PATCH

    def row(vector):
        return vector.astype(F32).reshape(1, -1)

    def to_items(array):
        return lax.all_to_all(array, PLANE, split_axis=0, concat_axis=0, tiled=True)

    some = 8
    joined_rows = 2 * local + 8
    tile_block = pl.BlockSpec((some, rows, cols, width), lambda i: (i, 0, 0, 0))
    flat_block = pl.BlockSpec((some, local, width), lambda i: (i, 0, 0))
    hidden0, joined = pl.pallas_call(
        merge_kernel,
        grid=(items // some,),
        in_specs=[tile_block, tile_block, whole((2 * width, width)), whole((width,))],
        out_specs=[flat_block, pl.BlockSpec((some, joined_rows, width), lambda i: (i, 0, 0))],
        out_shape=[sds((items, local, width), BF), sds((items, joined_rows, width), BF)],
        compiler_params=params(),
        cost_estimate=cost(items * local * 4 * width * width, 11e6),
        name="merge",
    )(tokens, skip_tokens, w_skip, b_skip)
    hidden0 = to_items(hidden0)
    hidden0 = hidden0.reshape(groups, share, local, width)
    target_patches = (
        target.reshape(items, rows, PATCH, cols, PATCH, chans)
        .transpose(0, 1, 3, 2, 4, 5)
        .reshape(items, local * patch_values)
    )
    high = lax.reduce_precision(target_patches, 8, 7)
    middle = lax.reduce_precision(target_patches - high, 8, 7)
    low = target_patches - high - middle
    thirds = jnp.concatenate([high, middle, low], 1).astype(BF).reshape(items, -1, width)
    joined = lax.dynamic_update_slice(joined, thirds, (0, 2 * local, 0))

    start = place * share
    joined_extra = jnp.concatenate(
        [
            lax.dynamic_slice_in_dim(extra_tokens, start, share, 0),
            lax.dynamic_slice_in_dim(extra_skip, start, share, 0),
        ],
        2,
    )
    extra_rows = share * EXTRA_PAD
    joined_extra = jnp.pad(joined_extra, ((0, 0), (0, EXTRA_PAD - 2), (0, 0)))
    joined_extra = joined_extra.reshape(extra_rows, 2 * width)
    hidden_extra = dot(joined_extra, w_skip, 1, 0) + row(b_skip)
    unit_extra, _ = norm_parts(hidden_extra)
    normed_extra = (unit_extra * row(norm1_gain) + row(norm1_shift)).astype(BF)
    pairs_extra = dot(normed_extra, w_qkv[:, width:], 1, 0).astype(BF)

    def by_head(block):
        return block.reshape(share, EXTRA_PAD, HEADS, head_dim).transpose(0, 2, 1, 3)

    key_extra = by_head(pairs_extra[:, :width])
    value_extra = by_head(pairs_extra[:, width:])

    weight = lax.dynamic_slice_in_dim(noise_weight(timesteps), start, share, 0)
    lanes = share * patch_values
    spread = jnp.tile(w_conv.reshape(9, chans, chans), (1, lanes // chans, lanes // chans))
    kernel = jnp.sum(jnp.asarray(conv_lanes(share)) * spread[None].astype(F32), 1).astype(BF)
    lane_rows = jnp.concatenate(
        [
            jnp.tile(b_head.astype(F32), share),
            jnp.tile(b_conv.astype(F32), lanes // chans),
            jnp.repeat(weight, patch_values),
        ]
    ).reshape(3, lanes)
    joined = lax.optimization_barrier(
        (joined, key_extra, value_extra, kernel, lane_rows, normed_extra)
    )[0]
    joined = to_items(joined).reshape(groups, share, joined_rows, width)
    thirds = joined[:, :, 2 * local : 2 * local + thirds.shape[1]].astype(F32)
    thirds = thirds.reshape(groups, share, 3, local, patch_values)
    target_own = (
        (thirds[:, :, 0] + thirds[:, :, 1] + thirds[:, :, 2])
        .transpose(0, 2, 1, 3)
        .reshape(per_item, share * patch_values)
    )

    vec = whole((width,))
    item_block = pl.BlockSpec((groups, 1, local, width), lambda i: (0, i, 0, 0))

    def per_share(*shape):
        return pl.BlockSpec((1,) + shape, lambda i: (i,) + (0,) * len(shape))

    normed1, qkv, probs, probs_extra, mixed, hidden1 = pl.pallas_call(
        attend_kernel,
        grid=(share,),
        in_specs=[
            item_block,
            per_share(HEADS, EXTRA_PAD, head_dim),
            per_share(HEADS, EXTRA_PAD, head_dim),
            vec,
            vec,
            vec,
            whole((width, 3 * width)),
            whole((width, width)),
        ],
        out_specs=[
            per_share(per_item, width),
            per_share(3 * width, per_item),
            per_share(HEADS, per_item, per_item),
            per_share(HEADS, EXTRA_PAD, per_item),
            per_share(width, per_item),
            per_share(per_item, width),
        ],
        out_shape=[
            sds((share, per_item, width), BF),
            sds((share, 3 * width, per_item), BF),
            sds((share, HEADS, per_item, per_item), BF),
            sds((share, HEADS, EXTRA_PAD, per_item), BF),
            sds((share, width, per_item), BF),
            sds((share, per_item, width), F32),
        ],
        scratch_shapes=[
            pltpu.VMEM((HEADS, per_item, per_item), F32),
            pltpu.VMEM((HEADS, EXTRA_PAD, per_item), F32),
        ],
        compiler_params=params(),
        cost_estimate=cost(count * (8 * width * width + 16 * per_item * width), 25e6, 3e6),
        name="attend",
    )(
        hidden0,
        key_extra,
        value_extra,
        norm1_gain,
        norm1_shift,
        b_out,
        w_qkv,
        w_out,
    )
    hidden1 = hidden1.reshape(count, width)

    chunk = width
    chunks = hidden_units // chunk
    by_col = pl.BlockSpec((1, count, chunk), lambda j: (j, 0, 0))
    active, slope, normed2, hidden2 = pl.pallas_call(
        forward_kernel,
        grid=(chunks,),
        in_specs=[
            whole((count, width)),
            vec,
            vec,
            whole((hidden_units,)),
            vec,
            pl.BlockSpec((width, chunk), lambda j: (0, j)),
            pl.BlockSpec((chunk, width), lambda j: (j, 0)),
        ],
        out_specs=[by_col, by_col, whole((count, width)), whole((count, width))],
        out_shape=[
            sds((chunks, count, chunk), BF),
            sds((chunks, count, chunk), BF),
            sds((count, width), BF),
            sds((count, width), F32),
        ],
        scratch_shapes=[pltpu.VMEM((chunks, chunk), F32)],
        compiler_params=params(),
        cost_estimate=cost(count * 4 * width * hidden_units, 25e6, 5e6),
        name="forward",
    )(hidden1, norm2_gain, norm2_shift, b_up, b_down, w_up, w_down)
    (
        result,
        grad_hidden2,
        grad_down,
        grad_head,
        sums_final,
        head_sum,
        conv_sum,
        conv_bias,
    ) = pl.pallas_call(
        functools.partial(turn_kernel, rows, cols, lax.axis_size("tx")),
        grid=(1,),
        in_specs=[
            whole((count, width)),
            vec,
            vec,
            whole((patch_values, width)),
            whole((9, lanes, lanes)),
            whole((3, lanes)),
            whole((per_item, lanes)),
            pl.BlockSpec(memory_space=pl.ANY),
        ],
        out_specs=[
            whole((per_item, lanes)),
            whole((count, width)),
            whole((count, width)),
            whole((1, lanes)),
            whole((8, width)),
            whole((share, lanes, width)),
            whole((9, lanes, lanes)),
            whole((1, lanes)),
        ],
        out_shape=[
            sds((per_item, lanes), BF),
            sds((count, width), F32),
            sds((count, width), BF),
            sds((1, lanes), F32),
            sds((8, width), F32),
            sds((share, lanes, width), F32),
            sds((9, lanes, lanes), F32),
            sds((1, lanes), F32),
        ],
        scratch_shapes=[pltpu.VMEM((count, width), F32)],
        compiler_params=params(),
        cost_estimate=cost(1e9, 10e6),
        name="turn",
    )(
        hidden2,
        final_gain,
        final_shift,
        w_head.T,
        kernel,
        lane_rows,
        target_own,
        joined,
    )

    any_place = pl.BlockSpec(memory_space=pl.ANY)
    table = place_table()
    core = lax.axis_index("tx") % 2
    core = core.astype(jnp.int32).reshape(1)
    core_spec = pl.BlockSpec(memory_space=pltpu.SMEM)

    def split_outs(units, rows, block_rows, own, cols, index):
        if can_split(own):
            spec = pl.BlockSpec(
                (units, block_rows // (2 * own), own, cols), lambda j: index(j) + (0, 0)
            )
            return spec, lambda n: sds((n, rows // (2 * own), own, cols), BF), 2
        spec = pl.BlockSpec((units, block_rows, cols), lambda j: index(j) + (0,))
        return spec, lambda n: sds((n, rows, cols), BF), 1

    own = width // devices
    half = width // 2
    units = 2 * chunks + 2
    chain_down = CHAIN_DOWN and can_split(own)
    if chain_down:
        down_specs = [
            pl.BlockSpec((8, chunk // (8 * own), own, half), lambda j: (0, j, 0, 0))
        ] * 2
        down_shapes = [sds((8, width // (2 * own), own, half), BF)] * 2
    else:
        down_specs = [pl.BlockSpec((chunk, width), lambda j: (j, 0))]
        down_shapes = [sds((hidden_units, width), BF)]
    grad_w_down = pl.pallas_call(
        functools.partial(down_kernel, own, chain_down),
        grid=(chunks,),
        in_specs=[by_col, whole((count, width)), core_spec],
        out_specs=down_specs,
        out_shape=down_shapes,
        compiler_params=params(),
        cost_estimate=cost(count * 2 * width * hidden_units, 11e6),
        name="down_weight",
    )(active, grad_down, core)
    if chain_down:
        sum_down = Sum(grad_w_down, 8, 1, half, table)
    else:
        out_down = lax.psum_scatter(
            grad_w_down[0], ALL, scatter_dimension=0, tiled=True
        ).astype(F32)

    up_spec, up_shape, up_outs = split_outs(2, width, width, own, half, lambda j: (j, 0))

    def held_col(j):
        return jnp.minimum(j, chunks - 1)

    grad_b_up, grad_hidden1, grad_branch, sums_up, *grad_w_up = pl.pallas_call(
        functools.partial(up_kernel, own),
        grid=(chunks + 1,),
        in_specs=[
            pl.BlockSpec((1, count, chunk), lambda j: (held_col(j), 0, 0)),
            whole((count, width)),
            pl.BlockSpec((chunk, width), lambda j: (held_col(j), 0)),
            pl.BlockSpec((width, chunk), lambda j: (0, held_col(j))),
            whole((count, width)),
            whole((count, width)),
            vec,
            whole((count, width)),
            whole((share, width, per_item)),
            core_spec,
        ]
        + [any_place] * len(grad_w_down),
        out_specs=[
            pl.BlockSpec((1, 8, chunk), lambda j: (held_col(j), 0, 0)),
            whole((count, width)),
            whole((count, width)),
            whole((8, width)),
        ]
        + [up_spec] * up_outs,
        out_shape=[
            sds((chunks, 8, chunk), F32),
            sds((count, width), F32),
            sds((count, width), BF),
            sds((8, width), F32),
        ]
        + [up_shape(units)] * up_outs,
        scratch_shapes=[pltpu.VMEM((count, width), F32)],
        compiler_params=params(),
        cost_estimate=cost(count * (6 * hidden_units + 2 * width) * width, 25e6),
        name="up_weight",
    )(
        slope,
        grad_down,
        w_down,
        w_up,
        normed2,
        hidden1,
        norm2_gain,
        grad_hidden2,
        mixed,
        core,
        *grad_w_down,
    )
    if can_split(own):
        sum_up = Sum(grad_w_up, units, 1, half, table)
    down_layout = ([(4, 2)], [(0, k // 2, k % 2) for k in range(8)])
    up_layout = (
        [(1, 2 * chunks), (1, 2)],
        [(0, 0, k) for k in range(2 * chunks)] + [(1, 0, 0), (1, 0, 1)],
    )
    late_layout = (
        [(1, 6), (2, 2)],
        [(0, 0, k) for k in range(6)] + [(1, 0, 0), (1, 1, 0), (1, 0, 1), (1, 1, 1)],
    )

    after = sum_up.sent if can_split(own) else []
    if chain_down:
        after, _ = run_tasks([(sum_down, None)], after, "serve_0")
        early = [(sum_down, None)]
    else:
        early = []
    grad_qkv, grad_key_extra, grad_value_extra = [], [], []
    sums_attend = jnp.zeros((8, width), F32)
    grad_hidden0 = None
    back_rows = share * local + 16
    for first, number in ((0, share - 1), (share - 1, 1)):

        def one(*shape, first=first):
            return pl.BlockSpec((1,) + shape, lambda i: (first + i,) + (0,) * len(shape))

        def own_item(*shape):
            return pl.BlockSpec((1,) + shape, lambda i: (i,) + (0,) * len(shape))

        held = [grad_hidden0] if first else []
        outs = pl.pallas_call(
            attend_back_kernel,
            grid=(number,),
            in_specs=[
                pl.BlockSpec(
                    (groups, 1, local, width), lambda i, first=first: (0, first + i, 0, 0)
                ),
                one(per_item, width),
                one(per_item, width),
                one(3 * width, per_item),
                one(HEADS, per_item, per_item),
                one(HEADS, EXTRA_PAD, per_item),
                one(HEADS, EXTRA_PAD, head_dim),
                one(HEADS, EXTRA_PAD, head_dim),
                vec,
                whole((width, 3 * width)),
                whole((width, width)),
                whole((8, width)),
            ]
            + [any_place] * (len(held) + len(after)),
            out_specs=[
                own_item(3 * width, per_item),
                own_item(HEADS, EXTRA_PAD, head_dim),
                own_item(HEADS, EXTRA_PAD, head_dim),
                pl.BlockSpec((groups, local, width), lambda i, first=first: (0, first + i, 0)),
                whole((8, width)),
            ],
            out_shape=[
                sds((number, 3 * width, per_item), BF),
                sds((number, HEADS, EXTRA_PAD, head_dim), F32),
                sds((number, HEADS, EXTRA_PAD, head_dim), F32),
                sds((groups, back_rows, width), BF),
                sds((8, width), F32),
            ],
            input_output_aliases={12: 3} if first else {},
            scratch_shapes=[
                pltpu.VMEM((width, per_item), BF),
                pltpu.VMEM((HEADS, per_item, per_item), F32),
                pltpu.VMEM((HEADS, EXTRA_PAD, per_item), F32),
                pltpu.VMEM((HEADS, per_item, per_item), BF),
                pltpu.VMEM((HEADS, EXTRA_PAD, per_item), BF),
            ],
            compiler_params=params(),
            cost_estimate=cost(
                per_item * (8 * width * width + 40 * per_item * width), 12e6
            ),
            name="attend_back",
        )(
            hidden0,
            grad_hidden1.reshape(share, per_item, width),
            grad_branch.reshape(share, per_item, width),
            qkv,
            probs,
            probs_extra,
            key_extra,
            value_extra,
            norm1_gain,
            w_qkv,
            w_out,
            sums_attend,
            *held,
            *after,
        )
        grad_qkv += [outs[0]] * number
        grad_key_extra += [outs[1]] * number
        grad_value_extra += [outs[2]] * number
        grad_hidden0, sums_attend = outs[3], outs[4]
        after = []
        if can_split(own) and not first:
            after, _ = run_tasks([(sum_up, None)] + early, [sums_attend], "serve_1")
    places_of = [i for number in (share - 1, 1) for i in range(number)]

    latent = result.reshape(groups, local * share * patch_values // width, width)
    pairs_extra, grad_extra, sums_attend, grad_back = pl.pallas_call(
        functools.partial(extra_back_kernel, share),
        grid=(1,),
        in_specs=[
            whole((extra_rows, width)),
            vec,
            pl.BlockSpec((width, width), lambda *_: (0, 1)),
            pl.BlockSpec((width, width), lambda *_: (0, 2)),
            whole(latent.shape),
            whole((8, width)),
        ]
        + [
            pl.BlockSpec((1, HEADS, EXTRA_PAD, head_dim), lambda *_, at=at: (at, 0, 0, 0))
            for at in places_of * 2
        ]
        + [any_place] * (1 + len(after)),
        out_specs=[
            whole((2, extra_rows, width)),
            whole((extra_rows, width)),
            whole((8, width)),
            pl.BlockSpec((groups, 16, width), lambda *_: (0, share * local // 16, 0)),
        ],
        out_shape=[
            sds((2, extra_rows, width), BF),
            sds((extra_rows, width), BF),
            sds((8, width), F32),
            sds((groups, back_rows, width), BF),
        ],
        input_output_aliases={6 + 2 * share: 3},
        compiler_params=params(),
        cost_estimate=cost(1e8, 5e6),
        name="extra_back",
    )(
        hidden_extra,
        norm1_gain,
        w_qkv,
        w_qkv,
        latent,
        sums_attend,
        *grad_key_extra,
        *grad_value_extra,
        grad_hidden0,
        *after,
    )

    late_spec, late_shape, late_outs = split_outs(
        2, width, width, own, width // 2, lambda j: (j, 0)
    )

    def skip_col(j):
        return jnp.maximum(j - 3, 0)

    def qkv_row(j):
        return jnp.minimum(j, 2)

    half = width // 2
    grad_late = pl.pallas_call(
        functools.partial(late_weight_kernel, own),
        grid=(5,),
        in_specs=[
            whole((share, per_item, width)),
            whole((extra_rows, width)),
            pl.BlockSpec(
                (1, extra_rows, width), lambda j: (jnp.clip(j - 1, 0, 1), 0, 0)
            ),
            whole(joined.shape),
            pl.BlockSpec((groups, back_rows, half), lambda j: (0, 0, skip_col(j))),
            whole((extra_rows, 2 * width)),
            pl.BlockSpec((extra_rows, half), lambda j: (0, skip_col(j))),
        ]
        + [
            pl.BlockSpec((1, width, per_item), lambda j, at=at: (at, qkv_row(j), 0))
            for at in places_of
        ]
        + [core_spec],
        out_specs=[late_spec] * late_outs,
        out_shape=[late_shape(10)] * late_outs,
        compiler_params=params(),
        cost_estimate=cost(count * 10 * width * width, 12e6),
        name="late_weight",
    )(
        normed1,
        normed_extra,
        pairs_extra,
        joined,
        grad_back,
        joined_extra,
        grad_extra,
        *grad_qkv,
        core,
    )

    def hold(values, *others):
        return lax.optimization_barrier((values, others))[0]

    if can_split(own):
        after, _ = run_tasks([(sum_up, None)] + early, [grad_late[0]], "serve_2")
        grad_late = [grad_late[0], hold(grad_late[1], after)]
        sum_late = Sum(grad_late, 10, 1, half, table)
    else:
        after = list(grad_late)

    stacked_count = 9 + patch_values
    stacked, shared = pl.pallas_call(
        pack_kernel,
        in_specs=[pl.BlockSpec(memory_space=pltpu.VMEM)] * 8 + [any_place] * len(after),
        out_specs=[pl.BlockSpec(memory_space=pltpu.VMEM)] * 2,
        out_shape=[sds((stacked_count, width), F32), sds((8, 128), F32)],
        compiler_params=params(),
        cost_estimate=cost(1e6, 1e6),
        name="pack",
    )(
        sums_attend,
        sums_up,
        sums_final,
        head_sum,
        grad_head,
        conv_sum,
        conv_bias,
        jnp.asarray(conv_lanes(share), BF),
        *after,
    )
    packed = jnp.concatenate(
        [
            stacked.reshape(stacked_count, devices, own).transpose(1, 0, 2).reshape(devices, -1),
            grad_b_up[:, 0].reshape(devices, -1),
            jnp.broadcast_to(shared[:4].reshape(1, -1), (devices, 512)),
        ],
        1,
    )
    packed_size = packed.shape[1]
    packed = jnp.pad(packed, ((0, 0), (0, (-packed.shape[1]) % 128)))
    if not can_split(own):
        wide = grad_w_up[0].transpose(1, 0, 2).reshape(width, -1)
        wide = lax.psum_scatter(wide, ALL, scatter_dimension=0, tiled=True).astype(F32)
        out_up, out_out = wide[:, :hidden_units], wide[:, hidden_units:]
        wide = grad_late[0][:6].transpose(1, 0, 2).reshape(width, -1)
        out_qkv = lax.psum_scatter(wide, ALL, scatter_dimension=0, tiled=True).astype(F32)
        tall = grad_late[0][6:].reshape(2, 2, width, half).transpose(1, 2, 0, 3)
        tall = tall.reshape(2 * width, width)
        out_skip = lax.psum_scatter(tall, ALL, scatter_dimension=0, tiled=True).astype(F32)
    else:
        after, _ = run_tasks([(sum_late, None), (sum_up, None)] + early, [packed], "serve_5")
    exchanged = lax.all_to_all(hold(packed, after), ALL, split_axis=0, concat_axis=0, tiled=True)
    if can_split(own):
        if chain_down:
            early = [(sum_down, down_layout)]
        after, results = run_tasks(
            [(sum_late, None), (sum_up, None)] + early, [exchanged], "serve_6"
        )
        if chain_down:
            out_down = results[0][0]
        after, results = run_tasks([(sum_late, None), (sum_up, up_layout)], after, "serve_7")
        out_up, out_out = results[0]
    back = to_items(hold(grad_back, after))
    if can_split(own):
        while sum_late.orders[0]:
            after, _ = run_tasks([(sum_late, None)], after, "serve_8")
    some_groups = max(groups // 2, 1)
    token_block = pl.BlockSpec(
        (some_groups * share, rows, cols, width), lambda i: (i, 0, 0, 0)
    )
    grad_tokens, grad_skip_tokens, grad_extra_all = pl.pallas_call(
        token_kernel,
        grid=(groups // some_groups,),
        in_specs=[
            pl.BlockSpec((some_groups, back_rows, width), lambda i: (i, 0, 0)),
            whole((2 * width, width)),
        ],
        out_specs=[
            token_block,
            token_block,
            pl.BlockSpec((some_groups, 16, 2 * width), lambda i: (i, 0, 0)),
        ],
        out_shape=[sds(tokens.shape, BF)] * 2 + [sds((groups, 16, 2 * width), BF)],
        compiler_params=params(),
        cost_estimate=cost(items * local * 4 * width * width, 8e6),
        name="tokens",
    )(hold(back, after), w_skip)
    summed = jnp.sum(hold(exchanged, after), 0)
    small = [summed[k * own : (k + 1) * own] for k in range(9)]
    own_head = summed[9 * own : stacked_count * own].reshape(patch_values, own).T
    up_low = stacked_count * own
    own_b_up = summed[up_low : up_low + hidden_units // devices]
    shared = summed[up_low + hidden_units // devices : packed_size].reshape(4, 128)

    latent_row = share * local + 2 * share
    latent = back[:, latent_row : latent_row + latent.shape[1]]
    latent_out = (
        hold(latent, after)
        .reshape(groups, rows, cols, share, PATCH, PATCH, chans)
        .transpose(0, 3, 1, 4, 2, 5, 6)
        .reshape(items, height, breadth, chans)
    )
    grad_joined_extra = grad_extra_all[:, : 2 * share].reshape(items, 2, 2 * width)
    if can_split(own):
        _, results = run_tasks([(sum_late, late_layout)], [grad_tokens, latent_out], "serve_9")
        out_qkv, out_skip = results[0]
    return (
        latent_out,
        grad_tokens,
        grad_skip_tokens,
        grad_joined_extra[..., :width],
        grad_joined_extra[..., width:],
        out_skip,
        small[0],
        small[1],
        small[2],
        out_qkv,
        out_out,
        small[3],
        small[4],
        small[5],
        out_up,
        own_b_up,
        out_down,
        small[6],
        small[7],
        small[8],
        own_head,
        shared[0, 64 : 64 + patch_values],
        shared[:, : 9 * chans].reshape(chans, 3, 3, chans).transpose(1, 2, 0, 3),
        shared[0, 96 : 96 + chans],
    )


def solution(mesh):
    tiles = P("batch", "ty", "tx", None)
    pairs = P("batch", None, None)
    matrix = P(ALL, None)
    vector = P(ALL)
    return jax.shard_map(
        per_device,
        mesh=mesh,
        in_specs=(tiles, tiles, pairs, pairs, P("batch"), tiles) + (P(),) * 19,
        out_specs=(
            tiles,
            tiles,
            tiles,
            pairs,
            pairs,
            matrix,
            vector,
            vector,
            vector,
            matrix,
            matrix,
            vector,
            vector,
            vector,
            matrix,
            vector,
            matrix,
            vector,
            vector,
            vector,
            matrix,
            P(),
            P(),
            P(),
        ),
        check_vma=False,
    )
```

```python
import functools

import jax
import jax.numpy as jnp
import numpy as np
from jax import lax
from jax.experimental import pallas as pl
from jax.experimental.pallas import tpu as pltpu
from jax.sharding import PartitionSpec as P

HEADS = 12
PATCH = 2
EXTRA_PAD = 8
CHAIN_DOWN = True
EPS = 1e-05
BF = jnp.bfloat16
F32 = jnp.float32
PLANE = ("ty", "tx")
ALL = ("batch", "ty", "tx")
MIB = 1024 * 1024


def dot(left, right, left_dim, right_dim):
    return lax.dot_general(
        left, right, (((left_dim,), (right_dim,)), ((), ())), preferred_element_type=F32
    )


def norm_parts(values):
    center = values - jnp.mean(values, -1, keepdims=True)
    scaled = lax.rsqrt(jnp.mean(center * center, -1, keepdims=True) + EPS)
    return center * scaled, scaled


def norm_back(inner, normed, scaled):
    return scaled * (
        inner
        - jnp.mean(inner, -1, keepdims=True)
        - normed * jnp.mean(inner * normed, -1, keepdims=True)
    )


def flat(ref):
    return ref[...].astype(F32).reshape(1, -1)


def row_sum(values):
    return jnp.sum(values, 0, keepdims=True)


def gelu_parts(upper):
    spread = 0.5 + 0.5 * lax.erf(upper * np.float32(0.5**0.5))
    bell = jnp.exp(upper * upper * -0.5) * np.float32((2 * np.pi) ** -0.5)
    return upper * spread, spread + upper * bell


def noise_weight(timesteps):
    frac = (timesteps.astype(F32) / 1000.0 + 0.008) / 1.008
    kept = jnp.cos(frac * (0.5 * jnp.pi)) ** 2
    return jnp.minimum(1.0, 5.0 * (1.0 - kept) / kept)


def can_split(own):
    return own % 8 == 0


def store_split(value, own, lane_refs):
    if len(lane_refs) == 1:
        lane_refs[0][...] = value.astype(BF)
        return
    keep_ref, send_ref, core_ref = lane_refs
    pairs = value.reshape(value.shape[0] // (2 * own), 2, own, value.shape[1])
    first = core_ref[0] == 0
    keep = jnp.where(first, pairs[:, 0], pairs[:, 1])
    send = jnp.where(first, pairs[:, 1], pairs[:, 0])
    keep_ref[...] = keep.astype(BF)
    send_ref[...] = send.astype(BF)


def merge_kernel(tokens_ref, skip_ref, w_skip_ref, b_skip_ref, hidden_ref, joined_ref):
    width = w_skip_ref.shape[1]
    local = tokens_ref.shape[1] * tokens_ref.shape[2]
    body = tokens_ref[...].reshape(-1, width)
    body_skip = skip_ref[...].reshape(-1, width)
    hidden = (
        dot(body, w_skip_ref[:width], 1, 0)
        + dot(body_skip, w_skip_ref[width:], 1, 0)
        + b_skip_ref[...].astype(F32).reshape(1, width)
    )
    hidden_ref[...] = hidden.astype(BF).reshape(-1, local, width)
    joined_ref[:, :local] = body.reshape(-1, local, width)
    joined_ref[:, local : 2 * local] = body_skip.reshape(-1, local, width)


def attend_kernel(
    hidden_ref,
    key_extra_ref,
    value_extra_ref,
    gain_ref,
    shift_ref,
    b_out_ref,
    w_qkv_ref,
    w_out_ref,
    normed_ref,
    qkv_ref,
    probs_ref,
    probs_extra_ref,
    mixed_ref,
    hidden1_ref,
    scores_ref,
    scores_extra_ref,
):
    width = w_out_ref.shape[0]
    head_dim = width // HEADS
    scale = head_dim ** (-0.5)
    rows = hidden_ref.shape[0] * hidden_ref.shape[2]
    hidden = hidden_ref[...].reshape(rows, width).astype(F32)
    unit, _ = norm_parts(hidden)
    normed = (unit * flat(gain_ref) + flat(shift_ref)).astype(BF)
    normed_ref[0] = normed
    qkv_ref[0] = dot(w_qkv_ref[...], normed, 0, 1).astype(BF)
    live = lax.broadcasted_iota(jnp.int32, (EXTRA_PAD, rows), 0) < 2
    for head in range(HEADS):
        low = head * head_dim
        query = qkv_ref[0, low : low + head_dim, :]
        key = qkv_ref[0, width + low : width + low + head_dim, :]
        scores_ref[head] = dot(key, query, 0, 0) * scale
        scores_extra = dot(key_extra_ref[0, head], query, 1, 0) * scale
        scores_extra_ref[head] = jnp.where(live, scores_extra, -1e30)
    for head in range(HEADS):
        scores, scores_extra = scores_ref[head], scores_extra_ref[head]
        top = jnp.maximum(
            jnp.max(scores, 0, keepdims=True), jnp.max(scores_extra, 0, keepdims=True)
        )
        raised = jnp.exp(scores - top)
        raised_extra = jnp.exp(scores_extra - top)
        share = 1.0 / (row_sum(raised) + row_sum(raised_extra))
        probs_ref[0, head] = (raised * share).astype(BF)
        probs_extra_ref[0, head] = (raised_extra * share).astype(BF)
    for head in range(HEADS):
        low = head * head_dim
        value = qkv_ref[0, 2 * width + low : 2 * width + low + head_dim, :]
        mixed = dot(value, probs_ref[0, head], 1, 0) + dot(
            value_extra_ref[0, head], probs_extra_ref[0, head], 0, 0
        )
        mixed_ref[0, low : low + head_dim, :] = mixed.astype(BF)
    hidden1_ref[0] = hidden + (dot(mixed_ref[0], w_out_ref[...], 0, 0) + flat(b_out_ref))


def forward_kernel(
    hidden1_ref,
    gain2_ref,
    shift2_ref,
    b_up_ref,
    b_down_ref,
    w_up_ref,
    w_down_ref,
    active_ref,
    slope_ref,
    normed2_ref,
    total,
    up_rows,
):
    step = pl.program_id(0)

    @pl.when(step == 0)
    def _():
        unit, _ = norm_parts(hidden1_ref[...])
        b_up = flat(b_up_ref)
        width = up_rows.shape[1]
        for j in range(up_rows.shape[0]):
            up_rows[j : j + 1] = b_up[:, j * width : (j + 1) * width]
        normed2_ref[...] = (unit * flat(gain2_ref) + flat(shift2_ref)).astype(BF)

    count = normed2_ref.shape[0]
    blocks = 3 if count % 48 == 0 else 1
    size = count // blocks
    rows = [slice(i * size, (i + 1) * size) for i in range(blocks)]

    def raise_rows(i):
        return dot(normed2_ref[rows[i]], w_up_ref[...], 1, 0) + up_rows[pl.ds(step, 1)]

    def activate(upper, i):
        active, slope = gelu_parts(upper)
        active = active.astype(BF)
        active_ref[0, rows[i]] = active
        slope_ref[0, rows[i]] = slope.astype(BF)
        return active

    def lower(active, i):
        part = dot(active, w_down_ref[...], 1, 0)
        base = jnp.where(step == 0, hidden1_ref[rows[i]] + flat(b_down_ref), total[rows[i]])
        total[rows[i]] = base + part

    upper = raise_rows(0)
    for i in range(blocks):
        following = raise_rows(i + 1) if i + 1 < blocks else None
        active = activate(upper, i)
        upper = following
        lower(active, i)


def turn_kernel(
    tile_rows,
    tile_cols,
    tiles_x,
    hidden2_ref,
    gainf_ref,
    shiftf_ref,
    w_head_ref,
    w_conv_ref,
    b_head_ref,
    b_conv_ref,
    weight_ref,
    target_ref,
    after_ref,
    result_ref,
    grad_hidden2_ref,
    grad_down_ref,
    grad_head_ref,
    sums_ref,
    head_sum_ref,
    conv_sum_ref,
    conv_bias_ref,
    total,
):
    per_item, lanes = target_ref.shape
    patch_values, width = w_head_ref.shape
    items = lanes // patch_values

    weight = flat(weight_ref)
    weight_lanes = jnp.concatenate(
        [jnp.broadcast_to(weight[:, i : i + 1], (1, patch_values)) for i in range(items)], 1
    )

    def head_of(i):
        parts = [w_head_ref[...]]
        if i > 0:
            parts = [jnp.zeros((i * patch_values, width), BF)] + parts
        if i < items - 1:
            parts = parts + [jnp.zeros((lanes - (i + 1) * patch_values, width), BF)]
        return jnp.concatenate(parts, 0)

    heads = [head_of(i) for i in range(items)]
    unit, scaled = norm_parts(hidden2_ref[...])
    total[...] = unit
    normedf = (unit * flat(gainf_ref) + flat(shiftf_ref)).astype(BF)
    normed2_final = [normedf[i * per_item : (i + 1) * per_item] for i in range(items)]
    patches = jnp.concatenate([flat(b_head_ref)] * items, 1)
    for i in range(items):
        patches = patches + dot(normed2_final[i], heads[i], 1, 1)
    patches = patches.astype(BF)

    def place(position):
        tile = position // (tile_rows * tile_cols)
        row = (tile // tiles_x) * tile_rows + (position // tile_cols) % tile_rows
        col = (tile % tiles_x) * tile_cols + position % tile_cols
        return row * 1024 + col

    own = place(lax.broadcasted_iota(jnp.int32, (per_item, 1), 0))
    other = place(lax.broadcasted_iota(jnp.int32, (1, per_item), 1))
    shifts = []
    for row_off in range(3):
        for col_off in range(3):
            wanted = own + ((row_off - 1) * 1024 + (col_off - 1))
            shifts.append(jnp.where(wanted == other, 1.0, 0.0).astype(BF))
    windows = [dot(shift, patches, 1, 0).astype(BF) for shift in shifts]
    result = jnp.concatenate([flat(b_conv_ref)] * (lanes // b_conv_ref.shape[0]), 1)
    for k in range(9):
        result = result + dot(windows[k], w_conv_ref[k], 1, 0)
    result_ref[...] = result.astype(BF)
    grad_result = (weight_lanes * (result - target_ref[...])).astype(BF)
    conv_bias_ref[...] = row_sum(grad_result.astype(F32))
    grad_patches = jnp.zeros(target_ref.shape, F32)
    for k in range(9):
        conv_sum_ref[k] = dot(windows[k], grad_result, 0, 0)
        moved = dot(shifts[8 - k], grad_result, 1, 0).astype(BF)
        grad_patches = grad_patches + dot(moved, w_conv_ref[k], 1, 1)
    grad_patches = grad_patches.astype(BF)
    grad_head_ref[...] = row_sum(grad_patches.astype(F32))
    sum_gain = jnp.zeros((1, unit.shape[1]), F32)
    sum_shift = sum_gain
    sum_down = sum_gain
    for i in range(items):
        rows = slice(i * per_item, (i + 1) * per_item)
        head_sum_ref[i] = dot(grad_patches, normed2_final[i], 0, 0)
        grad_normedf = dot(grad_patches, heads[i], 1, 0)
        unit_part = total[rows]
        sum_gain = sum_gain + row_sum(grad_normedf * unit_part)
        sum_shift = sum_shift + row_sum(grad_normedf)
        grad_hidden2 = norm_back(grad_normedf * flat(gainf_ref), unit_part, scaled[rows])
        grad_hidden2_ref[rows] = grad_hidden2
        grad_down = grad_hidden2.astype(BF)
        grad_down_ref[rows] = grad_down
        sum_down = sum_down + row_sum(grad_down.astype(F32))
    sums_ref[0:1] = sum_gain
    sums_ref[1:2] = sum_shift
    sums_ref[2:3] = sum_down


def down_kernel(own, split, active_ref, grad_down_ref, core_ref, *outs):
    total = dot(active_ref[0], grad_down_ref[...], 0, 0)
    if not split:
        outs[0][...] = total.astype(BF)
        return
    pairs = total.reshape(total.shape[0] // (8 * own), 2, 4, own, total.shape[1])
    first = core_ref[0] == 0
    half = total.shape[1] // 2
    for part in range(4):
        low, high = pairs[:, 0, part], pairs[:, 1, part]
        keep = jnp.where(first, low, high).astype(BF)
        send = jnp.where(first, high, low).astype(BF)
        for side in range(2):
            cols = slice(side * half, (side + 1) * half)
            outs[0][2 * part + side] = keep[:, :, cols]
            outs[1][2 * part + side] = send[:, :, cols]


def up_kernel(
    own,
    slope_ref,
    grad_down_ref,
    w_down_ref,
    w_up_ref,
    normed2_ref,
    hidden1_hbm,
    gain2_ref,
    grad_hidden2_hbm,
    mixed_hbm,
    core_ref,
    *rest,
):
    total, hidden1_ref, grad_hidden2_ref, mixed_ref, sems = rest[-5:]
    rest = rest[-11 if can_split(own) else -10 : -5]
    late_copies = [
        pltpu.make_async_copy(hidden1_hbm, hidden1_ref, sems.at[0]),
        pltpu.make_async_copy(grad_hidden2_hbm, grad_hidden2_ref, sems.at[1]),
        pltpu.make_async_copy(mixed_hbm, mixed_ref, sems.at[2]),
    ]

    @pl.when(pl.program_id(0) == 0)
    def _():
        for copy in late_copies:
            copy.start()

    grad_b_up_ref, grad_hidden1_ref, grad_branch_ref, sums_ref = rest[:4]
    rest = rest[4:]
    step = pl.program_id(0)
    steps = pl.num_programs(0)

    def store(value):
        half = value.shape[1] // 2
        for side in range(2):
            piece = value[:, side * half : (side + 1) * half]
            if can_split(own):
                store_split(piece, own, (rest[0].at[side], rest[1].at[side], core_ref))
            else:
                store_split(piece, own, (rest[0].at[side],))

    @pl.when(step < steps - 1)
    def _():
        grad_active = dot(grad_down_ref[...], w_down_ref[...], 1, 1)
        grad_upper = (grad_active * slope_ref[0].astype(F32)).astype(BF)
        grad_b_up_ref[0, 0:1] = row_sum(grad_upper.astype(F32))
        store(dot(normed2_ref[...], grad_upper, 0, 0))
        part = dot(grad_upper, w_up_ref[...], 1, 1)

        @pl.when(step == 0)
        def _():
            total[...] = part

        @pl.when(step > 0)
        def _():
            total[...] += part

    @pl.when(step == steps - 1)
    def _():
        for copy in late_copies:
            copy.wait()
        unit, scaled = norm_parts(hidden1_ref[...])
        grad_normed2 = total[...]
        sums_ref[0:1] = row_sum(grad_normed2 * unit)
        sums_ref[1:2] = row_sum(grad_normed2)
        grad_hidden1 = grad_hidden2_ref[...] + norm_back(
            grad_normed2 * flat(gain2_ref), unit, scaled
        )
        grad_hidden1_ref[...] = grad_hidden1
        grad_branch = grad_hidden1.astype(BF)
        grad_branch_ref[...] = grad_branch
        sums_ref[2:3] = row_sum(grad_branch.astype(F32))
        items, _, per_item = mixed_ref.shape
        value = dot(mixed_ref[0], grad_branch[:per_item], 1, 0)
        for item in range(1, items):
            rows = slice(item * per_item, (item + 1) * per_item)
            value = value + dot(mixed_ref[item], grad_branch[rows], 1, 0)
        store(value)


def attend_back_kernel(
    opening,
    hidden_ref,
    grad_hidden1_ref,
    grad_branch_ref,
    qkv_ref,
    probs_ref,
    probs_extra_ref,
    key_extra_ref,
    value_extra_ref,
    gain_ref,
    w_qkv_hbm,
    w_out_ref,
    sums_in_ref,
    *rest,
):
    (
        grad_qkv_ref,
        grad_key_extra_ref,
        grad_value_extra_ref,
        grad_hidden0_ref,
        sums_ref,
        grad_mixed_ref,
        grad_probs_ref,
        grad_probs_extra_ref,
        grad_scores_ref,
        grad_scores_extra_ref,
        w_qkv_ref,
        sem,
    ) = rest[-12:]
    step = pl.program_id(0)
    late_copy = pltpu.make_async_copy(w_qkv_hbm, w_qkv_ref, sem)

    @pl.when(step == 0)
    def _():
        late_copy.start()

    width = w_out_ref.shape[0]
    head_dim = width // HEADS
    scale = head_dim ** (-0.5)
    rows = hidden_ref.shape[0] * hidden_ref.shape[2]
    grad_mixed_ref[...] = dot(w_out_ref[...], grad_branch_ref[0], 1, 1).astype(BF)
    for head in range(HEADS):
        low = head * head_dim
        value = qkv_ref[0, 2 * width + low : 2 * width + low + head_dim, :]
        grad_mixed = grad_mixed_ref[low : low + head_dim, :]
        grad_probs_ref[head] = dot(value, grad_mixed, 0, 0)
        grad_probs_extra_ref[head] = dot(value_extra_ref[0, head], grad_mixed, 1, 0)
    for head in range(HEADS):
        probs = probs_ref[0, head].astype(F32)
        probs_extra = probs_extra_ref[0, head].astype(F32)
        grad_probs, grad_probs_extra = grad_probs_ref[head], grad_probs_extra_ref[head]
        common = row_sum(grad_probs * probs) + row_sum(grad_probs_extra * probs_extra)
        grad_scores_ref[head] = (probs * (grad_probs - common)).astype(BF)
        grad_scores_extra_ref[head] = (probs_extra * (grad_probs_extra - common)).astype(BF)
    for head in range(HEADS):
        low = head * head_dim
        query = qkv_ref[0, low : low + head_dim, :]
        key = qkv_ref[0, width + low : width + low + head_dim, :]
        grad_mixed = grad_mixed_ref[low : low + head_dim, :]
        grad_scores, grad_scores_extra = grad_scores_ref[head], grad_scores_extra_ref[head]
        grad_query = dot(key, grad_scores, 1, 0) + dot(
            key_extra_ref[0, head], grad_scores_extra, 0, 0
        )
        grad_key = dot(query, grad_scores, 1, 1)
        grad_value = dot(grad_mixed, probs_ref[0, head], 1, 1)
        grad_key_extra_ref[0, head] = dot(grad_scores_extra, query, 1, 1) * scale
        grad_value_extra_ref[0, head] = dot(probs_extra_ref[0, head], grad_mixed, 1, 1)
        grad_qkv_ref[0, low : low + head_dim, :] = (grad_query * scale).astype(BF)
        grad_qkv_ref[0, width + low : width + low + head_dim, :] = (grad_key * scale).astype(BF)
        grad_qkv_ref[0, 2 * width + low : 2 * width + low + head_dim, :] = grad_value.astype(BF)

    @pl.when(step == 0)
    def _():
        late_copy.wait()

    grad_normed = dot(grad_qkv_ref[0], w_qkv_ref[...], 0, 1)
    unit, scaled = norm_parts(hidden_ref[...].reshape(rows, width).astype(F32))

    @pl.when(pl.program_id(0) == 0)
    def _():
        sums_ref[...] = jnp.zeros_like(sums_ref) if opening else sums_in_ref[...]

    sums_ref[0:1] += row_sum(grad_normed * unit)
    sums_ref[1:2] += row_sum(grad_normed)
    grad_hidden0 = grad_hidden1_ref[0] + norm_back(grad_normed * flat(gain_ref), unit, scaled)
    grad_low = grad_hidden0.astype(BF)
    sums_ref[2:3] += row_sum(grad_low.astype(F32))
    grad_hidden0_ref[...] = grad_low.reshape(grad_hidden0_ref.shape)


def extra_back_kernel(
    share,
    hidden_ref,
    gain_ref,
    w_key_ref,
    w_value_ref,
    latent_ref,
    sums_in_ref,
    *rest,
):
    keys, values = rest[:share], rest[share : 2 * share]
    pairs_ref, grad_ref, sums_ref, back_ref = rest[-4:]
    width = hidden_ref.shape[1]

    def rows_of(refs):
        return jnp.concatenate(
            [jnp.concatenate([ref[0, head] for ref in refs], 0) for head in range(HEADS)], 1
        ).astype(BF)

    grad_key, grad_value = rows_of(keys), rows_of(values)
    pairs_ref[0] = grad_key
    pairs_ref[1] = grad_value
    grad_normed = dot(grad_key, w_key_ref[...], 1, 1) + dot(grad_value, w_value_ref[...], 1, 1)
    unit, scaled = norm_parts(hidden_ref[...])
    grad = norm_back(grad_normed * flat(gain_ref), unit, scaled).astype(BF)
    grad_ref[...] = grad
    wide = grad.astype(F32)
    sums_ref[0:1] = sums_in_ref[0:1] + row_sum(grad_normed * unit)
    sums_ref[1:2] = sums_in_ref[1:2] + row_sum(grad_normed)
    sums_ref[2:3] = sums_in_ref[2:3] + row_sum(wide)
    real = [wide[i * EXTRA_PAD : i * EXTRA_PAD + 2] for i in range(share)]
    fill = back_ref.shape[1] - 2 * share - latent_ref.shape[1]
    for group in range(back_ref.shape[0]):
        block = real + [latent_ref[group].astype(F32), jnp.zeros((fill, width), F32)]
        back_ref[group] = jnp.concatenate(block, 0).astype(BF)


def late_weight_kernel(
    own,
    normed_ref,
    normed_extra_ref,
    pairs_ref,
    joined_hbm,
    grad_ref,
    joined_extra_ref,
    grad_extra_ref,
    grad_qkv_0_ref,
    grad_qkv_1_ref,
    grad_qkv_2_ref,
    core_ref,
    *rest,
):
    joined_ref, sem = rest[-2:]
    rest = rest[:-2]
    step = pl.program_id(0)
    split = can_split(own)
    late_copy = pltpu.make_async_copy(joined_hbm, joined_ref, sem)

    @pl.when(step == 0)
    def _():
        late_copy.start()

    @pl.when(step == 3)
    def _():
        late_copy.wait()

    groups, items, _, width = joined_ref.shape
    local = (grad_ref.shape[1] - 16) // items

    @pl.when(step < 3)
    def _():
        total = dot(normed_extra_ref[...], pairs_ref[0], 0, 0)
        total = total * jnp.where(step == 0, 0.0, 1.0)
        for item, ref in enumerate((grad_qkv_0_ref, grad_qkv_1_ref, grad_qkv_2_ref)):
            total = total + dot(normed_ref[item], ref[0], 0, 1)
        half = width // 2
        for side in range(2):
            piece = total[:, side * half : (side + 1) * half]
            if split:
                store_split(piece, own, (rest[-2].at[side], rest[-1].at[side], core_ref))
            else:
                store_split(piece, own, (rest[-1].at[side],))

    @pl.when(step >= 3)
    def _():
        grad = grad_ref[:, : items * local].reshape(groups * items * local, -1)
        for side in range(2):
            joined = joined_ref[:, :, side * local : (side + 1) * local]
            joined = joined.reshape(groups * items * local, width)
            extra = joined_extra_ref[:, side * width : (side + 1) * width]
            total = dot(joined, grad, 0, 0) + dot(extra, grad_extra_ref[...], 0, 0)
            if not split:
                rest[-1][side] = total.astype(BF)
                continue
            pairs = total.reshape(width // (4 * own), 2, 2, own, total.shape[1])
            first = core_ref[0] == 0
            count = pairs.shape[0]
            for part in range(2):
                low, high = pairs[:, 0, part], pairs[:, 1, part]
                where = pl.ds(side * count, count)
                rest[-2][part, where] = jnp.where(first, low, high).astype(BF)
                rest[-1][part, where] = jnp.where(first, high, low).astype(BF)


def token_kernel(back_ref, w_skip_ref, tokens_ref, skip_ref, extra_ref):
    width = w_skip_ref.shape[1]
    items = tokens_ref.shape[0]
    local = tokens_ref.shape[1] * tokens_ref.shape[2]
    body = items // back_ref.shape[0] * local
    grad = back_ref[:, :body].reshape(items * local, width)
    tokens_ref[...] = dot(grad, w_skip_ref[:width], 1, 1).astype(BF).reshape(tokens_ref.shape)
    skip_ref[...] = dot(grad, w_skip_ref[width:], 1, 1).astype(BF).reshape(skip_ref.shape)
    extra = back_ref[:, body:].reshape(-1, width)
    extra_ref[...] = dot(extra, w_skip_ref[...], 1, 1).astype(BF).reshape(extra_ref.shape)


def fold_matrix(shape, low, wide, period):
    row = lax.broadcasted_iota(jnp.int32, shape, 0)
    col = lax.broadcasted_iota(jnp.int32, shape, 1)
    return jnp.where((col >= low) & (col < low + wide) & (row % period == col - low), 1.0, 0.0)


def pack_kernel(
    sums_attend_ref,
    sums_up_ref,
    sums_final_ref,
    head_sum_ref,
    grad_head_ref,
    conv_sum_ref,
    conv_bias_ref,
    table_ref,
    *rest,
):
    stacked_ref, shared_ref = rest[-2:]
    items, lanes, _ = head_sum_ref.shape
    values = lanes // items
    exact = functools.partial(
        jnp.dot, precision=lax.Precision.HIGHEST, preferred_element_type=F32
    )
    stacked_ref[0:1] = sums_attend_ref[2:3]
    stacked_ref[1:2] = sums_attend_ref[0:1]
    stacked_ref[2:3] = sums_attend_ref[1:2]
    stacked_ref[3:4] = sums_up_ref[2:3]
    stacked_ref[4:6] = sums_up_ref[0:2]
    stacked_ref[6:7] = sums_final_ref[2:3]
    stacked_ref[7:9] = sums_final_ref[0:2]
    head = head_sum_ref[0, 0:values]
    for item in range(1, items):
        head = head + head_sum_ref[item, item * values : (item + 1) * values]
    stacked_ref[9 : 9 + values] = head
    row = lax.broadcasted_iota(jnp.int32, (8, lanes), 0)
    col = lax.broadcasted_iota(jnp.int32, (8, lanes), 1)
    left = jnp.where(col % 4 == row, 1.0, 0.0)
    shared = jnp.zeros((8, 128), F32)
    for tap in range(9):
        picked = conv_sum_ref[0] * table_ref[0, tap].astype(F32)
        for k in range(1, 9):
            picked = picked + conv_sum_ref[k] * table_ref[k, tap].astype(F32)
        shared = shared + exact(exact(left, picked), fold_matrix((lanes, 128), 4 * tap, 4, 4))
    bias = exact(grad_head_ref[...], fold_matrix((lanes, 128), 64, values, values))
    bias = bias + exact(conv_bias_ref[...], fold_matrix((lanes, 128), 96, 4, 4))
    first = lax.broadcasted_iota(jnp.int32, (8, 128), 0) == 0
    shared_ref[...] = shared + jnp.where(first, bias, 0.0)


def whole(shape):
    return pl.BlockSpec(shape, lambda *_: (0,) * len(shape), pipeline_mode=pl.Buffered(1))


def params():
    return pltpu.CompilerParams(vmem_limit_bytes=60 * MIB)


def cost(flops, moved, transcendentals=0):
    del flops, moved, transcendentals
    return pl.CostEstimate(flops=1024, bytes_accessed=1024, transcendentals=0)


def sds(shape, dtype):
    return jax.ShapeDtypeStruct(shape, dtype)


def swap(block, axis, gap):
    count = lax.axis_size(axis)
    return lax.ppermute(block, axis, [(i, i ^ gap) for i in range(count)])


def serve_kernel(tasks, places_ref, *refs):
    del places_ref
    inputs = sum(len(parts) for task in tasks for parts in task["sides"])
    outs = refs[len(refs) - sum(len(task["outs"]) for task in tasks) :]
    at, out_at = 0, 0
    del inputs
    for task in tasks:
        values = []
        for parts in task["sides"]:
            total = refs[at][...].astype(F32)
            for k in range(1, len(parts)):
                total = total + refs[at + k][...].astype(F32)
            at += len(parts)
            values.append(total)
        task["emit"](values, outs[out_at : out_at + len(task["outs"])])
        out_at += len(task["outs"])


def serve(tasks, after, name, places):
    arrays, specs = [], []
    for task in tasks:
        for parts in task["sides"]:
            for array, starts, sizes in parts:
                index = tuple(
                    start // size if isinstance(start, int) else start
                    for start, size in zip(starts, sizes, strict=True)
                )

                def where(_, ref, index=index):
                    return tuple(i if isinstance(i, int) else ref[i[0]] for i in index)

                arrays.append(array)
                specs.append(pl.BlockSpec(tuple(sizes), where))
    outs = [out for task in tasks for out in task["outs"]]
    moved = sum(2 * int(np.prod(spec.block_shape)) for spec in specs)
    return pl.pallas_call(
        functools.partial(serve_kernel, tasks),
        grid_spec=pltpu.PrefetchScalarGridSpec(
            num_scalar_prefetch=1,
            grid=(1,),
            in_specs=specs + [pl.BlockSpec(memory_space=pl.ANY)] * len(after),
            out_specs=[
                pl.BlockSpec(out.shape, lambda _, ref, n=len(out.shape): (0,) * n) for out in outs
            ],
        ),
        out_shape=outs,
        compiler_params=params(),
        cost_estimate=cost(moved, 2 * moved),
        name=name,
    )(places, *arrays, *after)


def emit_low(values, outs):
    for value, out in zip(values, outs, strict=True):
        out[...] = value.astype(BF)


def place_table():
    own = [lax.axis_index("ty"), lax.axis_index("tx") // 2]
    batch = lax.axis_size("batch")
    own += [(lax.axis_index("batch") >> bit) % 2 for bit in range(batch.bit_length() - 1)]
    return jnp.stack([v for place in own for v in (place, 1 - place)]).astype(jnp.int32)


class Sum:
    def __init__(self, grads, units, inner, columns, table):
        batch = lax.axis_size("batch")
        bits = batch.bit_length() - 1
        rows = sum(grad.size for grad in grads) // (units * columns)
        self.own = rows // lax.axis_size(ALL) // inner
        self.columns = columns
        self.table = table
        self.dims = [units] + [2] * bits + [2, 2, 2, inner, self.own, columns]
        self.moves = {"y": bits + 1, "x": bits + 2, "c": bits + 3}
        self.places = {"y": (0, 1), "x": (2, 3)}
        self.links = {"y": ("ty", 1), "x": ("tx", 2), "c": ("tx", 1)}
        for bit in range(bits):
            self.moves[bit] = bits - bit
            self.places[bit] = (4 + 2 * bit, 5 + 2 * bit)
            self.links[bit] = ("batch", 1 << bit)
        self.cut = 0 if units > 1 else len(self.dims) - 3
        self.half = self.dims[self.cut] // 2
        tail = list(range(bits))
        self.orders = [["x", "y"] + tail, ["y", "x"] + tail]
        at = self.moves["c"]
        if len(grads) == 1:
            grad = grads[0].reshape(self.dims)
            core = lax.axis_index("tx") % 2
            keep = lax.dynamic_slice_in_dim(grad, core, 1, at)
            send = lax.dynamic_slice_in_dim(grad, 1 - core, 1, at)
        else:
            halved = list(self.dims)
            halved[at] = 1
            keep, send = grads[0].reshape(halved), grads[1].reshape(halved)
        self.sent = [send]
        received = swap(send, *self.links["c"])
        self.parts = [[(keep, ("c",)), (received, ("c",))] for _ in range(2)]
        self.done = [["c"], ["c"]]

    def pick(self, part, chosen, side):
        array, fixed = part
        starts, sizes = [0] * array.ndim, list(array.shape)
        for move, where in chosen.items():
            if move not in fixed:
                starts[self.moves[move]] = where
                sizes[self.moves[move]] = 1
        if "side" not in fixed:
            starts[self.cut], sizes[self.cut] = side * self.half, self.half
        return array, starts, sizes

    def task(self):
        if self.orders[0][0] == self.orders[1][0]:
            return self.joint_task()
        sides, outs = [], []
        for side in range(2):
            move = self.orders[side][0]
            chosen = {m: self.places[m][:1] for m in self.done[side] if m != "c"}
            chosen[move] = self.places[move][1:]
            parts = [self.pick(part, chosen, side) for part in self.parts[side]]
            sides.append(parts)
            outs.append(sds(tuple(parts[0][2]), BF))
        return {"sides": sides, "outs": outs, "emit": emit_low}

    def joint_task(self):
        move = self.orders[0][0]
        sides = []
        for side in range(2):
            chosen = {m: self.places[m][:1] for m in self.done[side] if m != "c"}
            chosen[move] = self.places[move][1:]
            sides.append([self.pick(part, chosen, side) for part in self.parts[side]])
        shape = list(sides[0][0][2])
        shape[self.cut] = 2 * self.half
        cut, half = self.cut, self.half

        def emit(values, outs):
            for side in range(2):
                index = [slice(None)] * len(shape)
                index[cut] = slice(side * half, (side + 1) * half)
                outs[0][tuple(index)] = values[side].astype(BF)

        return {"sides": sides, "outs": [sds(tuple(shape), BF)], "emit": emit}

    def accept(self, sent):
        if len(sent) == 1:
            move = self.orders[0][0]
            received = swap(sent[0], *self.links[move])
            for side in range(2):
                self.orders[side].pop(0)
                self.done[side].append(move)
                self.parts[side].append((received, tuple(self.done[side])))
            return
        for side in range(2):
            move = self.orders[side].pop(0)
            self.done[side].append(move)
            received = swap(sent[side], *self.links[move])
            self.parts[side].append((received, ("side",) + tuple(self.done[side])))

    def last_task(self, layout):
        sides = []
        for side in range(2):
            chosen = {m: self.places[m][:1] for m in self.done[side] if m != "c"}
            sides.append([self.pick(part, chosen, side) for part in self.parts[side]])
        shapes, units = layout
        own, columns, half = self.own, self.columns, self.half

        def emit(values, outs):
            for side in range(2):
                value = values[side].reshape(half, own, columns)
                for k in range(half):
                    out, row, col = units[side * half + k]
                    outs[out][
                        row * own : (row + 1) * own, col * columns : (col + 1) * columns
                    ] = value[k]

        outs = [sds((r * own, c * columns), F32) for r, c in shapes]
        return {"sides": sides, "outs": outs, "emit": emit}


def run_tasks(sums, after, name):
    places = sums[0][0].table
    tasks = []
    for sum_, layout in sums:
        tasks.append(sum_.task() if sum_.orders[0] else sum_.last_task(layout))
    outs = serve(tasks, after, name, places)
    results, at = [], 0
    for (sum_, _), task in zip(sums, tasks, strict=True):
        got = outs[at : at + len(task["outs"])]
        at += len(task["outs"])
        if sum_.orders[0]:
            sum_.accept(got)
        else:
            results.append(got)
    return outs, results


def conv_map():
    table = np.zeros((9, 9, 4, 4), np.float32)
    for row_off in range(3):
        for col_off in range(3):
            for p in range(4):
                for q in range(4):
                    i = 2 * (row_off - 1) + p // 2 - q // 2 + 1
                    j = 2 * (col_off - 1) + p % 2 - q % 2 + 1
                    if 0 <= i < 3 and 0 <= j < 3:
                        table[i * 3 + j, row_off * 3 + col_off, p, q] = 1.0
    return table


def conv_lanes(share):
    table = conv_map().transpose(1, 0, 2, 3)
    wide = np.kron(np.eye(share, dtype=np.float32), np.ones((16, 16), np.float32))
    small = np.repeat(np.repeat(table, 4, 2), 4, 3)
    return np.tile(small, (1, 1, share, share)) * wide


def per_device(
    tokens,
    skip_tokens,
    extra_tokens,
    extra_skip,
    timesteps,
    target,
    w_skip,
    b_skip,
    norm1_gain,
    norm1_shift,
    w_qkv,
    w_out,
    b_out,
    norm2_gain,
    norm2_shift,
    w_up,
    b_up,
    w_down,
    b_down,
    final_gain,
    final_shift,
    w_head,
    b_head,
    w_conv,
    b_conv,
):
    items, rows, cols, width = tokens.shape
    hidden_units = w_up.shape[1]
    local = rows * cols
    patch_values = w_head.shape[1]
    chans = w_conv.shape[3]
    devices = lax.axis_size(ALL)
    groups = lax.axis_size(PLANE)
    place = lax.axis_index(PLANE)
    share = items // groups
    per_item = groups * local
    count = share * per_item
    head_dim = width // HEADS
    height, breadth = rows * PATCH, cols * PATCH

    def row(vector):
        return vector.astype(F32).reshape(1, -1)

    def to_items(array):
        return lax.all_to_all(array, PLANE, split_axis=0, concat_axis=0, tiled=True)

    some = 8
    joined_rows = 2 * local + 8
    tile_block = pl.BlockSpec((some, rows, cols, width), lambda i: (i, 0, 0, 0))
    flat_block = pl.BlockSpec((some, local, width), lambda i: (i, 0, 0))
    hidden0, joined = pl.pallas_call(
        merge_kernel,
        grid=(items // some,),
        in_specs=[tile_block, tile_block, whole((2 * width, width)), whole((width,))],
        out_specs=[flat_block, pl.BlockSpec((some, joined_rows, width), lambda i: (i, 0, 0))],
        out_shape=[sds((items, local, width), BF), sds((items, joined_rows, width), BF)],
        compiler_params=params(),
        cost_estimate=cost(items * local * 4 * width * width, 11e6),
        name="merge",
    )(tokens, skip_tokens, w_skip, b_skip)
    hidden0 = to_items(hidden0)
    hidden0 = hidden0.reshape(groups, share, local, width)
    target_patches = (
        target.reshape(items, rows, PATCH, cols, PATCH, chans)
        .transpose(0, 1, 3, 2, 4, 5)
        .reshape(items, local * patch_values)
    )
    high = lax.reduce_precision(target_patches, 8, 7)
    middle = lax.reduce_precision(target_patches - high, 8, 7)
    low = target_patches - high - middle
    thirds = jnp.concatenate([high, middle, low], 1).astype(BF).reshape(items, -1, width)
    joined = lax.dynamic_update_slice(joined, thirds, (0, 2 * local, 0))

    start = place * share
    joined_extra = jnp.concatenate(
        [
            lax.dynamic_slice_in_dim(extra_tokens, start, share, 0),
            lax.dynamic_slice_in_dim(extra_skip, start, share, 0),
        ],
        2,
    )
    extra_rows = share * EXTRA_PAD
    joined_extra = jnp.pad(joined_extra, ((0, 0), (0, EXTRA_PAD - 2), (0, 0)))
    joined_extra = joined_extra.reshape(extra_rows, 2 * width)
    hidden_extra = dot(joined_extra, w_skip, 1, 0) + row(b_skip)
    unit_extra, _ = norm_parts(hidden_extra)
    normed_extra = (unit_extra * row(norm1_gain) + row(norm1_shift)).astype(BF)
    pairs_extra = dot(normed_extra, w_qkv[:, width:], 1, 0).astype(BF)

    def by_head(block):
        return block.reshape(share, EXTRA_PAD, HEADS, head_dim).transpose(0, 2, 1, 3)

    key_extra = by_head(pairs_extra[:, :width])
    value_extra = by_head(pairs_extra[:, width:])

    weight = lax.dynamic_slice_in_dim(noise_weight(timesteps), start, share, 0)
    lanes = share * patch_values
    spread = jnp.tile(w_conv.reshape(9, chans, chans), (1, lanes // chans, lanes // chans))
    kernel = jnp.sum(jnp.asarray(conv_lanes(share)) * spread[None].astype(F32), 1).astype(BF)
    table = place_table()
    joined, table, joined_extra = lax.optimization_barrier(
        (joined, table, joined_extra, key_extra, value_extra, kernel, weight, normed_extra)
    )[:3]
    joined = to_items(joined).reshape(groups, share, joined_rows, width)
    thirds = joined[:, :, 2 * local : 2 * local + thirds.shape[1]].astype(F32)
    thirds = thirds.reshape(groups, share, 3, local, patch_values)
    target_own = (
        (thirds[:, :, 0] + thirds[:, :, 1] + thirds[:, :, 2])
        .transpose(0, 2, 1, 3)
        .reshape(per_item, share * patch_values)
    )

    vec = whole((width,))
    item_block = pl.BlockSpec((groups, 1, local, width), lambda i: (0, i, 0, 0))

    def per_share(*shape):
        return pl.BlockSpec((1,) + shape, lambda i: (i,) + (0,) * len(shape))

    normed1, qkv, probs, probs_extra, mixed, hidden1 = pl.pallas_call(
        attend_kernel,
        grid=(share,),
        in_specs=[
            item_block,
            per_share(HEADS, EXTRA_PAD, head_dim),
            per_share(HEADS, EXTRA_PAD, head_dim),
            vec,
            vec,
            vec,
            whole((width, 3 * width)),
            whole((width, width)),
        ],
        out_specs=[
            per_share(per_item, width),
            per_share(3 * width, per_item),
            per_share(HEADS, per_item, per_item),
            per_share(HEADS, EXTRA_PAD, per_item),
            per_share(width, per_item),
            per_share(per_item, width),
        ],
        out_shape=[
            sds((share, per_item, width), BF),
            sds((share, 3 * width, per_item), BF),
            sds((share, HEADS, per_item, per_item), BF),
            sds((share, HEADS, EXTRA_PAD, per_item), BF),
            sds((share, width, per_item), BF),
            sds((share, per_item, width), F32),
        ],
        scratch_shapes=[
            pltpu.VMEM((HEADS, per_item, per_item), F32),
            pltpu.VMEM((HEADS, EXTRA_PAD, per_item), F32),
        ],
        compiler_params=params(),
        cost_estimate=cost(count * (8 * width * width + 16 * per_item * width), 25e6, 3e6),
        name="attend",
    )(
        hidden0,
        key_extra,
        value_extra,
        norm1_gain,
        norm1_shift,
        b_out,
        w_qkv,
        w_out,
    )
    hidden1 = hidden1.reshape(count, width)

    chunk = width
    chunks = hidden_units // chunk
    by_col = pl.BlockSpec((1, count, chunk), lambda j: (j, 0, 0))
    active, slope, normed2, hidden2 = pl.pallas_call(
        forward_kernel,
        grid=(chunks,),
        in_specs=[
            whole((count, width)),
            vec,
            vec,
            whole((hidden_units,)),
            vec,
            pl.BlockSpec((width, chunk), lambda j: (0, j)),
            pl.BlockSpec((chunk, width), lambda j: (j, 0)),
        ],
        out_specs=[by_col, by_col, whole((count, width)), whole((count, width))],
        out_shape=[
            sds((chunks, count, chunk), BF),
            sds((chunks, count, chunk), BF),
            sds((count, width), BF),
            sds((count, width), F32),
        ],
        scratch_shapes=[pltpu.VMEM((chunks, chunk), F32)],
        compiler_params=params(),
        cost_estimate=cost(count * 4 * width * hidden_units, 25e6, 5e6),
        name="forward",
    )(hidden1, norm2_gain, norm2_shift, b_up, b_down, w_up, w_down)
    (
        result,
        grad_hidden2,
        grad_down,
        grad_head,
        sums_final,
        head_sum,
        conv_sum,
        conv_bias,
    ) = pl.pallas_call(
        functools.partial(turn_kernel, rows, cols, lax.axis_size("tx")),
        grid=(1,),
        in_specs=[
            whole((count, width)),
            vec,
            vec,
            whole((patch_values, width)),
            whole((9, lanes, lanes)),
            whole((patch_values,)),
            whole((chans,)),
            whole((share,)),
            whole((per_item, lanes)),
            pl.BlockSpec(memory_space=pl.ANY),
        ],
        out_specs=[
            whole((per_item, lanes)),
            whole((count, width)),
            whole((count, width)),
            whole((1, lanes)),
            whole((8, width)),
            whole((share, lanes, width)),
            whole((9, lanes, lanes)),
            whole((1, lanes)),
        ],
        out_shape=[
            sds((per_item, lanes), BF),
            sds((count, width), F32),
            sds((count, width), BF),
            sds((1, lanes), F32),
            sds((8, width), F32),
            sds((share, lanes, width), F32),
            sds((9, lanes, lanes), F32),
            sds((1, lanes), F32),
        ],
        scratch_shapes=[pltpu.VMEM((count, width), F32)],
        compiler_params=params(),
        cost_estimate=cost(1e9, 10e6),
        name="turn",
    )(
        hidden2,
        final_gain,
        final_shift,
        w_head.T,
        kernel,
        b_head,
        b_conv,
        weight,
        target_own,
        joined,
    )

    any_place = pl.BlockSpec(memory_space=pl.ANY)
    core = lax.axis_index("tx") % 2
    core = core.astype(jnp.int32).reshape(1)
    core_spec = pl.BlockSpec(memory_space=pltpu.SMEM)

    def split_outs(units, rows, block_rows, own, cols, index):
        if can_split(own):
            spec = pl.BlockSpec(
                (units, block_rows // (2 * own), own, cols), lambda j: index(j) + (0, 0)
            )
            return spec, lambda n: sds((n, rows // (2 * own), own, cols), BF), 2
        spec = pl.BlockSpec((units, block_rows, cols), lambda j: index(j) + (0,))
        return spec, lambda n: sds((n, rows, cols), BF), 1

    own = width // devices
    half = width // 2
    units = 2 * chunks + 2
    chain_down = CHAIN_DOWN and can_split(own)
    if chain_down:
        down_specs = [
            pl.BlockSpec((8, chunk // (8 * own), own, half), lambda j: (0, j, 0, 0))
        ] * 2
        down_shapes = [sds((8, width // (2 * own), own, half), BF)] * 2
    else:
        down_specs = [pl.BlockSpec((chunk, width), lambda j: (j, 0))]
        down_shapes = [sds((hidden_units, width), BF)]
    grad_w_down = pl.pallas_call(
        functools.partial(down_kernel, own, chain_down),
        grid=(chunks,),
        in_specs=[by_col, whole((count, width)), core_spec],
        out_specs=down_specs,
        out_shape=down_shapes,
        compiler_params=params(),
        cost_estimate=cost(count * 2 * width * hidden_units, 11e6),
        name="down_weight",
    )(active, grad_down, core)
    if chain_down:
        sum_down = Sum(grad_w_down, 8, 1, half, table)
    else:
        out_down = lax.psum_scatter(
            grad_w_down[0], ALL, scatter_dimension=0, tiled=True
        ).astype(F32)

    up_spec, up_shape, up_outs = split_outs(2, width, width, own, half, lambda j: (j, 0))

    def held_col(j):
        return jnp.minimum(j, chunks - 1)

    grad_b_up, grad_hidden1, grad_branch, sums_up, *grad_w_up = pl.pallas_call(
        functools.partial(up_kernel, own),
        grid=(chunks + 1,),
        in_specs=[
            pl.BlockSpec((1, count, chunk), lambda j: (held_col(j), 0, 0)),
            whole((count, width)),
            pl.BlockSpec((chunk, width), lambda j: (held_col(j), 0)),
            pl.BlockSpec((width, chunk), lambda j: (0, held_col(j))),
            whole((count, width)),
            any_place,
            vec,
            any_place,
            any_place,
            core_spec,
        ]
        + [any_place] * len(grad_w_down),
        out_specs=[
            pl.BlockSpec((1, 8, chunk), lambda j: (held_col(j), 0, 0)),
            whole((count, width)),
            whole((count, width)),
            whole((8, width)),
        ]
        + [up_spec] * up_outs,
        out_shape=[
            sds((chunks, 8, chunk), F32),
            sds((count, width), F32),
            sds((count, width), BF),
            sds((8, width), F32),
        ]
        + [up_shape(units)] * up_outs,
        scratch_shapes=[
            pltpu.VMEM((count, width), F32),
            pltpu.VMEM((count, width), F32),
            pltpu.VMEM((count, width), F32),
            pltpu.VMEM((share, width, per_item), BF),
            pltpu.SemaphoreType.DMA((3,)),
        ],
        compiler_params=params(),
        cost_estimate=cost(count * (6 * hidden_units + 2 * width) * width, 25e6),
        name="up_weight",
    )(
        slope,
        grad_down,
        w_down,
        w_up,
        normed2,
        hidden1,
        norm2_gain,
        grad_hidden2,
        mixed,
        core,
        *grad_w_down,
    )
    if can_split(own):
        sum_up = Sum(grad_w_up, units, 1, half, table)
    down_layout = ([(4, 2)], [(0, k // 2, k % 2) for k in range(8)])
    up_layout = (
        [(1, 2 * chunks), (1, 2)],
        [(0, 0, k) for k in range(2 * chunks)] + [(1, 0, 0), (1, 0, 1)],
    )
    late_layout = (
        [(1, 6), (2, 2)],
        [(0, 0, k) for k in range(6)] + [(1, 0, 0), (1, 1, 0), (1, 0, 1), (1, 1, 1)],
    )

    after = sum_up.sent if can_split(own) else []
    if chain_down:
        after, _ = run_tasks([(sum_down, None)], after, "serve_0")
        early = [(sum_down, None)]
    else:
        early = []
    grad_qkv, grad_key_extra, grad_value_extra = [], [], []
    sums_attend = sums_up
    grad_hidden0 = None
    back_rows = share * local + 16
    for first, number in ((0, share - 1), (share - 1, 1)):

        def one(*shape, first=first):
            return pl.BlockSpec((1,) + shape, lambda i: (first + i,) + (0,) * len(shape))

        def own_item(*shape):
            return pl.BlockSpec((1,) + shape, lambda i: (i,) + (0,) * len(shape))

        held = [grad_hidden0] if first else []
        outs = pl.pallas_call(
            functools.partial(attend_back_kernel, first == 0),
            grid=(number,),
            in_specs=[
                pl.BlockSpec(
                    (groups, 1, local, width), lambda i, first=first: (0, first + i, 0, 0)
                ),
                one(per_item, width),
                one(per_item, width),
                one(3 * width, per_item),
                one(HEADS, per_item, per_item),
                one(HEADS, EXTRA_PAD, per_item),
                one(HEADS, EXTRA_PAD, head_dim),
                one(HEADS, EXTRA_PAD, head_dim),
                vec,
                any_place,
                whole((width, width)),
                whole((8, width)),
            ]
            + [any_place] * (len(held) + len(after)),
            out_specs=[
                own_item(3 * width, per_item),
                own_item(HEADS, EXTRA_PAD, head_dim),
                own_item(HEADS, EXTRA_PAD, head_dim),
                pl.BlockSpec((groups, local, width), lambda i, first=first: (0, first + i, 0)),
                whole((8, width)),
            ],
            out_shape=[
                sds((number, 3 * width, per_item), BF),
                sds((number, HEADS, EXTRA_PAD, head_dim), F32),
                sds((number, HEADS, EXTRA_PAD, head_dim), F32),
                sds((groups, back_rows, width), BF),
                sds((8, width), F32),
            ],
            input_output_aliases={12: 3} if first else {},
            scratch_shapes=[
                pltpu.VMEM((width, per_item), BF),
                pltpu.VMEM((HEADS, per_item, per_item), F32),
                pltpu.VMEM((HEADS, EXTRA_PAD, per_item), F32),
                pltpu.VMEM((HEADS, per_item, per_item), BF),
                pltpu.VMEM((HEADS, EXTRA_PAD, per_item), BF),
                pltpu.VMEM((width, 3 * width), BF),
                pltpu.SemaphoreType.DMA,
            ],
            compiler_params=params(),
            cost_estimate=cost(
                per_item * (8 * width * width + 40 * per_item * width), 12e6
            ),
            name="attend_back",
        )(
            hidden0,
            grad_hidden1.reshape(share, per_item, width),
            grad_branch.reshape(share, per_item, width),
            qkv,
            probs,
            probs_extra,
            key_extra,
            value_extra,
            norm1_gain,
            w_qkv,
            w_out,
            sums_attend,
            *held,
            *after,
        )
        grad_qkv += [outs[0]] * number
        grad_key_extra += [outs[1]] * number
        grad_value_extra += [outs[2]] * number
        grad_hidden0, sums_attend = outs[3], outs[4]
        after = []
        if can_split(own) and not first:
            after, _ = run_tasks([(sum_up, None)] + early, [sums_attend], "serve_1")
    places_of = [i for number in (share - 1, 1) for i in range(number)]

    latent = result.reshape(groups, local * share * patch_values // width, width)
    pairs_extra, grad_extra, sums_attend, grad_back = pl.pallas_call(
        functools.partial(extra_back_kernel, share),
        grid=(1,),
        in_specs=[
            whole((extra_rows, width)),
            vec,
            pl.BlockSpec((width, width), lambda *_: (0, 1)),
            pl.BlockSpec((width, width), lambda *_: (0, 2)),
            whole(latent.shape),
            whole((8, width)),
        ]
        + [
            pl.BlockSpec((1, HEADS, EXTRA_PAD, head_dim), lambda *_, at=at: (at, 0, 0, 0))
            for at in places_of * 2
        ]
        + [any_place] * (1 + len(after)),
        out_specs=[
            whole((2, extra_rows, width)),
            whole((extra_rows, width)),
            whole((8, width)),
            pl.BlockSpec((groups, 16, width), lambda *_: (0, share * local // 16, 0)),
        ],
        out_shape=[
            sds((2, extra_rows, width), BF),
            sds((extra_rows, width), BF),
            sds((8, width), F32),
            sds((groups, back_rows, width), BF),
        ],
        input_output_aliases={6 + 2 * share: 3},
        compiler_params=params(),
        cost_estimate=cost(1e8, 5e6),
        name="extra_back",
    )(
        hidden_extra,
        norm1_gain,
        w_qkv,
        w_qkv,
        latent,
        sums_attend,
        *grad_key_extra,
        *grad_value_extra,
        grad_hidden0,
        *after,
    )

    late_spec, late_shape, late_outs = split_outs(
        2, width, width, own, width // 2, lambda j: (j, 0)
    )

    def skip_col(j):
        return jnp.maximum(j - 3, 0)

    def qkv_row(j):
        return jnp.minimum(j, 2)

    half = width // 2
    grad_late = pl.pallas_call(
        functools.partial(late_weight_kernel, own),
        grid=(5,),
        in_specs=[
            whole((share, per_item, width)),
            whole((extra_rows, width)),
            pl.BlockSpec(
                (1, extra_rows, width), lambda j: (jnp.clip(j - 1, 0, 1), 0, 0)
            ),
            any_place,
            pl.BlockSpec((groups, back_rows, half), lambda j: (0, 0, skip_col(j))),
            whole((extra_rows, 2 * width)),
            pl.BlockSpec((extra_rows, half), lambda j: (0, skip_col(j))),
        ]
        + [
            pl.BlockSpec((1, width, per_item), lambda j, at=at: (at, qkv_row(j), 0))
            for at in places_of
        ]
        + [core_spec],
        out_specs=[late_spec] * late_outs,
        out_shape=[late_shape(10)] * late_outs,
        scratch_shapes=[pltpu.VMEM(joined.shape, BF), pltpu.SemaphoreType.DMA],
        compiler_params=params(),
        cost_estimate=cost(count * 10 * width * width, 12e6),
        name="late_weight",
    )(
        normed1,
        normed_extra,
        pairs_extra,
        joined,
        grad_back,
        joined_extra,
        grad_extra,
        *grad_qkv,
        core,
    )

    def hold(values, *others):
        return lax.optimization_barrier((values, others))[0]

    if can_split(own):
        after, _ = run_tasks([(sum_up, None)] + early, [grad_late[0]], "serve_2")
        grad_late = [grad_late[0], hold(grad_late[1], after)]
        sum_late = Sum(grad_late, 10, 1, half, table)
    else:
        after = list(grad_late)

    stacked_count = 9 + patch_values
    stacked, shared = pl.pallas_call(
        pack_kernel,
        in_specs=[pl.BlockSpec(memory_space=pltpu.VMEM)] * 8 + [any_place] * len(after),
        out_specs=[pl.BlockSpec(memory_space=pltpu.VMEM)] * 2,
        out_shape=[sds((stacked_count, width), F32), sds((8, 128), F32)],
        compiler_params=params(),
        cost_estimate=cost(1e6, 1e6),
        name="pack",
    )(
        sums_attend,
        sums_up,
        sums_final,
        head_sum,
        grad_head,
        conv_sum,
        conv_bias,
        jnp.asarray(conv_lanes(share), BF),
        *after,
    )
    packed = jnp.concatenate(
        [
            stacked.reshape(stacked_count, devices, own).transpose(1, 0, 2).reshape(devices, -1),
            grad_b_up[:, 0].reshape(devices, -1),
            jnp.broadcast_to(shared[:4].reshape(1, -1), (devices, 512)),
        ],
        1,
    )
    packed_size = packed.shape[1]
    packed = jnp.pad(packed, ((0, 0), (0, (-packed.shape[1]) % 128)))
    if not can_split(own):
        wide = grad_w_up[0].transpose(1, 0, 2).reshape(width, -1)
        wide = lax.psum_scatter(wide, ALL, scatter_dimension=0, tiled=True).astype(F32)
        out_up, out_out = wide[:, :hidden_units], wide[:, hidden_units:]
        wide = grad_late[0][:6].transpose(1, 0, 2).reshape(width, -1)
        out_qkv = lax.psum_scatter(wide, ALL, scatter_dimension=0, tiled=True).astype(F32)
        tall = grad_late[0][6:].reshape(2, 2, width, half).transpose(1, 2, 0, 3)
        tall = tall.reshape(2 * width, width)
        out_skip = lax.psum_scatter(tall, ALL, scatter_dimension=0, tiled=True).astype(F32)
    else:
        after, _ = run_tasks([(sum_late, None), (sum_up, None)] + early, [packed], "serve_5")
    exchanged = lax.all_to_all(hold(packed, after), ALL, split_axis=0, concat_axis=0, tiled=True)
    if can_split(own):
        if chain_down:
            early = [(sum_down, down_layout)]
        after, results = run_tasks(
            [(sum_late, None), (sum_up, None)] + early, [exchanged], "serve_6"
        )
        if chain_down:
            out_down = results[0][0]
        after, results = run_tasks([(sum_late, None), (sum_up, up_layout)], after, "serve_7")
        out_up, out_out = results[0]
    back = to_items(hold(grad_back, after))
    if can_split(own):
        while sum_late.orders[0]:
            after, _ = run_tasks([(sum_late, None)], after, "serve_8")
    some_groups = max(groups // 2, 1)
    token_block = pl.BlockSpec(
        (some_groups * share, rows, cols, width), lambda i: (i, 0, 0, 0)
    )
    grad_tokens, grad_skip_tokens, grad_extra_all = pl.pallas_call(
        token_kernel,
        grid=(groups // some_groups,),
        in_specs=[
            pl.BlockSpec((some_groups, back_rows, width), lambda i: (i, 0, 0)),
            whole((2 * width, width)),
        ],
        out_specs=[
            token_block,
            token_block,
            pl.BlockSpec((some_groups, 16, 2 * width), lambda i: (i, 0, 0)),
        ],
        out_shape=[sds(tokens.shape, BF)] * 2 + [sds((groups, 16, 2 * width), BF)],
        compiler_params=params(),
        cost_estimate=cost(items * local * 4 * width * width, 8e6),
        name="tokens",
    )(hold(back, after), w_skip)
    summed = jnp.sum(hold(exchanged, after), 0)
    small = [summed[k * own : (k + 1) * own] for k in range(9)]
    own_head = summed[9 * own : stacked_count * own].reshape(patch_values, own).T
    up_low = stacked_count * own
    own_b_up = summed[up_low : up_low + hidden_units // devices]
    shared = summed[up_low + hidden_units // devices : packed_size].reshape(4, 128)

    latent_row = share * local + 2 * share
    latent = back[:, latent_row : latent_row + latent.shape[1]]
    latent_out = (
        hold(latent, after)
        .reshape(groups, rows, cols, share, PATCH, PATCH, chans)
        .transpose(0, 3, 1, 4, 2, 5, 6)
        .reshape(items, height, breadth, chans)
    )
    grad_joined_extra = grad_extra_all[:, : 2 * share].reshape(items, 2, 2 * width)
    if can_split(own):
        _, results = run_tasks([(sum_late, late_layout)], [grad_tokens, latent_out], "serve_9")
        out_qkv, out_skip = results[0]
    return (
        latent_out,
        grad_tokens,
        grad_skip_tokens,
        grad_joined_extra[..., :width],
        grad_joined_extra[..., width:],
        out_skip,
        small[0],
        small[1],
        small[2],
        out_qkv,
        out_out,
        small[3],
        small[4],
        small[5],
        out_up,
        own_b_up,
        out_down,
        small[6],
        small[7],
        small[8],
        own_head,
        shared[0, 64 : 64 + patch_values],
        shared[:, : 9 * chans].reshape(chans, 3, 3, chans).transpose(1, 2, 0, 3),
        shared[0, 96 : 96 + chans],
    )


def solution(mesh):
    tiles = P("batch", "ty", "tx", None)
    pairs = P("batch", None, None)
    matrix = P(ALL, None)
    vector = P(ALL)
    return jax.shard_map(
        per_device,
        mesh=mesh,
        in_specs=(tiles, tiles, pairs, pairs, P("batch"), tiles) + (P(),) * 19,
        out_specs=(
            tiles,
            tiles,
            tiles,
            pairs,
            pairs,
            matrix,
            vector,
            vector,
            vector,
            matrix,
            matrix,
            vector,
            vector,
            vector,
            matrix,
            vector,
            matrix,
            vector,
            vector,
            vector,
            matrix,
            P(),
            P(),
            P(),
        ),
        check_vma=False,
    )
```

```python
import functools

import jax
import jax.numpy as jnp
import numpy as np
from jax import lax
from jax.experimental import pallas as pl
from jax.experimental.pallas import tpu as pltpu
from jax.sharding import PartitionSpec as P

HEADS = 12
PATCH = 2
EXTRA_PAD = 8
CHAIN_DOWN = True
EPS = 1e-05
BF = jnp.bfloat16
F32 = jnp.float32
PLANE = ("ty", "tx")
ALL = ("batch", "ty", "tx")
MIB = 1024 * 1024


def dot(left, right, left_dim, right_dim):
    return lax.dot_general(
        left, right, (((left_dim,), (right_dim,)), ((), ())), preferred_element_type=F32
    )


def norm_parts(values):
    center = values - jnp.mean(values, -1, keepdims=True)
    scaled = lax.rsqrt(jnp.mean(center * center, -1, keepdims=True) + EPS)
    return center * scaled, scaled


def norm_back(inner, normed, scaled):
    return scaled * (
        inner
        - jnp.mean(inner, -1, keepdims=True)
        - normed * jnp.mean(inner * normed, -1, keepdims=True)
    )


def flat(ref):
    return ref[...].astype(F32).reshape(1, -1)


def row_sum(values):
    return jnp.sum(values, 0, keepdims=True)


def gelu_parts(upper):
    spread = 0.5 + 0.5 * lax.erf(upper * np.float32(0.5**0.5))
    bell = jnp.exp(upper * upper * -0.5) * np.float32((2 * np.pi) ** -0.5)
    return upper * spread, spread + upper * bell


def noise_weight(timesteps):
    frac = (timesteps.astype(F32) / 1000.0 + 0.008) / 1.008
    kept = jnp.cos(frac * (0.5 * jnp.pi)) ** 2
    return jnp.minimum(1.0, 5.0 * (1.0 - kept) / kept)


def staggered(stages, groups):
    for step in range(len(stages) + len(groups) - 1):
        for index in reversed(range(len(stages))):
            if 0 <= step - index < len(groups):
                for member in groups[step - index]:
                    stages[index](member)


def can_split(own):
    return own % 8 == 0


def store_split(value, own, lane_refs):
    if len(lane_refs) == 1:
        lane_refs[0][...] = value.astype(BF)
        return
    keep_ref, send_ref, core_ref = lane_refs
    pairs = value.reshape(value.shape[0] // (2 * own), 2, own, value.shape[1])
    first = core_ref[0] == 0
    keep = jnp.where(first, pairs[:, 0], pairs[:, 1])
    send = jnp.where(first, pairs[:, 1], pairs[:, 0])
    keep_ref[...] = keep.astype(BF)
    send_ref[...] = send.astype(BF)


def merge_kernel(tokens_ref, skip_ref, w_skip_ref, b_skip_ref, hidden_ref, joined_ref):
    width = w_skip_ref.shape[1]
    local = tokens_ref.shape[1] * tokens_ref.shape[2]
    body = tokens_ref[...].reshape(-1, width)
    body_skip = skip_ref[...].reshape(-1, width)
    hidden = (
        dot(body, w_skip_ref[:width], 1, 0)
        + dot(body_skip, w_skip_ref[width:], 1, 0)
        + b_skip_ref[...].astype(F32).reshape(1, width)
    )
    hidden_ref[...] = hidden.astype(BF).reshape(-1, local, width)
    joined_ref[:, :local] = body.reshape(-1, local, width)
    joined_ref[:, local : 2 * local] = body_skip.reshape(-1, local, width)


def attend_kernel(
    hidden_ref,
    key_extra_ref,
    value_extra_ref,
    gain_ref,
    shift_ref,
    b_out_ref,
    w_qkv_ref,
    w_out_ref,
    normed_ref,
    qkv_ref,
    probs_ref,
    probs_extra_ref,
    mixed_ref,
    hidden1_ref,
    scores_ref,
    scores_extra_ref,
):
    width = w_out_ref.shape[0]
    head_dim = width // HEADS
    scale = head_dim ** (-0.5)
    rows = hidden_ref.shape[0] * hidden_ref.shape[2]
    hidden = hidden_ref[...].reshape(rows, width).astype(F32)
    unit, _ = norm_parts(hidden)
    normed = (unit * flat(gain_ref) + flat(shift_ref)).astype(BF)
    normed_ref[0] = normed
    qkv_ref[0] = dot(w_qkv_ref[...], normed, 0, 1).astype(BF)
    live = lax.broadcasted_iota(jnp.int32, (EXTRA_PAD, rows), 0) < 2
    def score(head):
        low = head * head_dim
        query = qkv_ref[0, low : low + head_dim, :]
        key = qkv_ref[0, width + low : width + low + head_dim, :]
        scores_ref[head] = dot(key, query, 0, 0) * scale
        scores_extra = dot(key_extra_ref[0, head], query, 1, 0) * scale
        scores_extra_ref[head] = jnp.where(live, scores_extra, -1e30)

    def weigh(head):
        scores, scores_extra = scores_ref[head], scores_extra_ref[head]
        top = jnp.maximum(
            jnp.max(scores, 0, keepdims=True), jnp.max(scores_extra, 0, keepdims=True)
        )
        raised = jnp.exp(scores - top)
        raised_extra = jnp.exp(scores_extra - top)
        share = 1.0 / (row_sum(raised) + row_sum(raised_extra))
        probs_ref[0, head] = (raised * share).astype(BF)
        probs_extra_ref[0, head] = (raised_extra * share).astype(BF)

    def mix(head):
        low = head * head_dim
        value = qkv_ref[0, 2 * width + low : 2 * width + low + head_dim, :]
        mixed = dot(value, probs_ref[0, head], 1, 0) + dot(
            value_extra_ref[0, head], probs_extra_ref[0, head], 0, 0
        )
        mixed_ref[0, low : low + head_dim, :] = mixed.astype(BF)

    staggered([score, weigh, mix], [range(low, low + 4) for low in range(0, HEADS, 4)])
    hidden1_ref[0] = hidden + (dot(mixed_ref[0], w_out_ref[...], 0, 0) + flat(b_out_ref))


def forward_kernel(
    hidden1_ref,
    gain2_ref,
    shift2_ref,
    b_up_ref,
    b_down_ref,
    w_up_ref,
    w_down_ref,
    active_ref,
    slope_ref,
    normed2_ref,
    total,
    up_rows,
):
    step = pl.program_id(0)

    @pl.when(step == 0)
    def _():
        unit, _ = norm_parts(hidden1_ref[...])
        b_up = flat(b_up_ref)
        width = up_rows.shape[1]
        for j in range(up_rows.shape[0]):
            up_rows[j : j + 1] = b_up[:, j * width : (j + 1) * width]
        normed2_ref[...] = (unit * flat(gain2_ref) + flat(shift2_ref)).astype(BF)

    count = normed2_ref.shape[0]
    blocks = 3 if count % 48 == 0 else 1
    size = count // blocks
    rows = [slice(i * size, (i + 1) * size) for i in range(blocks)]

    def raise_rows(i):
        return dot(normed2_ref[rows[i]], w_up_ref[...], 1, 0) + up_rows[pl.ds(step, 1)]

    def activate(upper, i):
        active, slope = gelu_parts(upper)
        active = active.astype(BF)
        active_ref[0, rows[i]] = active
        slope_ref[0, rows[i]] = slope.astype(BF)
        return active

    def lower(active, i):
        part = dot(active, w_down_ref[...], 1, 0)
        base = jnp.where(step == 0, hidden1_ref[rows[i]] + flat(b_down_ref), total[rows[i]])
        total[rows[i]] = base + part

    upper = raise_rows(0)
    for i in range(blocks):
        following = raise_rows(i + 1) if i + 1 < blocks else None
        active = activate(upper, i)
        upper = following
        lower(active, i)


def turn_kernel(
    tile_rows,
    tile_cols,
    tiles_x,
    hidden2_ref,
    gainf_ref,
    shiftf_ref,
    w_head_ref,
    w_conv_ref,
    b_head_ref,
    b_conv_ref,
    weight_ref,
    target_ref,
    after_ref,
    result_ref,
    grad_hidden2_ref,
    grad_down_ref,
    grad_head_ref,
    sums_ref,
    head_sum_ref,
    conv_sum_ref,
    conv_bias_ref,
    total,
):
    per_item, lanes = target_ref.shape
    patch_values, width = w_head_ref.shape
    items = lanes // patch_values

    weight = flat(weight_ref)
    weight_lanes = jnp.concatenate(
        [jnp.broadcast_to(weight[:, i : i + 1], (1, patch_values)) for i in range(items)], 1
    )

    def head_of(i):
        parts = [w_head_ref[...]]
        if i > 0:
            parts = [jnp.zeros((i * patch_values, width), BF)] + parts
        if i < items - 1:
            parts = parts + [jnp.zeros((lanes - (i + 1) * patch_values, width), BF)]
        return jnp.concatenate(parts, 0)

    heads = [head_of(i) for i in range(items)]
    unit, scaled = norm_parts(hidden2_ref[...])
    total[...] = unit
    normedf = (unit * flat(gainf_ref) + flat(shiftf_ref)).astype(BF)
    normed2_final = [normedf[i * per_item : (i + 1) * per_item] for i in range(items)]
    patches = jnp.concatenate([flat(b_head_ref)] * items, 1)
    for i in range(items):
        patches = patches + dot(normed2_final[i], heads[i], 1, 1)
    patches = patches.astype(BF)

    def place(position):
        tile = position // (tile_rows * tile_cols)
        row = (tile // tiles_x) * tile_rows + (position // tile_cols) % tile_rows
        col = (tile % tiles_x) * tile_cols + position % tile_cols
        return row * 1024 + col

    own = place(lax.broadcasted_iota(jnp.int32, (per_item, 1), 0))
    other = place(lax.broadcasted_iota(jnp.int32, (1, per_item), 1))
    shifts = []
    for row_off in range(3):
        for col_off in range(3):
            wanted = own + ((row_off - 1) * 1024 + (col_off - 1))
            shifts.append(jnp.where(wanted == other, 1.0, 0.0).astype(BF))
    windows = [dot(shift, patches, 1, 0).astype(BF) for shift in shifts]
    result = jnp.concatenate([flat(b_conv_ref)] * (lanes // b_conv_ref.shape[0]), 1)
    for k in range(9):
        result = result + dot(windows[k], w_conv_ref[k], 1, 0)
    result_ref[...] = result.astype(BF)
    grad_result = (weight_lanes * (result - target_ref[...])).astype(BF)
    conv_bias_ref[...] = row_sum(grad_result.astype(F32))
    grad_patches = jnp.zeros(target_ref.shape, F32)
    for k in range(9):
        conv_sum_ref[k] = dot(windows[k], grad_result, 0, 0)
        moved = dot(shifts[8 - k], grad_result, 1, 0).astype(BF)
        grad_patches = grad_patches + dot(moved, w_conv_ref[k], 1, 1)
    grad_patches = grad_patches.astype(BF)
    grad_head_ref[...] = row_sum(grad_patches.astype(F32))
    sum_gain = jnp.zeros((1, unit.shape[1]), F32)
    sum_shift = sum_gain
    sum_down = sum_gain
    for i in range(items):
        rows = slice(i * per_item, (i + 1) * per_item)
        head_sum_ref[i] = dot(grad_patches, normed2_final[i], 0, 0)
        grad_normedf = dot(grad_patches, heads[i], 1, 0)
        unit_part = total[rows]
        sum_gain = sum_gain + row_sum(grad_normedf * unit_part)
        sum_shift = sum_shift + row_sum(grad_normedf)
        grad_hidden2 = norm_back(grad_normedf * flat(gainf_ref), unit_part, scaled[rows])
        grad_hidden2_ref[rows] = grad_hidden2
        grad_down = grad_hidden2.astype(BF)
        grad_down_ref[rows] = grad_down
        sum_down = sum_down + row_sum(grad_down.astype(F32))
    sums_ref[0:1] = sum_gain
    sums_ref[1:2] = sum_shift
    sums_ref[2:3] = sum_down


def down_kernel(own, split, active_ref, grad_down_ref, core_ref, *outs):
    total = dot(active_ref[0], grad_down_ref[...], 0, 0)
    if not split:
        outs[0][...] = total.astype(BF)
        return
    pairs = total.reshape(total.shape[0] // (8 * own), 2, 4, own, total.shape[1])
    first = core_ref[0] == 0
    half = total.shape[1] // 2
    for part in range(4):
        low, high = pairs[:, 0, part], pairs[:, 1, part]
        keep = jnp.where(first, low, high).astype(BF)
        send = jnp.where(first, high, low).astype(BF)
        for side in range(2):
            cols = slice(side * half, (side + 1) * half)
            outs[0][2 * part + side] = keep[:, :, cols]
            outs[1][2 * part + side] = send[:, :, cols]


def up_kernel(
    own,
    slope_ref,
    grad_down_ref,
    w_down_ref,
    w_up_ref,
    normed2_ref,
    hidden1_hbm,
    gain2_ref,
    grad_hidden2_hbm,
    mixed_hbm,
    core_ref,
    *rest,
):
    total, hidden1_ref, grad_hidden2_ref, mixed_ref, sems = rest[-5:]
    rest = rest[-11 if can_split(own) else -10 : -5]
    late_copies = [
        pltpu.make_async_copy(hidden1_hbm, hidden1_ref, sems.at[0]),
        pltpu.make_async_copy(grad_hidden2_hbm, grad_hidden2_ref, sems.at[1]),
        pltpu.make_async_copy(mixed_hbm, mixed_ref, sems.at[2]),
    ]

    @pl.when(pl.program_id(0) == 0)
    def _():
        for copy in late_copies:
            copy.start()

    grad_b_up_ref, grad_hidden1_ref, grad_branch_ref, sums_ref = rest[:4]
    rest = rest[4:]
    step = pl.program_id(0)
    steps = pl.num_programs(0)

    def store(value):
        half = value.shape[1] // 2
        for side in range(2):
            piece = value[:, side * half : (side + 1) * half]
            if can_split(own):
                store_split(piece, own, (rest[0].at[side], rest[1].at[side], core_ref))
            else:
                store_split(piece, own, (rest[0].at[side],))

    @pl.when(step < steps - 1)
    def _():
        grad_active = dot(grad_down_ref[...], w_down_ref[...], 1, 1)
        grad_upper = (grad_active * slope_ref[0].astype(F32)).astype(BF)
        grad_b_up_ref[0, 0:1] = row_sum(grad_upper.astype(F32))
        store(dot(normed2_ref[...], grad_upper, 0, 0))
        part = dot(grad_upper, w_up_ref[...], 1, 1)

        @pl.when(step == 0)
        def _():
            total[...] = part

        @pl.when(step > 0)
        def _():
            total[...] += part

    @pl.when(step == steps - 1)
    def _():
        for copy in late_copies:
            copy.wait()
        unit, scaled = norm_parts(hidden1_ref[...])
        grad_normed2 = total[...]
        sums_ref[0:1] = row_sum(grad_normed2 * unit)
        sums_ref[1:2] = row_sum(grad_normed2)
        grad_hidden1 = grad_hidden2_ref[...] + norm_back(
            grad_normed2 * flat(gain2_ref), unit, scaled
        )
        grad_hidden1_ref[...] = grad_hidden1
        grad_branch = grad_hidden1.astype(BF)
        grad_branch_ref[...] = grad_branch
        sums_ref[2:3] = row_sum(grad_branch.astype(F32))
        items, _, per_item = mixed_ref.shape
        value = dot(mixed_ref[0], grad_branch[:per_item], 1, 0)
        for item in range(1, items):
            rows = slice(item * per_item, (item + 1) * per_item)
            value = value + dot(mixed_ref[item], grad_branch[rows], 1, 0)
        store(value)


def attend_back_kernel(
    opening,
    hidden_ref,
    grad_hidden1_ref,
    grad_branch_ref,
    qkv_ref,
    probs_ref,
    probs_extra_ref,
    key_extra_ref,
    value_extra_ref,
    gain_ref,
    w_qkv_hbm,
    w_out_ref,
    sums_in_ref,
    *rest,
):
    (
        grad_qkv_ref,
        grad_key_extra_ref,
        grad_value_extra_ref,
        grad_hidden0_ref,
        sums_ref,
        grad_mixed_ref,
        grad_probs_ref,
        grad_probs_extra_ref,
        grad_scores_ref,
        grad_scores_extra_ref,
        w_qkv_ref,
        sem,
    ) = rest[-12:]
    step = pl.program_id(0)
    late_copy = pltpu.make_async_copy(w_qkv_hbm, w_qkv_ref, sem)

    @pl.when(step == 0)
    def _():
        late_copy.start()

    width = w_out_ref.shape[0]
    head_dim = width // HEADS
    scale = head_dim ** (-0.5)
    rows = hidden_ref.shape[0] * hidden_ref.shape[2]
    grad_mixed_ref[...] = dot(w_out_ref[...], grad_branch_ref[0], 1, 1).astype(BF)
    for head in range(HEADS):
        low = head * head_dim
        value = qkv_ref[0, 2 * width + low : 2 * width + low + head_dim, :]
        grad_mixed = grad_mixed_ref[low : low + head_dim, :]
        grad_probs_ref[head] = dot(value, grad_mixed, 0, 0)
        grad_probs_extra_ref[head] = dot(value_extra_ref[0, head], grad_mixed, 1, 0)
    for head in range(HEADS):
        probs = probs_ref[0, head].astype(F32)
        probs_extra = probs_extra_ref[0, head].astype(F32)
        grad_probs, grad_probs_extra = grad_probs_ref[head], grad_probs_extra_ref[head]
        common = row_sum(grad_probs * probs) + row_sum(grad_probs_extra * probs_extra)
        grad_scores_ref[head] = (probs * (grad_probs - common)).astype(BF)
        grad_scores_extra_ref[head] = (probs_extra * (grad_probs_extra - common)).astype(BF)
    for head in range(HEADS):
        low = head * head_dim
        query = qkv_ref[0, low : low + head_dim, :]
        key = qkv_ref[0, width + low : width + low + head_dim, :]
        grad_mixed = grad_mixed_ref[low : low + head_dim, :]
        grad_scores, grad_scores_extra = grad_scores_ref[head], grad_scores_extra_ref[head]
        grad_query = dot(key, grad_scores, 1, 0) + dot(
            key_extra_ref[0, head], grad_scores_extra, 0, 0
        )
        grad_key = dot(query, grad_scores, 1, 1)
        grad_value = dot(grad_mixed, probs_ref[0, head], 1, 1)
        grad_key_extra_ref[0, head] = dot(grad_scores_extra, query, 1, 1) * scale
        grad_value_extra_ref[0, head] = dot(probs_extra_ref[0, head], grad_mixed, 1, 1)
        grad_qkv_ref[0, low : low + head_dim, :] = (grad_query * scale).astype(BF)
        grad_qkv_ref[0, width + low : width + low + head_dim, :] = (grad_key * scale).astype(BF)
        grad_qkv_ref[0, 2 * width + low : 2 * width + low + head_dim, :] = grad_value.astype(BF)

    @pl.when(step == 0)
    def _():
        late_copy.wait()

    grad_normed = dot(grad_qkv_ref[0], w_qkv_ref[...], 0, 1)
    unit, scaled = norm_parts(hidden_ref[...].reshape(rows, width).astype(F32))

    @pl.when(pl.program_id(0) == 0)
    def _():
        sums_ref[...] = jnp.zeros_like(sums_ref) if opening else sums_in_ref[...]

    sums_ref[0:1] += row_sum(grad_normed * unit)
    sums_ref[1:2] += row_sum(grad_normed)
    grad_hidden0 = grad_hidden1_ref[0] + norm_back(grad_normed * flat(gain_ref), unit, scaled)
    grad_low = grad_hidden0.astype(BF)
    sums_ref[2:3] += row_sum(grad_low.astype(F32))
    grad_hidden0_ref[...] = grad_low.reshape(grad_hidden0_ref.shape)


def extra_back_kernel(
    share,
    hidden_ref,
    gain_ref,
    w_key_ref,
    w_value_ref,
    latent_ref,
    sums_in_ref,
    *rest,
):
    keys, values = rest[:share], rest[share : 2 * share]
    pairs_ref, grad_ref, sums_ref, back_ref = rest[-4:]
    width = hidden_ref.shape[1]

    def rows_of(refs):
        return jnp.concatenate(
            [jnp.concatenate([ref[0, head] for ref in refs], 0) for head in range(HEADS)], 1
        ).astype(BF)

    grad_key, grad_value = rows_of(keys), rows_of(values)
    pairs_ref[0] = grad_key
    pairs_ref[1] = grad_value
    grad_normed = dot(grad_key, w_key_ref[...], 1, 1) + dot(grad_value, w_value_ref[...], 1, 1)
    unit, scaled = norm_parts(hidden_ref[...])
    grad = norm_back(grad_normed * flat(gain_ref), unit, scaled).astype(BF)
    grad_ref[...] = grad
    wide = grad.astype(F32)
    sums_ref[0:1] = sums_in_ref[0:1] + row_sum(grad_normed * unit)
    sums_ref[1:2] = sums_in_ref[1:2] + row_sum(grad_normed)
    sums_ref[2:3] = sums_in_ref[2:3] + row_sum(wide)
    real = [wide[i * EXTRA_PAD : i * EXTRA_PAD + 2] for i in range(share)]
    fill = back_ref.shape[1] - 2 * share - latent_ref.shape[1]
    for group in range(back_ref.shape[0]):
        block = real + [latent_ref[group].astype(F32), jnp.zeros((fill, width), F32)]
        back_ref[group] = jnp.concatenate(block, 0).astype(BF)


def late_weight_kernel(
    own,
    normed_ref,
    normed_extra_ref,
    pairs_ref,
    joined_hbm,
    grad_ref,
    joined_extra_ref,
    grad_extra_ref,
    grad_qkv_0_ref,
    grad_qkv_1_ref,
    grad_qkv_2_ref,
    core_ref,
    *rest,
):
    joined_ref, sem = rest[-2:]
    rest = rest[:-2]
    step = pl.program_id(0)
    split = can_split(own)
    late_copy = pltpu.make_async_copy(joined_hbm, joined_ref, sem)

    @pl.when(step == 0)
    def _():
        late_copy.start()

    @pl.when(step == 3)
    def _():
        late_copy.wait()

    groups, items, _, width = joined_ref.shape
    local = (grad_ref.shape[1] - 16) // items

    @pl.when(step < 3)
    def _():
        total = dot(normed_extra_ref[...], pairs_ref[0], 0, 0)
        total = total * jnp.where(step == 0, 0.0, 1.0)
        for item, ref in enumerate((grad_qkv_0_ref, grad_qkv_1_ref, grad_qkv_2_ref)):
            total = total + dot(normed_ref[item], ref[0], 0, 1)
        half = width // 2
        for side in range(2):
            piece = total[:, side * half : (side + 1) * half]
            if split:
                store_split(piece, own, (rest[-2].at[side], rest[-1].at[side], core_ref))
            else:
                store_split(piece, own, (rest[-1].at[side],))

    @pl.when(step >= 3)
    def _():
        grad = grad_ref[:, : items * local].reshape(groups * items * local, -1)
        for side in range(2):
            joined = joined_ref[:, :, side * local : (side + 1) * local]
            joined = joined.reshape(groups * items * local, width)
            extra = joined_extra_ref[:, side * width : (side + 1) * width]
            total = dot(joined, grad, 0, 0) + dot(extra, grad_extra_ref[...], 0, 0)
            if not split:
                rest[-1][side] = total.astype(BF)
                continue
            pairs = total.reshape(width // (4 * own), 2, 2, own, total.shape[1])
            first = core_ref[0] == 0
            count = pairs.shape[0]
            for part in range(2):
                low, high = pairs[:, 0, part], pairs[:, 1, part]
                where = pl.ds(side * count, count)
                rest[-2][part, where] = jnp.where(first, low, high).astype(BF)
                rest[-1][part, where] = jnp.where(first, high, low).astype(BF)


def token_kernel(back_ref, w_skip_ref, tokens_ref, skip_ref, extra_ref):
    width = w_skip_ref.shape[1]
    items = tokens_ref.shape[0]
    local = tokens_ref.shape[1] * tokens_ref.shape[2]
    body = items // back_ref.shape[0] * local
    grad = back_ref[:, :body].reshape(items * local, width)
    tokens_ref[...] = dot(grad, w_skip_ref[:width], 1, 1).astype(BF).reshape(tokens_ref.shape)
    skip_ref[...] = dot(grad, w_skip_ref[width:], 1, 1).astype(BF).reshape(skip_ref.shape)
    extra = back_ref[:, body:].reshape(-1, width)
    extra_ref[...] = dot(extra, w_skip_ref[...], 1, 1).astype(BF).reshape(extra_ref.shape)


def fold_matrix(shape, low, wide, period):
    row = lax.broadcasted_iota(jnp.int32, shape, 0)
    col = lax.broadcasted_iota(jnp.int32, shape, 1)
    return jnp.where((col >= low) & (col < low + wide) & (row % period == col - low), 1.0, 0.0)


def pack_kernel(
    sums_attend_ref,
    sums_up_ref,
    sums_final_ref,
    head_sum_ref,
    grad_head_ref,
    conv_sum_ref,
    conv_bias_ref,
    table_ref,
    *rest,
):
    stacked_ref, shared_ref = rest[-2:]
    items, lanes, _ = head_sum_ref.shape
    values = lanes // items
    exact = functools.partial(
        jnp.dot, precision=lax.Precision.HIGHEST, preferred_element_type=F32
    )
    stacked_ref[0:1] = sums_attend_ref[2:3]
    stacked_ref[1:2] = sums_attend_ref[0:1]
    stacked_ref[2:3] = sums_attend_ref[1:2]
    stacked_ref[3:4] = sums_up_ref[2:3]
    stacked_ref[4:6] = sums_up_ref[0:2]
    stacked_ref[6:7] = sums_final_ref[2:3]
    stacked_ref[7:9] = sums_final_ref[0:2]
    head = head_sum_ref[0, 0:values]
    for item in range(1, items):
        head = head + head_sum_ref[item, item * values : (item + 1) * values]
    stacked_ref[9 : 9 + values] = head
    row = lax.broadcasted_iota(jnp.int32, (8, lanes), 0)
    col = lax.broadcasted_iota(jnp.int32, (8, lanes), 1)
    left = jnp.where(col % 4 == row, 1.0, 0.0)
    shared = jnp.zeros((8, 128), F32)
    for tap in range(9):
        picked = conv_sum_ref[0] * table_ref[0, tap].astype(F32)
        for k in range(1, 9):
            picked = picked + conv_sum_ref[k] * table_ref[k, tap].astype(F32)
        shared = shared + exact(exact(left, picked), fold_matrix((lanes, 128), 4 * tap, 4, 4))
    bias = exact(grad_head_ref[...], fold_matrix((lanes, 128), 64, values, values))
    bias = bias + exact(conv_bias_ref[...], fold_matrix((lanes, 128), 96, 4, 4))
    first = lax.broadcasted_iota(jnp.int32, (8, 128), 0) == 0
    shared_ref[...] = shared + jnp.where(first, bias, 0.0)


def whole(shape):
    return pl.BlockSpec(shape, lambda *_: (0,) * len(shape), pipeline_mode=pl.Buffered(1))


def params():
    return pltpu.CompilerParams(vmem_limit_bytes=60 * MIB)


def cost(flops, moved, transcendentals=0):
    del flops, moved, transcendentals
    return pl.CostEstimate(flops=1024, bytes_accessed=1024, transcendentals=0)


def sds(shape, dtype):
    return jax.ShapeDtypeStruct(shape, dtype)


def swap(block, axis, gap):
    count = lax.axis_size(axis)
    return lax.ppermute(block, axis, [(i, i ^ gap) for i in range(count)])


def serve_kernel(tasks, places_ref, *refs):
    del places_ref
    inputs = sum(len(parts) for task in tasks for parts in task["sides"])
    outs = refs[len(refs) - sum(len(task["outs"]) for task in tasks) :]
    at, out_at = 0, 0
    del inputs
    for task in tasks:
        values = []
        for parts in task["sides"]:
            total = refs[at][...].astype(F32)
            for k in range(1, len(parts)):
                total = total + refs[at + k][...].astype(F32)
            at += len(parts)
            values.append(total)
        task["emit"](values, outs[out_at : out_at + len(task["outs"])])
        out_at += len(task["outs"])


def serve(tasks, after, name, places):
    arrays, specs = [], []
    for task in tasks:
        for parts in task["sides"]:
            for array, starts, sizes in parts:
                index = tuple(
                    start // size if isinstance(start, int) else start
                    for start, size in zip(starts, sizes, strict=True)
                )

                def where(_, ref, index=index):
                    return tuple(i if isinstance(i, int) else ref[i[0]] for i in index)

                arrays.append(array)
                specs.append(pl.BlockSpec(tuple(sizes), where))
    outs = [out for task in tasks for out in task["outs"]]
    moved = sum(2 * int(np.prod(spec.block_shape)) for spec in specs)
    return pl.pallas_call(
        functools.partial(serve_kernel, tasks),
        grid_spec=pltpu.PrefetchScalarGridSpec(
            num_scalar_prefetch=1,
            grid=(1,),
            in_specs=specs + [pl.BlockSpec(memory_space=pl.ANY)] * len(after),
            out_specs=[
                pl.BlockSpec(out.shape, lambda _, ref, n=len(out.shape): (0,) * n) for out in outs
            ],
        ),
        out_shape=outs,
        compiler_params=params(),
        cost_estimate=cost(moved, 2 * moved),
        name=name,
    )(places, *arrays, *after)


def emit_low(values, outs):
    for value, out in zip(values, outs, strict=True):
        out[...] = value.astype(BF)


def place_table():
    own = [lax.axis_index("ty"), lax.axis_index("tx") // 2]
    batch = lax.axis_size("batch")
    own += [(lax.axis_index("batch") >> bit) % 2 for bit in range(batch.bit_length() - 1)]
    return jnp.stack([v for place in own for v in (place, 1 - place)]).astype(jnp.int32)


class Sum:
    def __init__(self, grads, units, inner, columns, table):
        batch = lax.axis_size("batch")
        bits = batch.bit_length() - 1
        rows = sum(grad.size for grad in grads) // (units * columns)
        self.own = rows // lax.axis_size(ALL) // inner
        self.columns = columns
        self.table = table
        self.dims = [units] + [2] * bits + [2, 2, 2, inner, self.own, columns]
        self.moves = {"y": bits + 1, "x": bits + 2, "c": bits + 3}
        self.places = {"y": (0, 1), "x": (2, 3)}
        self.links = {"y": ("ty", 1), "x": ("tx", 2), "c": ("tx", 1)}
        for bit in range(bits):
            self.moves[bit] = bits - bit
            self.places[bit] = (4 + 2 * bit, 5 + 2 * bit)
            self.links[bit] = ("batch", 1 << bit)
        self.cut = 0 if units > 1 else len(self.dims) - 3
        self.half = self.dims[self.cut] // 2
        tail = list(range(bits))
        self.orders = [["x", "y"] + tail, ["y", "x"] + tail]
        at = self.moves["c"]
        if len(grads) == 1:
            grad = grads[0].reshape(self.dims)
            core = lax.axis_index("tx") % 2
            keep = lax.dynamic_slice_in_dim(grad, core, 1, at)
            send = lax.dynamic_slice_in_dim(grad, 1 - core, 1, at)
        else:
            halved = list(self.dims)
            halved[at] = 1
            keep, send = grads[0].reshape(halved), grads[1].reshape(halved)
        self.sent = [send]
        received = swap(send, *self.links["c"])
        self.parts = [[(keep, ("c",)), (received, ("c",))] for _ in range(2)]
        self.done = [["c"], ["c"]]

    def pick(self, part, chosen, side):
        array, fixed = part
        starts, sizes = [0] * array.ndim, list(array.shape)
        for move, where in chosen.items():
            if move not in fixed:
                starts[self.moves[move]] = where
                sizes[self.moves[move]] = 1
        if "side" not in fixed:
            starts[self.cut], sizes[self.cut] = side * self.half, self.half
        return array, starts, sizes

    def task(self):
        if self.orders[0][0] == self.orders[1][0]:
            return self.joint_task()
        sides, outs = [], []
        for side in range(2):
            move = self.orders[side][0]
            chosen = {m: self.places[m][:1] for m in self.done[side] if m != "c"}
            chosen[move] = self.places[move][1:]
            parts = [self.pick(part, chosen, side) for part in self.parts[side]]
            sides.append(parts)
            outs.append(sds(tuple(parts[0][2]), BF))
        return {"sides": sides, "outs": outs, "emit": emit_low}

    def joint_task(self):
        move = self.orders[0][0]
        sides = []
        for side in range(2):
            chosen = {m: self.places[m][:1] for m in self.done[side] if m != "c"}
            chosen[move] = self.places[move][1:]
            sides.append([self.pick(part, chosen, side) for part in self.parts[side]])
        shape = list(sides[0][0][2])
        shape[self.cut] = 2 * self.half
        cut, half = self.cut, self.half

        def emit(values, outs):
            for side in range(2):
                index = [slice(None)] * len(shape)
                index[cut] = slice(side * half, (side + 1) * half)
                outs[0][tuple(index)] = values[side].astype(BF)

        return {"sides": sides, "outs": [sds(tuple(shape), BF)], "emit": emit}

    def accept(self, sent):
        if len(sent) == 1:
            move = self.orders[0][0]
            received = swap(sent[0], *self.links[move])
            for side in range(2):
                self.orders[side].pop(0)
                self.done[side].append(move)
                self.parts[side].append((received, tuple(self.done[side])))
            return
        for side in range(2):
            move = self.orders[side].pop(0)
            self.done[side].append(move)
            received = swap(sent[side], *self.links[move])
            self.parts[side].append((received, ("side",) + tuple(self.done[side])))

    def last_task(self, layout):
        sides = []
        for side in range(2):
            chosen = {m: self.places[m][:1] for m in self.done[side] if m != "c"}
            sides.append([self.pick(part, chosen, side) for part in self.parts[side]])
        shapes, units = layout
        own, columns, half = self.own, self.columns, self.half

        def emit(values, outs):
            for side in range(2):
                value = values[side].reshape(half, own, columns)
                for k in range(half):
                    out, row, col = units[side * half + k]
                    outs[out][
                        row * own : (row + 1) * own, col * columns : (col + 1) * columns
                    ] = value[k]

        outs = [sds((r * own, c * columns), F32) for r, c in shapes]
        return {"sides": sides, "outs": outs, "emit": emit}


def run_tasks(sums, after, name):
    places = sums[0][0].table
    tasks = []
    for sum_, layout in sums:
        tasks.append(sum_.task() if sum_.orders[0] else sum_.last_task(layout))
    outs = serve(tasks, after, name, places)
    results, at = [], 0
    for (sum_, _), task in zip(sums, tasks, strict=True):
        got = outs[at : at + len(task["outs"])]
        at += len(task["outs"])
        if sum_.orders[0]:
            sum_.accept(got)
        else:
            results.append(got)
    return outs, results


def conv_map():
    table = np.zeros((9, 9, 4, 4), np.float32)
    for row_off in range(3):
        for col_off in range(3):
            for p in range(4):
                for q in range(4):
                    i = 2 * (row_off - 1) + p // 2 - q // 2 + 1
                    j = 2 * (col_off - 1) + p % 2 - q % 2 + 1
                    if 0 <= i < 3 and 0 <= j < 3:
                        table[i * 3 + j, row_off * 3 + col_off, p, q] = 1.0
    return table


def conv_lanes(share):
    table = conv_map().transpose(1, 0, 2, 3)
    wide = np.kron(np.eye(share, dtype=np.float32), np.ones((16, 16), np.float32))
    small = np.repeat(np.repeat(table, 4, 2), 4, 3)
    return np.tile(small, (1, 1, share, share)) * wide


def per_device(
    tokens,
    skip_tokens,
    extra_tokens,
    extra_skip,
    timesteps,
    target,
    w_skip,
    b_skip,
    norm1_gain,
    norm1_shift,
    w_qkv,
    w_out,
    b_out,
    norm2_gain,
    norm2_shift,
    w_up,
    b_up,
    w_down,
    b_down,
    final_gain,
    final_shift,
    w_head,
    b_head,
    w_conv,
    b_conv,
):
    items, rows, cols, width = tokens.shape
    hidden_units = w_up.shape[1]
    local = rows * cols
    patch_values = w_head.shape[1]
    chans = w_conv.shape[3]
    devices = lax.axis_size(ALL)
    groups = lax.axis_size(PLANE)
    place = lax.axis_index(PLANE)
    share = items // groups
    per_item = groups * local
    count = share * per_item
    head_dim = width // HEADS
    height, breadth = rows * PATCH, cols * PATCH

    def row(vector):
        return vector.astype(F32).reshape(1, -1)

    def to_items(array):
        return lax.all_to_all(array, PLANE, split_axis=0, concat_axis=0, tiled=True)

    some = 12
    joined_rows = 2 * local + 8
    tile_block = pl.BlockSpec((some, rows, cols, width), lambda i: (i, 0, 0, 0))
    flat_block = pl.BlockSpec((some, local, width), lambda i: (i, 0, 0))
    hidden0, joined = pl.pallas_call(
        merge_kernel,
        grid=(items // some,),
        in_specs=[tile_block, tile_block, whole((2 * width, width)), whole((width,))],
        out_specs=[flat_block, pl.BlockSpec((some, joined_rows, width), lambda i: (i, 0, 0))],
        out_shape=[sds((items, local, width), BF), sds((items, joined_rows, width), BF)],
        compiler_params=params(),
        cost_estimate=cost(items * local * 4 * width * width, 11e6),
        name="merge",
    )(tokens, skip_tokens, w_skip, b_skip)
    hidden0 = to_items(hidden0)
    hidden0 = hidden0.reshape(groups, share, local, width)
    target_patches = (
        target.reshape(items, rows, PATCH, cols, PATCH, chans)
        .transpose(0, 1, 3, 2, 4, 5)
        .reshape(items, local * patch_values)
    )
    high = lax.reduce_precision(target_patches, 8, 7)
    middle = lax.reduce_precision(target_patches - high, 8, 7)
    low = target_patches - high - middle
    thirds = jnp.concatenate([high, middle, low], 1).astype(BF).reshape(items, -1, width)
    joined = lax.dynamic_update_slice(joined, thirds, (0, 2 * local, 0))

    start = place * share
    joined_extra = jnp.concatenate(
        [
            lax.dynamic_slice_in_dim(extra_tokens, start, share, 0),
            lax.dynamic_slice_in_dim(extra_skip, start, share, 0),
        ],
        2,
    )
    extra_rows = share * EXTRA_PAD
    joined_extra = jnp.pad(joined_extra, ((0, 0), (0, EXTRA_PAD - 2), (0, 0)))
    joined_extra = joined_extra.reshape(extra_rows, 2 * width)
    hidden_extra = dot(joined_extra, w_skip, 1, 0) + row(b_skip)
    unit_extra, _ = norm_parts(hidden_extra)
    normed_extra = (unit_extra * row(norm1_gain) + row(norm1_shift)).astype(BF)
    pairs_extra = dot(normed_extra, w_qkv[:, width:], 1, 0).astype(BF)

    def by_head(block):
        return block.reshape(share, EXTRA_PAD, HEADS, head_dim).transpose(0, 2, 1, 3)

    key_extra = by_head(pairs_extra[:, :width])
    value_extra = by_head(pairs_extra[:, width:])

    weight = lax.dynamic_slice_in_dim(noise_weight(timesteps), start, share, 0)
    lanes = share * patch_values
    spread = jnp.tile(w_conv.reshape(9, chans, chans), (1, lanes // chans, lanes // chans))
    kernel = jnp.sum(jnp.asarray(conv_lanes(share)) * spread[None].astype(F32), 1).astype(BF)
    table = place_table()
    joined, table, joined_extra = lax.optimization_barrier(
        (joined, table, joined_extra, key_extra, value_extra, kernel, weight, normed_extra)
    )[:3]
    joined = to_items(joined).reshape(groups, share, joined_rows, width)
    thirds = joined[:, :, 2 * local : 2 * local + thirds.shape[1]].astype(F32)
    thirds = thirds.reshape(groups, share, 3, local, patch_values)
    target_own = (
        (thirds[:, :, 0] + thirds[:, :, 1] + thirds[:, :, 2])
        .transpose(0, 2, 1, 3)
        .reshape(per_item, share * patch_values)
    )

    vec = whole((width,))
    item_block = pl.BlockSpec((groups, 1, local, width), lambda i: (0, i, 0, 0))

    def per_share(*shape):
        return pl.BlockSpec((1,) + shape, lambda i: (i,) + (0,) * len(shape))

    normed1, qkv, probs, probs_extra, mixed, hidden1 = pl.pallas_call(
        attend_kernel,
        grid=(share,),
        in_specs=[
            item_block,
            per_share(HEADS, EXTRA_PAD, head_dim),
            per_share(HEADS, EXTRA_PAD, head_dim),
            vec,
            vec,
            vec,
            whole((width, 3 * width)),
            whole((width, width)),
        ],
        out_specs=[
            per_share(per_item, width),
            per_share(3 * width, per_item),
            per_share(HEADS, per_item, per_item),
            per_share(HEADS, EXTRA_PAD, per_item),
            per_share(width, per_item),
            per_share(per_item, width),
        ],
        out_shape=[
            sds((share, per_item, width), BF),
            sds((share, 3 * width, per_item), BF),
            sds((share, HEADS, per_item, per_item), BF),
            sds((share, HEADS, EXTRA_PAD, per_item), BF),
            sds((share, width, per_item), BF),
            sds((share, per_item, width), F32),
        ],
        scratch_shapes=[
            pltpu.VMEM((HEADS, per_item, per_item), F32),
            pltpu.VMEM((HEADS, EXTRA_PAD, per_item), F32),
        ],
        compiler_params=params(),
        cost_estimate=cost(count * (8 * width * width + 16 * per_item * width), 25e6, 3e6),
        name="attend",
    )(
        hidden0,
        key_extra,
        value_extra,
        norm1_gain,
        norm1_shift,
        b_out,
        w_qkv,
        w_out,
    )
    hidden1 = hidden1.reshape(count, width)

    chunk = width
    chunks = hidden_units // chunk
    by_col = pl.BlockSpec((1, count, chunk), lambda j: (j, 0, 0))
    active, slope, normed2, hidden2 = pl.pallas_call(
        forward_kernel,
        grid=(chunks,),
        in_specs=[
            whole((count, width)),
            vec,
            vec,
            whole((hidden_units,)),
            vec,
            pl.BlockSpec((width, chunk), lambda j: (0, j)),
            pl.BlockSpec((chunk, width), lambda j: (j, 0)),
        ],
        out_specs=[by_col, by_col, whole((count, width)), whole((count, width))],
        out_shape=[
            sds((chunks, count, chunk), BF),
            sds((chunks, count, chunk), BF),
            sds((count, width), BF),
            sds((count, width), F32),
        ],
        scratch_shapes=[pltpu.VMEM((chunks, chunk), F32)],
        compiler_params=params(),
        cost_estimate=cost(count * 4 * width * hidden_units, 25e6, 5e6),
        name="forward",
    )(hidden1, norm2_gain, norm2_shift, b_up, b_down, w_up, w_down)
    (
        result,
        grad_hidden2,
        grad_down,
        grad_head,
        sums_final,
        head_sum,
        conv_sum,
        conv_bias,
    ) = pl.pallas_call(
        functools.partial(turn_kernel, rows, cols, lax.axis_size("tx")),
        grid=(1,),
        in_specs=[
            whole((count, width)),
            vec,
            vec,
            whole((patch_values, width)),
            whole((9, lanes, lanes)),
            whole((patch_values,)),
            whole((chans,)),
            whole((share,)),
            whole((per_item, lanes)),
            pl.BlockSpec(memory_space=pl.ANY),
        ],
        out_specs=[
            whole((per_item, lanes)),
            whole((count, width)),
            whole((count, width)),
            whole((1, lanes)),
            whole((8, width)),
            whole((share, lanes, width)),
            whole((9, lanes, lanes)),
            whole((1, lanes)),
        ],
        out_shape=[
            sds((per_item, lanes), BF),
            sds((count, width), F32),
            sds((count, width), BF),
            sds((1, lanes), F32),
            sds((8, width), F32),
            sds((share, lanes, width), F32),
            sds((9, lanes, lanes), F32),
            sds((1, lanes), F32),
        ],
        scratch_shapes=[pltpu.VMEM((count, width), F32)],
        compiler_params=params(),
        cost_estimate=cost(1e9, 10e6),
        name="turn",
    )(
        hidden2,
        final_gain,
        final_shift,
        w_head.T,
        kernel,
        b_head,
        b_conv,
        weight,
        target_own,
        joined,
    )

    any_place = pl.BlockSpec(memory_space=pl.ANY)
    core = lax.axis_index("tx") % 2
    core = core.astype(jnp.int32).reshape(1)
    core_spec = pl.BlockSpec(memory_space=pltpu.SMEM)

    def split_outs(units, rows, block_rows, own, cols, index):
        if can_split(own):
            spec = pl.BlockSpec(
                (units, block_rows // (2 * own), own, cols), lambda j: index(j) + (0, 0)
            )
            return spec, lambda n: sds((n, rows // (2 * own), own, cols), BF), 2
        spec = pl.BlockSpec((units, block_rows, cols), lambda j: index(j) + (0,))
        return spec, lambda n: sds((n, rows, cols), BF), 1

    own = width // devices
    half = width // 2
    units = 2 * chunks + 2
    chain_down = CHAIN_DOWN and can_split(own)
    if chain_down:
        down_specs = [
            pl.BlockSpec((8, chunk // (8 * own), own, half), lambda j: (0, j, 0, 0))
        ] * 2
        down_shapes = [sds((8, width // (2 * own), own, half), BF)] * 2
    else:
        down_specs = [pl.BlockSpec((chunk, width), lambda j: (j, 0))]
        down_shapes = [sds((hidden_units, width), BF)]
    grad_w_down = pl.pallas_call(
        functools.partial(down_kernel, own, chain_down),
        grid=(chunks,),
        in_specs=[by_col, whole((count, width)), core_spec],
        out_specs=down_specs,
        out_shape=down_shapes,
        compiler_params=params(),
        cost_estimate=cost(count * 2 * width * hidden_units, 11e6),
        name="down_weight",
    )(active, grad_down, core)
    if chain_down:
        sum_down = Sum(grad_w_down, 8, 1, half, table)
    else:
        out_down = lax.psum_scatter(
            grad_w_down[0], ALL, scatter_dimension=0, tiled=True
        ).astype(F32)

    up_spec, up_shape, up_outs = split_outs(2, width, width, own, half, lambda j: (j, 0))

    def held_col(j):
        return jnp.minimum(j, chunks - 1)

    grad_b_up, grad_hidden1, grad_branch, sums_up, *grad_w_up = pl.pallas_call(
        functools.partial(up_kernel, own),
        grid=(chunks + 1,),
        in_specs=[
            pl.BlockSpec((1, count, chunk), lambda j: (held_col(j), 0, 0)),
            whole((count, width)),
            pl.BlockSpec((chunk, width), lambda j: (held_col(j), 0)),
            pl.BlockSpec((width, chunk), lambda j: (0, held_col(j))),
            whole((count, width)),
            any_place,
            vec,
            any_place,
            any_place,
            core_spec,
        ]
        + [any_place] * len(grad_w_down),
        out_specs=[
            pl.BlockSpec((1, 8, chunk), lambda j: (held_col(j), 0, 0)),
            whole((count, width)),
            whole((count, width)),
            whole((8, width)),
        ]
        + [up_spec] * up_outs,
        out_shape=[
            sds((chunks, 8, chunk), F32),
            sds((count, width), F32),
            sds((count, width), BF),
            sds((8, width), F32),
        ]
        + [up_shape(units)] * up_outs,
        scratch_shapes=[
            pltpu.VMEM((count, width), F32),
            pltpu.VMEM((count, width), F32),
            pltpu.VMEM((count, width), F32),
            pltpu.VMEM((share, width, per_item), BF),
            pltpu.SemaphoreType.DMA((3,)),
        ],
        compiler_params=params(),
        cost_estimate=cost(count * (6 * hidden_units + 2 * width) * width, 25e6),
        name="up_weight",
    )(
        slope,
        grad_down,
        w_down,
        w_up,
        normed2,
        hidden1,
        norm2_gain,
        grad_hidden2,
        mixed,
        core,
        *grad_w_down,
    )
    if can_split(own):
        sum_up = Sum(grad_w_up, units, 1, half, table)
    down_layout = ([(4, 2)], [(0, k // 2, k % 2) for k in range(8)])
    up_layout = (
        [(1, 2 * chunks), (1, 2)],
        [(0, 0, k) for k in range(2 * chunks)] + [(1, 0, 0), (1, 0, 1)],
    )
    late_layout = (
        [(1, 6), (2, 2)],
        [(0, 0, k) for k in range(6)] + [(1, 0, 0), (1, 1, 0), (1, 0, 1), (1, 1, 1)],
    )

    after = sum_up.sent if can_split(own) else []
    if chain_down:
        after, _ = run_tasks([(sum_down, None)], after, "serve_0")
        early = [(sum_down, None)]
    else:
        early = []
    grad_qkv, grad_key_extra, grad_value_extra = [], [], []
    sums_attend = sums_up
    grad_hidden0 = None
    back_rows = share * local + 16
    for first, number in ((0, share - 1), (share - 1, 1)):

        def one(*shape, first=first):
            return pl.BlockSpec((1,) + shape, lambda i: (first + i,) + (0,) * len(shape))

        def own_item(*shape):
            return pl.BlockSpec((1,) + shape, lambda i: (i,) + (0,) * len(shape))

        held = [grad_hidden0] if first else []
        outs = pl.pallas_call(
            functools.partial(attend_back_kernel, first == 0),
            grid=(number,),
            in_specs=[
                pl.BlockSpec(
                    (groups, 1, local, width), lambda i, first=first: (0, first + i, 0, 0)
                ),
                one(per_item, width),
                one(per_item, width),
                one(3 * width, per_item),
                one(HEADS, per_item, per_item),
                one(HEADS, EXTRA_PAD, per_item),
                one(HEADS, EXTRA_PAD, head_dim),
                one(HEADS, EXTRA_PAD, head_dim),
                vec,
                any_place,
                whole((width, width)),
                whole((8, width)),
            ]
            + [any_place] * (len(held) + len(after)),
            out_specs=[
                own_item(3 * width, per_item),
                own_item(HEADS, EXTRA_PAD, head_dim),
                own_item(HEADS, EXTRA_PAD, head_dim),
                pl.BlockSpec((groups, local, width), lambda i, first=first: (0, first + i, 0)),
                whole((8, width)),
            ],
            out_shape=[
                sds((number, 3 * width, per_item), BF),
                sds((number, HEADS, EXTRA_PAD, head_dim), F32),
                sds((number, HEADS, EXTRA_PAD, head_dim), F32),
                sds((groups, back_rows, width), BF),
                sds((8, width), F32),
            ],
            input_output_aliases={12: 3} if first else {},
            scratch_shapes=[
                pltpu.VMEM((width, per_item), BF),
                pltpu.VMEM((HEADS, per_item, per_item), F32),
                pltpu.VMEM((HEADS, EXTRA_PAD, per_item), F32),
                pltpu.VMEM((HEADS, per_item, per_item), BF),
                pltpu.VMEM((HEADS, EXTRA_PAD, per_item), BF),
                pltpu.VMEM((width, 3 * width), BF),
                pltpu.SemaphoreType.DMA,
            ],
            compiler_params=params(),
            cost_estimate=cost(
                per_item * (8 * width * width + 40 * per_item * width), 12e6
            ),
            name="attend_back",
        )(
            hidden0,
            grad_hidden1.reshape(share, per_item, width),
            grad_branch.reshape(share, per_item, width),
            qkv,
            probs,
            probs_extra,
            key_extra,
            value_extra,
            norm1_gain,
            w_qkv,
            w_out,
            sums_attend,
            *held,
            *after,
        )
        grad_qkv += [outs[0]] * number
        grad_key_extra += [outs[1]] * number
        grad_value_extra += [outs[2]] * number
        grad_hidden0, sums_attend = outs[3], outs[4]
        after = []
        if can_split(own) and not first:
            after, _ = run_tasks([(sum_up, None)] + early, [sums_attend], "serve_1")
    places_of = [i for number in (share - 1, 1) for i in range(number)]

    latent = result.reshape(groups, local * share * patch_values // width, width)
    pairs_extra, grad_extra, sums_attend, grad_back = pl.pallas_call(
        functools.partial(extra_back_kernel, share),
        grid=(1,),
        in_specs=[
            whole((extra_rows, width)),
            vec,
            pl.BlockSpec((width, width), lambda *_: (0, 1)),
            pl.BlockSpec((width, width), lambda *_: (0, 2)),
            whole(latent.shape),
            whole((8, width)),
        ]
        + [
            pl.BlockSpec((1, HEADS, EXTRA_PAD, head_dim), lambda *_, at=at: (at, 0, 0, 0))
            for at in places_of * 2
        ]
        + [any_place] * (1 + len(after)),
        out_specs=[
            whole((2, extra_rows, width)),
            whole((extra_rows, width)),
            whole((8, width)),
            pl.BlockSpec((groups, 16, width), lambda *_: (0, share * local // 16, 0)),
        ],
        out_shape=[
            sds((2, extra_rows, width), BF),
            sds((extra_rows, width), BF),
            sds((8, width), F32),
            sds((groups, back_rows, width), BF),
        ],
        input_output_aliases={6 + 2 * share: 3},
        compiler_params=params(),
        cost_estimate=cost(1e8, 5e6),
        name="extra_back",
    )(
        hidden_extra,
        norm1_gain,
        w_qkv,
        w_qkv,
        latent,
        sums_attend,
        *grad_key_extra,
        *grad_value_extra,
        grad_hidden0,
        *after,
    )

    late_spec, late_shape, late_outs = split_outs(
        2, width, width, own, width // 2, lambda j: (j, 0)
    )

    def skip_col(j):
        return jnp.maximum(j - 3, 0)

    def qkv_row(j):
        return jnp.minimum(j, 2)

    half = width // 2
    grad_late = pl.pallas_call(
        functools.partial(late_weight_kernel, own),
        grid=(5,),
        in_specs=[
            whole((share, per_item, width)),
            whole((extra_rows, width)),
            pl.BlockSpec(
                (1, extra_rows, width), lambda j: (jnp.clip(j - 1, 0, 1), 0, 0)
            ),
            any_place,
            pl.BlockSpec((groups, back_rows, half), lambda j: (0, 0, skip_col(j))),
            whole((extra_rows, 2 * width)),
            pl.BlockSpec((extra_rows, half), lambda j: (0, skip_col(j))),
        ]
        + [
            pl.BlockSpec((1, width, per_item), lambda j, at=at: (at, qkv_row(j), 0))
            for at in places_of
        ]
        + [core_spec],
        out_specs=[late_spec] * late_outs,
        out_shape=[late_shape(10)] * late_outs,
        scratch_shapes=[pltpu.VMEM(joined.shape, BF), pltpu.SemaphoreType.DMA],
        compiler_params=params(),
        cost_estimate=cost(count * 10 * width * width, 12e6),
        name="late_weight",
    )(
        normed1,
        normed_extra,
        pairs_extra,
        joined,
        grad_back,
        joined_extra,
        grad_extra,
        *grad_qkv,
        core,
    )

    def hold(values, *others):
        return lax.optimization_barrier((values, others))[0]

    if can_split(own):
        after, _ = run_tasks([(sum_up, None)] + early, [grad_late[0]], "serve_2")
        grad_late = [grad_late[0], hold(grad_late[1], after)]
        sum_late = Sum(grad_late, 10, 1, half, table)
    else:
        after = list(grad_late)

    stacked_count = 9 + patch_values
    stacked, shared = pl.pallas_call(
        pack_kernel,
        in_specs=[pl.BlockSpec(memory_space=pltpu.VMEM)] * 8 + [any_place] * len(after),
        out_specs=[pl.BlockSpec(memory_space=pltpu.VMEM)] * 2,
        out_shape=[sds((stacked_count, width), F32), sds((8, 128), F32)],
        compiler_params=params(),
        cost_estimate=cost(1e6, 1e6),
        name="pack",
    )(
        sums_attend,
        sums_up,
        sums_final,
        head_sum,
        grad_head,
        conv_sum,
        conv_bias,
        jnp.asarray(conv_lanes(share), BF),
        *after,
    )
    packed = jnp.concatenate(
        [
            stacked.reshape(stacked_count, devices, own).transpose(1, 0, 2).reshape(devices, -1),
            grad_b_up[:, 0].reshape(devices, -1),
            jnp.broadcast_to(shared[:4].reshape(1, -1), (devices, 512)),
        ],
        1,
    )
    packed_size = packed.shape[1]
    packed = jnp.pad(packed, ((0, 0), (0, (-packed.shape[1]) % 128)))
    if not can_split(own):
        wide = grad_w_up[0].transpose(1, 0, 2).reshape(width, -1)
        wide = lax.psum_scatter(wide, ALL, scatter_dimension=0, tiled=True).astype(F32)
        out_up, out_out = wide[:, :hidden_units], wide[:, hidden_units:]
        wide = grad_late[0][:6].transpose(1, 0, 2).reshape(width, -1)
        out_qkv = lax.psum_scatter(wide, ALL, scatter_dimension=0, tiled=True).astype(F32)
        tall = grad_late[0][6:].reshape(2, 2, width, half).transpose(1, 2, 0, 3)
        tall = tall.reshape(2 * width, width)
        out_skip = lax.psum_scatter(tall, ALL, scatter_dimension=0, tiled=True).astype(F32)
    else:
        after, _ = run_tasks([(sum_late, None), (sum_up, None)] + early, [packed], "serve_5")
    exchanged = lax.all_to_all(hold(packed, after), ALL, split_axis=0, concat_axis=0, tiled=True)
    if can_split(own):
        if chain_down:
            early = [(sum_down, down_layout)]
        after, results = run_tasks(
            [(sum_late, None), (sum_up, None)] + early, [exchanged], "serve_6"
        )
        if chain_down:
            out_down = results[0][0]
        after, results = run_tasks([(sum_late, None), (sum_up, up_layout)], after, "serve_7")
        out_up, out_out = results[0]
    back = to_items(hold(grad_back, after))
    if can_split(own):
        while sum_late.orders[0]:
            after, _ = run_tasks([(sum_late, None)], after, "serve_8")
    some_groups = groups
    token_block = pl.BlockSpec(
        (some_groups * share, rows, cols, width), lambda i: (i, 0, 0, 0)
    )
    grad_tokens, grad_skip_tokens, grad_extra_all = pl.pallas_call(
        token_kernel,
        grid=(groups // some_groups,),
        in_specs=[
            pl.BlockSpec((some_groups, back_rows, width), lambda i: (i, 0, 0)),
            whole((2 * width, width)),
        ],
        out_specs=[
            token_block,
            token_block,
            pl.BlockSpec((some_groups, 16, 2 * width), lambda i: (i, 0, 0)),
        ],
        out_shape=[sds(tokens.shape, BF)] * 2 + [sds((groups, 16, 2 * width), BF)],
        compiler_params=params(),
        cost_estimate=cost(items * local * 4 * width * width, 8e6),
        name="tokens",
    )(hold(back, after), w_skip)
    summed = jnp.sum(hold(exchanged, after), 0)
    small = [summed[k * own : (k + 1) * own] for k in range(9)]
    own_head = summed[9 * own : stacked_count * own].reshape(patch_values, own).T
    up_low = stacked_count * own
    own_b_up = summed[up_low : up_low + hidden_units // devices]
    shared = summed[up_low + hidden_units // devices : packed_size].reshape(4, 128)

    latent_row = share * local + 2 * share
    latent = back[:, latent_row : latent_row + latent.shape[1]]
    latent_out = (
        hold(latent, after)
        .reshape(groups, rows, cols, share, PATCH, PATCH, chans)
        .transpose(0, 3, 1, 4, 2, 5, 6)
        .reshape(items, height, breadth, chans)
    )
    grad_joined_extra = grad_extra_all[:, : 2 * share].reshape(items, 2, 2 * width)
    if can_split(own):
        _, results = run_tasks([(sum_late, late_layout)], [grad_tokens, latent_out], "serve_9")
        out_qkv, out_skip = results[0]
    return (
        latent_out,
        grad_tokens,
        grad_skip_tokens,
        grad_joined_extra[..., :width],
        grad_joined_extra[..., width:],
        out_skip,
        small[0],
        small[1],
        small[2],
        out_qkv,
        out_out,
        small[3],
        small[4],
        small[5],
        out_up,
        own_b_up,
        out_down,
        small[6],
        small[7],
        small[8],
        own_head,
        shared[0, 64 : 64 + patch_values],
        shared[:, : 9 * chans].reshape(chans, 3, 3, chans).transpose(1, 2, 0, 3),
        shared[0, 96 : 96 + chans],
    )


def solution(mesh):
    tiles = P("batch", "ty", "tx", None)
    pairs = P("batch", None, None)
    matrix = P(ALL, None)
    vector = P(ALL)
    return jax.shard_map(
        per_device,
        mesh=mesh,
        in_specs=(tiles, tiles, pairs, pairs, P("batch"), tiles) + (P(),) * 19,
        out_specs=(
            tiles,
            tiles,
            tiles,
            pairs,
            pairs,
            matrix,
            vector,
            vector,
            vector,
            matrix,
            matrix,
            vector,
            vector,
            vector,
            matrix,
            vector,
            matrix,
            vector,
            vector,
            vector,
            matrix,
            P(),
            P(),
            P(),
        ),
        check_vma=False,
    )
```
